128 devices in a mesh: seq: 8 (over x, core), tp: 16 (over z, y).
Axes of the slice: x: 4, y: 4, z: 4, core: 2. Of those that a mesh axis runs over, the one named last changes fastest.
Arguments:
- tokens: bfloat16 [4096, 4096], P('seq'), may hold values from -6 to 6
- norm_gain: bfloat16 [4096], replicated, may hold values from 0.5 to 1.5
- w_query: bfloat16 [4096, 4096], P(None, 'tp'), may hold values from -0.09375 to 0.09375
- w_key: bfloat16 [4096, 1024], P(None, 'tp'), may hold values from -0.09375 to 0.09375
- w_value: bfloat16 [4096, 1024], P(None, 'tp'), may hold values from -0.09375 to 0.09375
- w_out: bfloat16 [4096, 4096], P('tp'), may hold values from -0.09375 to 0.09375
- prefix_keys: bfloat16 [16384, 1024], P('seq', 'tp')
- prefix_values: bfloat16 [16384, 1024], P('seq', 'tp'), may hold values from -6 to 6
- keep_rows: int32 [8, 8, 384], P('seq'), may hold values from 0 to 511, all different within a row
- owners: int32 [8, 8, 384, 1], P('seq'), may hold values from 0 to 127; in each aligned block of 384 rows (0 to 383, 384 to 767, ..., all dimensions but the last counted through in order) at most 4 rows name the same one
Outputs:
- attn_out: bfloat16 [4096, 4096], P('seq', 'tp')
- kept_cache: bfloat16 [32768, 256], P(('seq', 'tp'))
The draws below stay inside these ranges and needn't reach their ends.
Inputs may be any that keep to these rules, and one draw needn't show every extreme that they name: `keep_rows`: the 384 rows of one span and head are distinct. `owners`: at most 4 entries of one span and head name the same owner, a bound that some of them reach.
All inputs are finite; a program needn't handle non-finite values.
Results may differ from the reference program's by a relative error of at most 0.03.
Values may be sent and summed in bfloat16 or wider, within the bound.
No kernel may reach another device: no remote copies, remote signals or barrier semaphores. Data moves between devices by JAX's collectives and lax.ppermute only.
A program may use at most 128 MiB of HBM per device.

```python
import math
import jax
import jax.numpy as jnp
import numpy as np
from jax import lax

D = 4096
HD = 128
QH_DEV = 2
HQ = 32
KVH = 8
SPAN = 512
TOKENS = 4096
PREFIX = 16384
KEEP = 384
CAP = 4
N_SEQ = 8
DEVICES = 128


def draw_prefix_keys(key, part):
    key = jax.random.fold_in(key, 11)
    base = jax.random.normal(key, (PREFIX, KVH * HD), jnp.float32)
    return base.astype(jnp.bfloat16)


def steps_of(rng, dims, cuts, smallest, top_value):
    loudness = 1.0
    for position, parts in cuts:
        steps = jax.random.uniform(jax.random.fold_in(jax.random.fold_in(rng, 6), position), (parts,), jnp.float32, smallest / len(cuts), top_value / len(cuts))
        loudness = loudness * jnp.repeat(jnp.exp(steps), dims[position] // parts).reshape((-1,) + (1,) * (len(dims) - 1 - position))
    return loudness


def picks_of(rng, rows, count, top, lift):
    sequence = jax.random.permutation(jax.random.fold_in(rng, 1), count)
    pull = sequence
    for power in range(3):
        pull = pull * pull // count
    pull = pull * lift // count
    tickets = jax.random.randint(jax.random.fold_in(rng, 2), (rows, count), 0, 4096) + pull
    sure = jax.random.permutation(jax.random.fold_in(rng, 3), rows)[jnp.arange(count) % rows]
    tickets = jnp.where(jnp.arange(rows)[:, None] == sure[None, :], 1 << 14, tickets)
    merit = tickets * count + jnp.arange(count)
    return lax.top_k(merit.astype(jnp.int32), top)[1].astype(jnp.int32)


def routed_block(key, own, number, rows, amount, top, limit, skew):
    ranking = jax.random.permutation(key, amount)
    heavy_load, ordinary = load_shares(amount, rows * top, limit, skew, True), load_shares(amount, rows * top, limit, skew, False)
    places = jnp.arange(amount)

    def named(sizes, turn):
        used = int((sizes > 0).sum())
        fixed = max(1, used // 4)
        moved = fixed + (places - fixed + turn * (used - fixed)) % max(1, amount - fixed)
        return jnp.zeros((amount,), jnp.int32).at[ranking[jnp.where(places < fixed, places, moved)]].set(jnp.asarray(sizes, jnp.int32))

    sizes = jnp.where(number % 4 == 0, named(heavy_load, number // 4), named(ordinary, number - number // 4 - 1))
    mixed = jax.random.permutation(jax.random.fold_in(own, 3), amount)
    giver, sink = mixed[0:amount // 2 * 2:2], mixed[1:amount // 2 * 2:2]
    room = jnp.minimum(sizes[giver] - 1, limit - sizes[sink]) // 2
    room = jnp.where((giver == ranking[0]) | (sink == ranking[0]) | (sizes[sink] == 0), 0, jnp.maximum(room, 0))
    moved = jax.random.randint(jax.random.fold_in(own, 4), (amount // 2,), 0, 1 << 20) % (room + 1)
    sizes = sizes.at[giver].add(-moved).at[sink].add(moved)
    items = jnp.searchsorted(jnp.cumsum(sizes), jnp.arange(rows * top), side="right").astype(jnp.int32)
    grid = items.reshape(top, rows).T
    grid = grid[jax.random.permutation(jax.random.fold_in(own, 1), rows)]
    turn = jax.random.randint(jax.random.fold_in(own, 2), (rows, 1), 0, top)
    return jnp.take_along_axis(grid, (jnp.arange(top)[None, :] + turn) % top, axis=1)


def load_shares(count, total, most, slope, full):
    loads = [(1 << 20) // math.isqrt(rank ** slope) + 1 for rank in range(1, count + 1)]
    largest = most if full else min(most, max(-(-total // count), total * loads[0] // sum(loads)))
    least = 1 if total - largest >= count - 1 else 0
    holding, surplus = [largest] + [least] * (count - 1), total - largest - least * (count - 1)
    while surplus > 0:
        movable = [i for i in range(1, count) if holding[i] < largest] or [i for i in range(1, count) if holding[i] < most]
        mass, budget = sum([loads[i] for i in movable]), surplus
        for i in movable:
            more = min(most - holding[i], max(1, budget * loads[i] // mass), surplus)
            holding[i] = holding[i] + more
            surplus = surplus - more
    return np.array(holding)


def scatter_about(stream_key, extent, deviation, bound, cuts=(), held_as=jnp.bfloat16):
    loudness = steps_of(stream_key, extent, cuts, -0.22, 0.18) if cuts else 1.0
    result = jax.random.normal(stream_key, extent, jnp.float32) * deviation * loudness
    return jnp.minimum(jnp.maximum(result, -bound), bound).astype(held_as)


def setup_inputs(seed: int = 0) -> dict:
    seeds = jax.random.split(jax.random.key(seed), 11)
    tokens = scatter_about(seeds[0], (TOKENS, D), 1.0, 6.0, ((0, 8),))
    norm_gain = jnp.clip(1.0 + 0.1 * jax.random.normal(seeds[1], (D,), jnp.float32), 0.5, 1.5).astype(jnp.bfloat16)
    w_query = scatter_about(seeds[2], (D, HQ * HD), D ** -0.5, 0.09375, ((1, 16),))
    w_key = scatter_about(seeds[3], (D, KVH * HD), D ** -0.5, 0.09375, ((1, 16),))
    w_value = scatter_about(seeds[4], (D, KVH * HD), D ** -0.5, 0.09375, ((1, 16),))
    w_out = scatter_about(seeds[5], (HQ * HD, D), (HQ * HD) ** -0.5, 0.09375, ((0, 16),))
    prefix_keys = draw_prefix_keys(jax.random.fold_in(seeds[10], 71), 0)
    prefix_values = scatter_about(seeds[7], (PREFIX, KVH * HD), 1.0, 6.0, ((0, 8), (1, 16)))
    keep_rows = picks_of(seeds[8], N_SEQ * KVH, SPAN, KEEP, 0).reshape((N_SEQ, KVH, KEEP))
    owners_keys = jax.random.split(jax.random.fold_in(seeds[9], 1), N_SEQ * KVH * KEEP // KEEP)
    owners_turns = jax.random.permutation(jax.random.fold_in(seeds[9], 3), N_SEQ * KVH * KEEP // KEEP)
    owners = jax.vmap(lambda own, number: routed_block(jax.random.fold_in(seeds[9], 2), own, number, KEEP, DEVICES, 1, CAP, 2))(owners_keys, owners_turns).reshape((N_SEQ, KVH, KEEP, 1))
    return dict(tokens=tokens, norm_gain=norm_gain, w_query=w_query, w_key=w_key, w_value=w_value, w_out=w_out, prefix_keys=prefix_keys, prefix_values=prefix_values, keep_rows=keep_rows, owners=owners)


EPSILON = 1e-05
ROPE_BASE = 500000.0

def hadamard(width):
    index = jnp.arange(width, dtype=jnp.int32)
    both = index[:, None] & index[None, :]
    parity = jnp.zeros((width, width), jnp.int32)
    for bit in range(width.bit_length() - 1):
        parity = parity + (both >> bit & 1)
    sign = 1 - 2 * (parity % 2)
    return sign.astype(jnp.float32) / math.sqrt(width)

def rotary(matrix, positions):
    half = matrix.shape[-1] // 2
    freq = jnp.exp(-jnp.arange(half, dtype=jnp.float32) * (2.0 * math.log(ROPE_BASE) / matrix.shape[-1]))
    angle = positions.astype(jnp.float32)[:, None] * freq[None, :]
    cosine = jnp.cos(angle)[:, None, :]
    sine = jnp.sin(angle)[:, None, :]
    first = matrix[..., :half]
    second = matrix[..., half:]
    return jnp.concatenate([first * cosine - second * sine, second * cosine + first * sine], -1)

def reference(tokens, norm_gain, w_query, w_key, w_value, w_out, prefix_keys, prefix_values, keep_rows, owners):
    hidden = tokens.astype(jnp.float32)
    scale = lax.rsqrt(lax.optimization_barrier(jnp.mean(hidden * hidden, -1, keepdims=True)) + EPSILON)
    normed = (hidden * scale * norm_gain.astype(jnp.float32)).astype(jnp.bfloat16)
    query = jnp.dot(normed, w_query, preferred_element_type=jnp.float32).reshape(TOKENS, HQ, HD)
    key = jnp.dot(normed, w_key, preferred_element_type=jnp.float32).reshape(TOKENS, KVH, HD)
    value = jnp.dot(normed, w_value, preferred_element_type=jnp.float32).reshape(TOKENS, KVH, HD).astype(jnp.bfloat16)
    positions = PREFIX + jnp.arange(TOKENS, dtype=jnp.int32)
    query = (rotary(query, positions) * HD ** (-0.5)).astype(jnp.bfloat16)
    key = rotary(key, positions).astype(jnp.bfloat16)
    had = hadamard(HD)
    rotated = jnp.einsum('thd,de->the', query.astype(jnp.float32), had, precision=lax.Precision.HIGHEST).astype(jnp.bfloat16)
    token_index = jnp.arange(TOKENS, dtype=jnp.int32)
    causal = token_index[None, :] <= token_index[:, None]

    def one_head(head):
        group = head // (2 * QH_DEV)
        plain_q = lax.dynamic_index_in_dim(query, head, 1, False)
        turned_q = lax.dynamic_index_in_dim(rotated, head, 1, False)
        pre_k = lax.dynamic_slice_in_dim(prefix_keys, (group * HD).astype(jnp.int32), HD, 1)
        pre_v = lax.dynamic_slice_in_dim(prefix_values, (group * HD).astype(jnp.int32), HD, 1)
        own_k = lax.dynamic_index_in_dim(key, group, 1, False)
        own_v = lax.dynamic_index_in_dim(value, group, 1, False)
        score_pre = jnp.dot(turned_q, pre_k.T, preferred_element_type=jnp.float32)
        score_own = jnp.dot(plain_q, own_k.T, preferred_element_type=jnp.float32)
        score_own = jnp.where(causal, score_own, -jnp.inf)
        top = jnp.maximum(lax.optimization_barrier(jnp.max(score_pre, -1)), lax.optimization_barrier(jnp.max(score_own, -1)))
        weight_pre = jnp.exp(score_pre - top[:, None])
        weight_own = jnp.exp(score_own - top[:, None])
        total = lax.optimization_barrier(jnp.sum(weight_pre, -1)) + lax.optimization_barrier(jnp.sum(weight_own, -1))
        mixed_pre = jnp.dot(weight_pre.astype(jnp.bfloat16), pre_v, preferred_element_type=jnp.float32)
        mixed = jnp.dot(mixed_pre, had, precision=lax.Precision.HIGHEST)
        mixed = mixed + jnp.dot(weight_own.astype(jnp.bfloat16), own_v, preferred_element_type=jnp.float32)
        return (mixed / total[:, None]).astype(jnp.bfloat16)
    context = lax.map(one_head, jnp.arange(HQ, dtype=jnp.int32))
    context = jnp.transpose(context, (1, 0, 2)).reshape(TOKENS, HQ * HD)
    attn_out = jnp.dot(context, w_out, preferred_element_type=jnp.float32).astype(jnp.bfloat16)
    span_keys = key.reshape(N_SEQ, SPAN, KVH, HD)
    span_values = value.reshape(N_SEQ, SPAN, KVH, HD)
    device_ids = jnp.arange(DEVICES, dtype=jnp.int32)
    sources = N_SEQ * KVH

    def one_source(source):
        span_id = source // KVH
        group = source % KVH
        rows = keep_rows[span_id, group]
        dest = owners[span_id, group, :, 0]
        picked_k = span_keys[span_id, :, group][rows].astype(jnp.float32)
        picked_v = span_values[span_id, :, group][rows].astype(jnp.float32)
        pair = jnp.concatenate([jnp.dot(picked_k, had, precision=lax.Precision.HIGHEST), jnp.dot(picked_v, had, precision=lax.Precision.HIGHEST)], -1)
        onehot = (dest[:, None] == device_ids[None, :]).astype(jnp.int32)
        slot = lax.optimization_barrier(jnp.sum((jnp.cumsum(onehot, 0) - onehot) * onehot, 1))
        where = dest * (sources * CAP) + source * CAP + slot
        return (where.astype(jnp.int32), pair)
    places, pairs = lax.map(one_source, jnp.arange(sources, dtype=jnp.int32))
    kept = jnp.zeros((DEVICES * sources * CAP, 2 * HD), jnp.float32)
    kept = kept.at[places.reshape(-1)].set(pairs.reshape(-1, 2 * HD))
    return (attn_out, kept.astype(jnp.bfloat16))
```

```python
import functools
import math

import jax
import jax.numpy as jnp
import numpy as np
from jax import lax
from jax.experimental import pallas as pl
from jax.experimental.pallas import tpu as pltpu
from jax.sharding import PartitionSpec as P

EPSILON = 1e-05
ROPE_BASE = 500000.0
LOWEST = -1e30
LOG2E = math.log2(math.e)
SAFE_BOUND = 60.0
HD = 128
HALF = 64
AXES = ("seq", "tp")
RING = 4
TILE = 512

NT = (((1,), (1,)), ((), ()))
TN = (((0,), (1,)), ((), ()))
F32 = jnp.float32
BF16 = jnp.bfloat16


def device_at(x, core, z, y):
    return ((x % RING) * 2 + core) * RING * RING + (z % RING) * RING + y % RING


def pairs_of(move):
    return [
        (device_at(x, c, z, y), device_at(*move(x, c, z, y)))
        for x in range(RING)
        for c in range(2)
        for z in range(RING)
        for y in range(RING)
    ]


def send(value, move):
    return lax.ppermute(value, AXES, pairs_of(move))


def to_sibling(value):
    return send(value, lambda x, c, z, y: (x, 1 - c, z, y))


def to_head_pair(value):
    return send(value, lambda x, c, z, y: (x, c, z, y ^ 1))


def along_x(value, step):
    return send(value, lambda x, c, z, y: (x + step, c, z, y))


def along_first(value, step):
    return send(
        value, lambda x, c, z, y: (x, c, z + step, y) if c == 0 else (x, c, z, y + step)
    )


def along_second(value, step):
    return send(
        value, lambda x, c, z, y: (x, c, z, y + step) if c == 0 else (x, c, z + step, y)
    )


def signs():
    index = np.arange(HD)
    both = index[:, None] & index[None, :]
    parity = np.zeros((HD, HD), np.int64)
    for bit in range(7):
        parity += both >> bit & 1
    plain = (1 - 2 * (parity % 2)).astype(np.float32)
    return np.stack([plain, np.roll(plain, HALF, axis=1)])


def rope_tables(span, spans, prefix):
    freq = np.exp(-np.arange(HALF) * (2.0 * math.log(ROPE_BASE) / HD))
    freq = np.concatenate([freq, freq])
    near = np.arange(span)[:, None] * freq[None, :]
    far = (prefix + span * np.arange(spans))[:, None] * freq[None, :]
    near = np.stack([np.cos(near), np.sin(near)]).astype(np.float32)
    far = np.stack([np.cos(far), np.sin(far)]).astype(np.float32)
    return near, far


def rope_factors(near, far, number):
    cos_far, sin_far = far[0, pl.ds(number, 1), :], far[1, pl.ds(number, 1), :]
    cosine = near[0] * cos_far - near[1] * sin_far
    sine = near[1] * cos_far + near[0] * sin_far
    lane = lax.broadcasted_iota(jnp.int32, (1, HD), 1)
    return cosine, jnp.where(lane < HALF, -sine, sine)


def project_kernel(
    info, tokens, gain, w_q, w_kt, w_vt, near, far, sign, w_out,
    q_out, kv_out, w0, w1, w2, w3,
    w_kv, sems,
):
    step = pl.program_id(0)
    core, z, y, parity, number = info[1], info[2], info[3], info[4], info[5]
    pieces = (w0, w1, w2, w3)

    def copies():
        for d in range(RING):
            for k in range(RING):
                row = lax.rem(z + jnp.where(core == 0, d, k), RING)
                col = lax.rem(y + jnp.where(core == 0, k, d), RING)
                begin = pl.multiple_of((row * RING + col) * 256, 256)
                yield pltpu.make_async_copy(
                    w_out.at[:, pl.ds(begin, 256)],
                    pieces[d].at[:, pl.ds(k * 256, 256)],
                    sems.at[d * RING + k],
                )

    @pl.when(step == 0)
    def _():
        for copy in copies():
            copy.start()
        w_kv[:HALF, :] = w_kt[...]
        w_kv[HALF:, :] = w_vt[...]

    hidden = tokens[...].astype(F32)
    scale = lax.rsqrt(jnp.mean(hidden * hidden, -1, keepdims=True) + EPSILON)
    normed = (hidden * scale * gain[...].astype(F32)).astype(BF16)
    query = jnp.dot(normed, w_q[...], preferred_element_type=F32)
    kv_out[...] = lax.dot_general(normed, w_kv[...], NT, preferred_element_type=F32).astype(BF16)
    cosine, sine = rope_factors(near, far, number)
    turn = sign[parity]
    for h in range(2):
        part = query[:, h * HD:(h + 1) * HD]
        part = part * cosine + pltpu.roll(part, HALF, 1) * sine
        part = (part * HD ** -0.5).astype(BF16)
        part = jnp.dot(part, turn, preferred_element_type=F32)
        q_out[h] = (part * (HD ** -0.5 * LOG2E)).astype(BF16)

    @pl.when(step == pl.num_programs(0) - 1)
    def _():
        for copy in copies():
            copy.wait()


def project(info, tokens, gain, w_q, w_kt, w_vt, near, far, sign, w_out):
    span, width = tokens.shape
    block = 128
    any_spec = pl.BlockSpec(memory_space=pl.ANY)
    whole = lambda shape: pl.BlockSpec(shape, lambda i: (0,) * len(shape))
    piece = jax.ShapeDtypeStruct((256, 1024), BF16)
    out = pl.pallas_call(
        project_kernel,
        grid=(span // block,),
        in_specs=[
            pl.BlockSpec(memory_space=pltpu.SMEM),
            pl.BlockSpec((block, width), lambda i: (i, 0)),
            whole((1, width)),
            whole((width, 2 * HD)),
            whole((HALF, width)),
            whole((HALF, width)),
            pl.BlockSpec((2, block, HD), lambda i: (0, i, 0)),
            whole(far.shape),
            whole((2, HD, HD)),
            any_spec,
        ],
        out_specs=[
            pl.BlockSpec((2, block, HD), lambda i: (0, i, 0)),
            pl.BlockSpec((block, HD), lambda i: (i, 0)),
        ] + [any_spec] * 4,
        out_shape=[
            jax.ShapeDtypeStruct((2, span, HD), BF16),
            jax.ShapeDtypeStruct((span, HD), BF16),
        ] + [piece] * 4,
        scratch_shapes=[pltpu.VMEM((HD, width), BF16), pltpu.SemaphoreType.DMA((16,))],
        compiler_params=pltpu.CompilerParams(vmem_limit_bytes=32 << 20),
        cost_estimate=pl.CostEstimate(
            flops=2 * span * width * 384, bytes_accessed=11 << 20, transcendentals=0
        ),
    )(info, tokens, gain, w_q, w_kt, w_vt, near, far, sign, w_out)
    return out[0].reshape(2 * span, HD), out[1], out[2:]


def segment_kernel(info, own, other, near, far, sign, rows, owners, seg_out, kept_out):
    parity, number, group = info[4], info[5], info[6]
    odd = parity == 1
    mine, theirs = own[...].astype(F32), other[...].astype(F32)
    first = jnp.where(odd, theirs, mine)
    second = jnp.where(odd, mine, theirs)
    lane = lax.broadcasted_iota(jnp.int32, (1, HD), 1)
    key = jnp.where(lane < HALF, first, pltpu.roll(second, HALF, 1))
    value = jnp.where(lane < HALF, pltpu.roll(first, HALF, 1), second).astype(BF16)
    cosine, sine = rope_factors(near, far, number)
    key = (key * cosine + pltpu.roll(key, HALF, 1) * sine).astype(BF16)
    turn = sign[parity]
    unit = HD ** -0.5
    seg_out[:HD, :] = (lax.dot_general(turn, key, TN, preferred_element_type=F32) * unit).astype(BF16)
    seg_out[HD:, :] = (lax.dot_general(turn, value, TN, preferred_element_type=F32) * unit).astype(BF16)
    plain = sign[0]
    pair = jnp.concatenate(
        [
            (jnp.dot(key, plain, preferred_element_type=F32) * unit).astype(BF16),
            (jnp.dot(value, plain, preferred_element_type=F32) * unit).astype(BF16),
        ],
        1,
    )
    span, keep = own.shape[0], rows.shape[1]
    row = rows[pl.ds(group, 1), :]
    owner = owners[pl.ds(group, 1), :]
    slot_row = lax.broadcasted_iota(jnp.int32, (64, keep), 0)
    mine_owner = slot_row * 2 + parity
    named = owner == mine_owner
    named_f = jnp.where(named, 1.0, 0.0)
    before = lax.broadcasted_iota(jnp.int32, (keep, keep), 0) < lax.broadcasted_iota(
        jnp.int32, (keep, keep), 1
    )
    rank = jnp.dot(
        named_f.astype(BF16), jnp.where(before, 1.0, 0.0).astype(BF16), preferred_element_type=F32
    )
    picks = jnp.concatenate(
        [jnp.where(jnp.logical_and(named, rank == j), 1.0, 0.0) for j in range(4)], 0
    ).astype(BF16)
    places = jnp.where(
        lax.broadcasted_iota(jnp.int32, (span, keep), 0) == row, 1.0, 0.0
    ).astype(BF16)
    chosen = lax.dot_general(picks, places, NT, preferred_element_type=F32).astype(BF16)
    kept = jnp.dot(chosen, pair, preferred_element_type=F32).astype(BF16)
    for j in range(4):
        kept_out[:, j * 256:(j + 1) * 256] = kept[j * 64:(j + 1) * 64, :]


def vmem():
    return pl.BlockSpec(memory_space=pltpu.VMEM)


def smem():
    return pl.BlockSpec(memory_space=pltpu.SMEM)


def segment(info, own, other, near, far, sign, rows, owners):
    span = own.shape[0]
    return pl.pallas_call(
        segment_kernel,
        in_specs=[smem()] + [vmem()] * 7,
        out_specs=[vmem(), vmem()],
        out_shape=[
            jax.ShapeDtypeStruct((2 * HD, span), BF16),
            jax.ShapeDtypeStruct((64, 1024), BF16),
        ],
        compiler_params=pltpu.CompilerParams(vmem_limit_bytes=24 << 20),
        cost_estimate=pl.CostEstimate(
            flops=400_000_000, bytes_accessed=2 << 20, transcendentals=0
        ),
    )(info, own, other, near, far, sign, rows, owners)


def attend_kernel(
    step, info, q, own, other, sib_own, sib_other, seg, sib_seg, out, acc, total, top
):
    x, core = info[0], info[1]
    rows = q.shape[0]
    span = seg.shape[1]
    blocks = own.shape[1] // TILE
    prefix = ((own, other), (sib_own, sib_other))

    def prefix_tile(pair, columns):
        mine, theirs = pair
        keys = jnp.concatenate([mine[:HALF, columns], theirs[:HALF, columns]], 0)
        values = jnp.concatenate([mine[HALF:, columns], theirs[HALF:, columns]], 0)
        return keys, values

    squares = []
    for pair in prefix:
        for ref in pair:
            half = ref[:HALF, :].astype(F32)
            squares.append(jnp.sum(half * half, 0, keepdims=True))
    longest = jnp.maximum(jnp.max(squares[0] + squares[1]), jnp.max(squares[2] + squares[3]))
    for ref in (seg, sib_seg):
        part = ref[:HD, :].astype(F32)
        longest = jnp.maximum(longest, jnp.max(jnp.sum(part * part, 0, keepdims=True)))
    query_f = q[...].astype(F32)
    widest = jnp.max(jnp.sum(query_f * query_f, 1, keepdims=True))
    calm = longest * widest < SAFE_BOUND * SAFE_BOUND

    if step == 0:
        whole_flags = (None, core == 1)
    else:
        later = lax.rem(x + RING - step, RING) > x
        whole_flags = (later, later)

    def causal(begin, count):
        token = lax.rem(lax.broadcasted_iota(jnp.int32, (count, span), 0) + begin, span)
        return lax.broadcasted_iota(jnp.int32, (count, span), 1) <= token

    @pl.when(calm)
    def _():
        def tile(keys, values, first=False, masked=False):
            scores = jnp.dot(q[...], keys, preferred_element_type=F32)
            weights = jnp.exp2(scores)
            if masked:
                weights = jnp.where(causal(0, rows), weights, 0.0)
            part = weights[:, :HD]
            for i in range(1, TILE // HD):
                part = part + weights[:, i * HD:(i + 1) * HD]
            mixed = lax.dot_general(weights.astype(BF16), values, NT, preferred_element_type=F32)
            if first:
                acc[...] = mixed
                total[...] = part
            else:
                acc[...] += mixed
                total[...] += part

        for number, pair in enumerate(prefix):
            for b in range(blocks):
                keys, values = prefix_tile(pair, slice(b * TILE, (b + 1) * TILE))
                tile(keys, values, first=number == 0 and b == 0)
        for ref, flag in zip((seg, sib_seg), whole_flags):
            if flag is None:
                tile(ref[:HD, :], ref[HD:, :], masked=True)
            else:
                @pl.when(flag)
                def _(ref=ref):
                    tile(ref[:HD, :], ref[HD:, :])
        top[...] = jnp.zeros_like(top)

    @pl.when(jnp.logical_not(calm))
    def _():
        acc[...] = jnp.zeros_like(acc)
        total[...] = jnp.zeros_like(total)
        top[...] = jnp.full_like(top, LOWEST)
        chunk = 256

        def tile(keys, values, masked=False):
            def some_rows(r, carry):
                begin = pl.multiple_of(r * chunk, chunk)
                at = pl.ds(begin, chunk)
                scores = jnp.dot(q[at, :], keys, preferred_element_type=F32)
                if masked:
                    scores = jnp.where(causal(begin, chunk), scores, -jnp.inf)
                old = top[at, :]
                new = jnp.maximum(old, jnp.max(scores, 1, keepdims=True))
                weights = jnp.exp2(scores - new[:, :1])
                factor = jnp.exp2(old - new)
                part = weights[:, :HD]
                for i in range(1, TILE // HD):
                    part = part + weights[:, i * HD:(i + 1) * HD]
                mixed = lax.dot_general(
                    weights.astype(BF16), values, NT, preferred_element_type=F32
                )
                acc[at, :] = acc[at, :] * factor + mixed
                total[at, :] = total[at, :] * factor + part
                top[at, :] = new
                return carry

            lax.fori_loop(0, rows // chunk, some_rows, 0)

        for pair in prefix:
            def some_keys(b, carry, pair=pair):
                tile(*prefix_tile(pair, pl.ds(pl.multiple_of(b * TILE, TILE), TILE)))
                return carry

            lax.fori_loop(0, blocks, some_keys, 0)
        for ref, flag in zip((seg, sib_seg), whole_flags):
            if flag is None:
                tile(ref[:HD, :], ref[HD:, :], masked=True)
            else:
                @pl.when(flag)
                def _(ref=ref):
                    tile(ref[:HD, :], ref[HD:, :])

    summed = jnp.sum(total[...], 1, keepdims=True)
    out[:rows, :] = (acc[...] / summed).astype(BF16)
    level = top[...] + jnp.log2(summed)
    eye = lax.broadcasted_iota(jnp.int32, (1, HD, HD), 1) == lax.broadcasted_iota(
        jnp.int32, (1, HD, HD), 2
    )
    packed = jnp.sum(jnp.where(eye, level.reshape(rows // HD, HD, HD), 0.0), 1)
    high = packed.astype(BF16).astype(F32)
    rest = packed - high
    middle = rest.astype(BF16).astype(F32)
    low = rest - middle
    out[rows:, :] = jnp.concatenate([high, middle, low, jnp.zeros_like(high)], 0).astype(BF16)


def attend(step, info, q, own, other, sib_own, sib_other, seg, sib_seg):
    rows = q.shape[0]
    return pl.pallas_call(
        functools.partial(attend_kernel, step),
        in_specs=[smem()] + [vmem()] * 7,
        out_specs=vmem(),
        out_shape=jax.ShapeDtypeStruct((rows + 32, HD), BF16),
        scratch_shapes=[pltpu.VMEM((rows, HD), F32)] * 3,
        compiler_params=pltpu.CompilerParams(vmem_limit_bytes=32 << 20),
        cost_estimate=pl.CostEstimate(
            flops=8 * rows * HD * 4096, bytes_accessed=4 << 20, transcendentals=rows * 4096
        ),
    )(info, q, own, other, sib_own, sib_other, seg, sib_seg)


def split(value):
    high = value.astype(BF16)
    return high, (value - high.astype(F32)).astype(BF16)


def merge_kernel(info, p0, p1, p2, p3, sign, out):
    parity = info[4]
    parts = (p0, p1, p2, p3)
    rows = p0.shape[0] - 32
    count = rows // HD
    levels = []
    for part in parts:
        stats = part[rows:, :].astype(F32)
        levels.append(stats[:count] + stats[count:2 * count] + stats[2 * count:3 * count])
    most = functools.reduce(jnp.maximum, levels)
    shares = [jnp.exp2(level - most) for level in levels]
    whole = functools.reduce(jnp.add, shares)
    shares = [share / whole for share in shares]
    eye = lax.broadcasted_iota(jnp.int32, (HD, HD), 0) == lax.broadcasted_iota(
        jnp.int32, (HD, HD), 1
    )
    turn = sign[parity]
    per_head = count // 2
    for b in range(count):
        left, right = [], []
        for share, part in zip(shares, parts):
            block = part[b * HD:(b + 1) * HD, :]
            high, low = split(share[b:b + 1, :])
            for piece in (high, low):
                left.append(jnp.where(eye, piece.astype(F32), 0.0).astype(BF16))
                right.append(block)
        mixed = jnp.dot(
            jnp.concatenate(left, 1), jnp.concatenate(right, 0), preferred_element_type=F32
        )
        high, low = split(mixed)
        plain = lax.dot_general(high, turn, NT, preferred_element_type=F32)
        plain = plain + lax.dot_general(low, turn, NT, preferred_element_type=F32)
        head, place = b // per_head, b % per_head
        out[place * HD:(place + 1) * HD, head * HD:(head + 1) * HD] = (
            plain * HD ** -0.5
        ).astype(BF16)


def merge(info, parts, sign):
    rows = parts[0].shape[0] - 32
    return pl.pallas_call(
        merge_kernel,
        in_specs=[smem()] + [vmem()] * 5,
        out_specs=vmem(),
        out_shape=jax.ShapeDtypeStruct((rows // 2, 2 * HD), BF16),
        compiler_params=pltpu.CompilerParams(vmem_limit_bytes=24 << 20),
        cost_estimate=pl.CostEstimate(
            flops=400_000_000, bytes_accessed=2 << 20, transcendentals=0
        ),
    )(info, *parts, sign)


def out_kernel(c0, c1, c2, c3, w0, w1, w2, w3, o0, o1, o2, o3):
    outs = (o0, o1, o2, o3)
    for k in (2, 1, 3, 0):
        columns = slice(k * 256, (k + 1) * 256)
        whole = None
        for c, w in ((c0, w0), (c1, w1), (c2, w2), (c3, w3)):
            part = jnp.dot(c[...], w[:, columns], preferred_element_type=F32)
            whole = part if whole is None else whole + part
        outs[k][...] = whole.astype(outs[k].dtype)


def project_out(contexts, weights):
    span = contexts[0].shape[0]
    return pl.pallas_call(
        out_kernel,
        in_specs=[vmem()] * 8,
        out_specs=[vmem()] * 4,
        out_shape=[jax.ShapeDtypeStruct((span, 256), F32 if k == 0 else BF16) for k in range(4)],
        compiler_params=pltpu.CompilerParams(vmem_limit_bytes=24 << 20),
        cost_estimate=pl.CostEstimate(
            flops=2 * span * 1024 * 1024, bytes_accessed=5 << 20, transcendentals=0
        ),
    )(*contexts, *weights)


def shards(
    tokens, norm_gain, w_query, w_key, w_value, w_out, prefix_keys, prefix_values, keep_rows, owners
):
    seq = lax.axis_index("seq")
    tp = lax.axis_index("tp")
    seq_count = lax.axis_size("seq")
    span = tokens.shape[0]
    prefix_len = prefix_keys.shape[0] * seq_count
    info = jnp.stack(
        [seq // 2, seq % 2, tp // RING, tp % RING, tp % 2, seq, tp // 2, seq * 0]
    ).astype(jnp.int32)
    near, far = rope_tables(span, seq_count, prefix_len)
    near, far = jnp.asarray(near), jnp.asarray(far)
    sign = jnp.asarray(signs(), BF16)

    own = jnp.concatenate([prefix_keys.T, prefix_values.T], 0)
    other = to_head_pair(own)
    sib_own = to_sibling(own)
    q, kv, pieces = project(
        info, tokens, norm_gain.reshape(1, -1), w_query, w_key.T, w_value.T, near, far, sign, w_out
    )
    kv_other = to_head_pair(kv)
    queries = [q] + [along_x(q, d) for d in (1, 2, 3)]
    weights = [pieces[0]] + [along_first(pieces[d], d) for d in (1, 2, 3)]
    sib_other = to_sibling(other)
    seg, kept = segment(
        info, kv, kv_other, near, far, sign, keep_rows[0], owners.reshape(owners.shape[1:3])
    )
    sib_seg = to_sibling(seg)
    parts = [None] * RING
    for d in (3, 1, 2, 0):
        part = attend(d, info, queries[d], own, other, sib_own, sib_other, seg, sib_seg)
        parts[d] = along_x(part, -d) if d else part
    context = merge(info, parts, sign)
    contexts = [context] + [along_first(context, d) for d in (1, 2, 3)]
    shares = project_out(contexts, weights)
    arrived = [along_second(shares[k], k).astype(F32) for k in (1, 2, 3)]
    attn_out = (shares[0] + arrived[0] + arrived[1] + arrived[2]).astype(BF16)

    tps = lax.axis_size("tp")
    kept = lax.all_to_all(kept, "seq", 0, 0, tiled=True)
    kept = kept.reshape(seq_count, tps // 2, 1024).swapaxes(0, 1).reshape(-1, 1024)
    same = [list(range(0, tps, 2)), list(range(1, tps, 2))]
    kept = lax.all_to_all(kept, "tp", 0, 0, axis_index_groups=same, tiled=True)
    kept = kept.reshape(tps // 2, seq_count, 1024).swapaxes(0, 1)
    return attn_out, kept.reshape(-1, 2 * HD)


def solution(mesh):
    return jax.shard_map(
        shards,
        mesh=mesh,
        in_specs=(
            P("seq", None),
            P(),
            P(None, "tp"),
            P(None, "tp"),
            P(None, "tp"),
            P("tp", None),
            P("seq", "tp"),
            P("seq", "tp"),
            P("seq", None, None),
            P("seq", None, None, None),
        ),
        out_specs=(P("seq", "tp"), P(("seq", "tp"), None)),
        check_vma=False,
    )
```

```python
import functools
import math

import jax
import jax.numpy as jnp
import numpy as np
from jax import lax
from jax.experimental import pallas as pl
from jax.experimental.pallas import tpu as pltpu
from jax.sharding import PartitionSpec as P

EPSILON = 1e-05
ROPE_BASE = 500000.0
LOWEST = -1e30
LOG2E = math.log2(math.e)
SAFE_BOUND = 60.0
HD = 128
HALF = 64
AXES = ("seq", "tp")
RING = 4
TILE = 512
CHUNKS = 4
EXTRA = 32 + 128

NT = (((1,), (1,)), ((), ()))
TN = (((0,), (1,)), ((), ()))
F32 = jnp.float32
BF16 = jnp.bfloat16


def device_at(x, core, z, y):
    return ((x & 3) * 2 + core) * 16 + (z & 3) * 4 + (y & 3)


def pairs_of(move):
    return [
        (device_at(x, c, z, y), device_at(*move(x, c, z, y)))
        for x in range(RING)
        for c in range(2)
        for z in range(RING)
        for y in range(RING)
    ]


def send(value, move):
    return lax.ppermute(value, AXES, pairs_of(move))


def to_sibling(value):
    return send(value, lambda x, c, z, y: (x, 1 - c, z, y))


def to_head_pair(value):
    return send(value, lambda x, c, z, y: (x, c, z, y ^ 1))


def along_x(value, step):
    return send(value, lambda x, c, z, y: (x + step, c, z, y))


def along_first(value, step):
    return send(
        value, lambda x, c, z, y: (x, c, z + step, y) if c == 0 else (x, c, z, y + step)
    )


def along_second(value, step):
    return send(
        value, lambda x, c, z, y: (x, c, z, y + step) if c == 0 else (x, c, z + step, y)
    )


def signs():
    index = np.arange(HD)
    both = index[:, None] & index[None, :]
    parity = np.zeros((HD, HD), np.int64)
    for bit in range(7):
        parity += both >> bit & 1
    plain = (1 - 2 * (parity % 2)).astype(np.float32)
    return np.stack([plain, np.roll(plain, HALF, axis=1)])


def rope_tables(span, spans, prefix):
    freq = np.exp(-np.arange(HALF) * (2.0 * math.log(ROPE_BASE) / HD))
    freq = np.concatenate([freq, freq])
    near = np.arange(span)[:, None] * freq[None, :]
    far = (prefix + span * np.arange(spans))[:, None] * freq[None, :]
    near = np.stack([np.cos(near), np.sin(near)]).astype(np.float32)
    far = np.stack([np.cos(far), np.sin(far)]).astype(np.float32)
    return near, far


def rope_factors(near, far, number):
    cos_far, sin_far = far[0, pl.ds(number, 1), :], far[1, pl.ds(number, 1), :]
    cosine = near[0] * cos_far - near[1] * sin_far
    sine = near[1] * cos_far + near[0] * sin_far
    lane = lax.broadcasted_iota(jnp.int32, (1, HD), 1)
    return cosine, jnp.where(lane < HALF, -sine, sine)


def project_kernel(
    info, tokens, gain, w_q, w_kt, w_vt, near, far, sign, w_out, q_out, kv_out, w0, w1, w2, w3,
    held, held_q, held_kv, held_near, held_w, sum_q, sum_kv, sems, cut_sems,
):
    core, z, y, parity, number = info[1], info[2], info[3], info[4], info[5]
    span, width = tokens.shape
    block = width // CHUNKS
    parts = [pl.ds(i * block, block) for i in range(CHUNKS)]
    arrive = []
    for i, at in enumerate(parts):
        moves = (
            (tokens.at[:, at], held.at[:, at]),
            (w_q.at[at], held_q.at[at]),
            (w_kt.at[:, at], held_kv.at[:HALF, at]),
            (w_vt.at[:, at], held_kv.at[HALF:, at]),
        )
        arrive.append([
            pltpu.make_async_copy(start, end, sems.at[4 * i + j])
            for j, (start, end) in enumerate(moves)
        ])
    tables = pltpu.make_async_copy(near, held_near, sems.at[4 * CHUNKS])
    for copies in arrive:
        for copy in copies:
            copy.start()
    tables.start()
    whole = pltpu.make_async_copy(w_out, held_w, sems.at[4 * CHUNKS + 1])
    whole.start()
    cuts = []
    for d, piece in enumerate((w0, w1, w2, w3)):
        for k in range(RING):
            row = (z + jnp.where(core == 0, d, k)) & 3
            col = (y + jnp.where(core == 0, k, d)) & 3
            begin = pl.multiple_of((row * RING + col) * 256, 256)
            cuts.append(
                pltpu.make_async_copy(
                    held_w.at[:, pl.ds(begin, 256)],
                    piece.at[:, pl.ds(k * 256, 256)],
                    cut_sems.at[d * RING + k],
                )
            )
    squares = None
    per = block // HD
    for i, at in enumerate(parts):
        for copy in arrive[i]:
            copy.wait()
        gains = jnp.concatenate([gain[j:j + 1, :] for j in range(i * per, (i + 1) * per)], 1)
        begin, end = i * block, (i + 1) * block
        hidden = held[:, begin:end].astype(F32)
        weighted = (hidden * gains.astype(F32)).astype(BF16)
        hidden = hidden * hidden
        for j in range(per):
            square = hidden[:, j * HD:(j + 1) * HD]
            squares = square if squares is None else squares + square
        part_q = jnp.dot(weighted, held_q[begin:end, :], preferred_element_type=F32)
        part_kv = lax.dot_general(
            weighted, held_kv[:, begin:end], NT, preferred_element_type=F32
        )
        if i == 0:
            sum_q[...] = part_q
            sum_kv[...] = part_kv
        else:
            sum_q[...] += part_q
            sum_kv[...] += part_kv
    whole.wait()
    for copy in cuts:
        copy.start()
    scale = lax.rsqrt(jnp.sum(squares, -1, keepdims=True) / width + EPSILON)
    kv_out[...] = (sum_kv[...] * scale).astype(BF16)
    tables.wait()
    cosine, sine = rope_factors(held_near, far, number)
    turn = sign[parity]
    for h in range(2):
        head = sum_q[:, h * HD:(h + 1) * HD] * scale
        head = head * cosine + pltpu.roll(head, HALF, 1) * sine
        head = (head * HD ** -0.5).astype(BF16)
        head = jnp.dot(head, turn, preferred_element_type=F32)
        q_out[h * span:(h + 1) * span, :] = (head * (HD ** -0.5 * LOG2E)).astype(BF16)
    for copy in cuts:
        copy.wait()


def project(info, tokens, gain, w_q, w_kt, w_vt, near, far, sign, w_out):
    span, width = tokens.shape
    remain = pl.BlockSpec(memory_space=pl.ANY)
    return pl.pallas_call(
        project_kernel,
        in_specs=[smem(), remain, vmem()] + [remain] * 4 + [vmem(), vmem(), remain],
        out_specs=[vmem(), vmem()] + [remain] * 4,
        out_shape=[
            jax.ShapeDtypeStruct((2 * span, HD), BF16),
            jax.ShapeDtypeStruct((span, HD), BF16),
        ] + [jax.ShapeDtypeStruct((w_out.shape[0], 1024), BF16)] * 4,
        scratch_shapes=[
            pltpu.VMEM((span, width), BF16),
            pltpu.VMEM((width, 2 * HD), BF16),
            pltpu.VMEM((HD, width), BF16),
            pltpu.VMEM(near.shape, F32),
            pltpu.VMEM(w_out.shape, BF16),
            pltpu.VMEM((span, 2 * HD), F32),
            pltpu.VMEM((span, HD), F32),
            pltpu.SemaphoreType.DMA((4 * CHUNKS + 2,)),
            pltpu.SemaphoreType.DMA((RING * RING,)),
        ],
        compiler_params=pltpu.CompilerParams(vmem_limit_bytes=60 << 20),
        cost_estimate=pl.CostEstimate(
            flops=2 * span * width * 384, bytes_accessed=7 << 20, transcendentals=0
        ),
    )(info, tokens, gain, w_q, w_kt, w_vt, near, far, sign, w_out)


def segment_kernel(info, own, other, near, far, sign, rows, owners, seg_out, stay_out, go_out):
    x, core, z, y, parity, number, group = (info[i] for i in range(7))
    odd = parity == 1
    mine, theirs = own[...].astype(F32), other[...].astype(F32)
    first = jnp.where(odd, theirs, mine)
    second = jnp.where(odd, mine, theirs)
    lane = lax.broadcasted_iota(jnp.int32, (1, HD), 1)
    key = jnp.where(lane < HALF, first, pltpu.roll(second, HALF, 1))
    value = jnp.where(lane < HALF, pltpu.roll(first, HALF, 1), second).astype(BF16)
    cosine, sine = rope_factors(near, far, number)
    key = (key * cosine + pltpu.roll(key, HALF, 1) * sine).astype(BF16)
    turn = sign[parity]
    unit = HD ** -0.5
    seg_out[:HD, :] = (lax.dot_general(turn, key, TN, preferred_element_type=F32) * unit).astype(BF16)
    seg_out[HD:, :] = (lax.dot_general(turn, value, TN, preferred_element_type=F32) * unit).astype(BF16)
    plain = sign[0]
    pair = jnp.concatenate(
        [
            (jnp.dot(key, plain, preferred_element_type=F32) * unit).astype(BF16),
            (jnp.dot(value, plain, preferred_element_type=F32) * unit).astype(BF16),
        ],
        1,
    )
    span, keep = own.shape[0], rows.shape[1]
    row = rows[pl.ds(group, 1), :]
    owner = owners[pl.ds(group, 1), :]
    place = lax.broadcasted_iota(jnp.int32, (256, 1), 0)
    to_core = jnp.where(place >= 128, 1 - core, core)
    step_first, step_second = (place >> 3) & 3, (place >> 1) & 3
    to_x = (x + (place >> 5)) & 3
    to_z = (z + jnp.where(to_core == 0, step_first, step_second)) & 3
    to_y = (y + jnp.where(to_core == 0, step_second, step_first)) & 3
    named = owner == device_at(to_x, to_core, to_z, to_y)
    before = lax.broadcasted_iota(jnp.int32, (keep, keep), 0) < lax.broadcasted_iota(
        jnp.int32, (keep, keep), 1
    )
    rank = jnp.dot(
        jnp.where(named, 1.0, 0.0).astype(BF16),
        jnp.where(before, 1.0, 0.0).astype(BF16),
        preferred_element_type=F32,
    )
    slot = (2 * parity + (place & 1)).astype(F32)
    picks = jnp.where(jnp.logical_and(named, rank == slot), 1.0, 0.0).astype(BF16)
    places = jnp.where(
        lax.broadcasted_iota(jnp.int32, (span, keep), 0) == row, 1.0, 0.0
    ).astype(BF16)
    chosen = lax.dot_general(picks, places, NT, preferred_element_type=F32).astype(BF16)
    kept = jnp.dot(chosen, pair, preferred_element_type=F32).astype(BF16)
    stay_out[...] = kept[:128, :]
    go_out[...] = kept[128:, :]


def vmem():
    return pl.BlockSpec(memory_space=pltpu.VMEM)


def smem():
    return pl.BlockSpec(memory_space=pltpu.SMEM)


def segment(info, own, other, near, far, sign, rows, owners):
    span = own.shape[0]
    return pl.pallas_call(
        segment_kernel,
        in_specs=[smem()] + [vmem()] * 7,
        out_specs=[vmem()] * 3,
        out_shape=[jax.ShapeDtypeStruct((2 * HD, span), BF16)]
        + [jax.ShapeDtypeStruct((128, 2 * HD), BF16)] * 2,
        compiler_params=pltpu.CompilerParams(vmem_limit_bytes=24 << 20),
        cost_estimate=pl.CostEstimate(
            flops=400_000_000, bytes_accessed=2 << 20, transcendentals=0
        ),
    )(info, own, other, near, far, sign, rows, owners)


def attend_kernel(
    step, info, q, own, other, sib_own, sib_other, seg, sib_seg, stay, came, out, acc, total, top, held
):
    x, core = info[0], info[1]
    rows = q.shape[0]
    span = seg.shape[1]
    blocks = own.shape[1] // TILE
    prefix = ((own, other), (sib_own, sib_other))

    def prefix_tile(pair, columns):
        mine, theirs = pair
        keys = jnp.concatenate([mine[:HALF, columns], theirs[:HALF, columns]], 0)
        values = jnp.concatenate([mine[HALF:, columns], theirs[HALF:, columns]], 0)
        return keys, values

    squares = []
    for pair in prefix:
        for ref in pair:
            half = ref[:HALF, :].astype(F32)
            squares.append(jnp.sum(half * half, 0, keepdims=True))
    longest = jnp.maximum(jnp.max(squares[0] + squares[1]), jnp.max(squares[2] + squares[3]))
    for ref in (seg, sib_seg):
        part = ref[:HD, :].astype(F32)
        longest = jnp.maximum(longest, jnp.max(jnp.sum(part * part, 0, keepdims=True)))
    query_f = q[...].astype(F32)
    widest = jnp.max(jnp.sum(query_f * query_f, 1, keepdims=True))
    calm = longest * widest < SAFE_BOUND * SAFE_BOUND

    if step == 0:
        whole_flags = (None, core == 1)
    else:
        later = lax.rem(x + RING - step, RING) > x
        whole_flags = (later, later)

    def causal(begin, count):
        token = lax.rem(lax.broadcasted_iota(jnp.int32, (count, span), 0) + begin, span)
        return lax.broadcasted_iota(jnp.int32, (count, span), 1) <= token

    acc[...] = jnp.zeros_like(acc)
    total[...] = jnp.zeros_like(total)

    @pl.when(calm)
    def _():
        def tile(keys, values, masked=False):
            scores = jnp.dot(q[...], keys, preferred_element_type=F32)
            weights = jnp.exp2(scores)
            if masked:
                weights = jnp.where(causal(0, rows), weights, 0.0)
            part = weights[:, :HD]
            for i in range(1, TILE // HD):
                part = part + weights[:, i * HD:(i + 1) * HD]
            mixed = lax.dot_general(weights.astype(BF16), values, NT, preferred_element_type=F32)
            acc[...] += mixed
            total[...] += part

        for pair in prefix:
            def some_tiles(i, carry, pair=pair):
                for j in range(2):
                    begin = pl.multiple_of((2 * i + j) * TILE, TILE)
                    tile(*prefix_tile(pair, pl.ds(begin, TILE)))
                return carry

            lax.fori_loop(0, blocks // 2, some_tiles, 0)
        for ref, flag in zip((seg, sib_seg), whole_flags):
            if flag is None:
                tile(ref[:HD, :], ref[HD:, :], masked=True)
            else:
                @pl.when(flag)
                def _(ref=ref):
                    tile(ref[:HD, :], ref[HD:, :])
        top[...] = jnp.zeros_like(top)

    @pl.when(jnp.logical_not(calm))
    def _():
        top[...] = jnp.full_like(top, LOWEST)
        chunk = 256
        seg_flag = 1 if whole_flags[0] is None else whole_flags[0].astype(jnp.int32)
        sib_flag = whole_flags[1].astype(jnp.int32)

        def some_keys(b, carry):
            column = pl.ds(pl.multiple_of(lax.rem(b, blocks) * TILE, TILE), TILE)
            for number, pair in enumerate(prefix):
                @pl.when(b // blocks == number)
                def _(pair=pair):
                    for i in range(2):
                        for j, ref in enumerate(pair):
                            begin = i * HD + j * HALF
                            held[begin:begin + HALF, :] = ref[i * HALF:(i + 1) * HALF, column]

            for number, ref in enumerate((seg, sib_seg)):
                @pl.when(b == 2 * blocks + number)
                def _(ref=ref):
                    held[...] = ref[...]

            last = b == 2 * blocks
            flag = jnp.where(last, seg_flag, jnp.where(b > 2 * blocks, sib_flag, 1))
            causal_from = 0 if step else jnp.where(last, 0, -span)

            def some_rows(r, carry):
                begin = pl.multiple_of(r * chunk, chunk)
                at = pl.ds(begin, chunk)
                scores = jnp.dot(q[at, :], held[:HD, :], preferred_element_type=F32)
                if step == 0:
                    token = lax.rem(
                        lax.broadcasted_iota(jnp.int32, (chunk, span), 0) + begin, span
                    )
                    column = lax.broadcasted_iota(jnp.int32, (chunk, span), 1) + causal_from
                    scores = jnp.where(column <= token, scores, -jnp.inf)
                old = top[at, :]
                new = jnp.maximum(old, jnp.max(scores, 1, keepdims=True))
                weights = jnp.exp2(scores - new[:, :1])
                factor = jnp.exp2(old - new)
                part = weights[:, :HD]
                for i in range(1, TILE // HD):
                    part = part + weights[:, i * HD:(i + 1) * HD]
                mixed = lax.dot_general(
                    weights.astype(BF16), held[HD:, :], NT, preferred_element_type=F32
                )
                acc[at, :] = acc[at, :] * factor + mixed
                total[at, :] = total[at, :] * factor + part
                top[at, :] = new
                return carry

            @pl.when(flag == 1)
            def _():
                lax.fori_loop(0, rows // chunk, some_rows, 0)

            return carry

        lax.fori_loop(0, 2 * blocks + 2, some_keys, 0)

    summed = jnp.sum(total[...], 1, keepdims=True)
    out[:rows, :] = (acc[...] / summed).astype(BF16)
    level = top[...] + jnp.log2(summed)
    eye = lax.broadcasted_iota(jnp.int32, (1, HD, HD), 1) == lax.broadcasted_iota(
        jnp.int32, (1, HD, HD), 2
    )
    packed = jnp.sum(jnp.where(eye, level.reshape(rows // HD, HD, HD), 0.0), 1)
    high = packed.astype(BF16).astype(F32)
    rest = packed - high
    middle = rest.astype(BF16).astype(F32)
    low = rest - middle
    out[rows:rows + 32, :] = jnp.concatenate(
        [high, middle, low, jnp.zeros_like(high)], 0
    ).astype(BF16)
    back = (RING - step) % RING
    for i, ref in enumerate((stay, came, stay, came)):
        out[rows + 32 * (i + 1):rows + 32 * (i + 2), :] = ref[
            32 * back:32 * (back + 1), i // 2 * HD:(i // 2 + 1) * HD
        ]


def attend(step, info, q, *rest):
    rows = q.shape[0]
    return pl.pallas_call(
        functools.partial(attend_kernel, step),
        in_specs=[smem()] + [vmem()] * 9,
        out_specs=vmem(),
        out_shape=jax.ShapeDtypeStruct((rows + EXTRA, HD), BF16),
        scratch_shapes=[pltpu.VMEM((rows, HD), F32)] * 3 + [pltpu.VMEM((2 * HD, TILE), BF16)],
        compiler_params=pltpu.CompilerParams(vmem_limit_bytes=32 << 20),
        cost_estimate=pl.CostEstimate(
            flops=8 * rows * HD * 4096, bytes_accessed=4 << 20, transcendentals=rows * 4096
        ),
    )(info, q, *rest)


def split(value):
    high = value.astype(BF16)
    return high, (value - high.astype(F32)).astype(BF16)


def shuffle(rows, source):
    here = lax.broadcasted_iota(jnp.int32, (256, 256), 0)
    there = lax.broadcasted_iota(jnp.int32, (256, 256), 1)
    moves = jnp.where(source(here) == there, 1.0, 0.0).astype(BF16)
    return jnp.dot(moves, rows, preferred_element_type=F32).astype(BF16)


def merge_kernel(info, p0, p1, p2, p3, sign, *outs):
    parity = info[4]
    parts = (p0, p1, p2, p3)
    rows = p0.shape[0] - EXTRA
    count = rows // HD
    levels = []
    for part in parts:
        stats = part[rows:rows + 32, :].astype(F32)
        levels.append(stats[:count] + stats[count:2 * count] + stats[2 * count:3 * count])
    most = functools.reduce(jnp.maximum, levels)
    shares = [jnp.exp2(level - most) for level in levels]
    whole = functools.reduce(jnp.add, shares)
    shares = [share / whole for share in shares]
    eye = lax.broadcasted_iota(jnp.int32, (HD, HD), 0) == lax.broadcasted_iota(
        jnp.int32, (HD, HD), 1
    )
    turn = sign[parity]
    per_head = count // 2
    for b in range(count):
        left, right = [], []
        for share, part in zip(shares, parts):
            block = part[b * HD:(b + 1) * HD, :]
            high, low = split(share[b:b + 1, :])
            for piece in (high, low):
                left.append(jnp.where(eye, piece.astype(F32), 0.0).astype(BF16))
                right.append(block)
        mixed = jnp.dot(
            jnp.concatenate(left, 1), jnp.concatenate(right, 0), preferred_element_type=F32
        )
        high, low = split(mixed)
        plain = lax.dot_general(high, turn, NT, preferred_element_type=F32)
        plain = plain + lax.dot_general(low, turn, NT, preferred_element_type=F32)
        head, place = b // per_head, b % per_head
        block = (plain * HD ** -0.5).astype(BF16)
        for out in outs:
            out[place * HD:(place + 1) * HD, head * HD:(head + 1) * HD] = block
    kept = jnp.concatenate(
        [
            jnp.concatenate([part[rows + 32:rows + 96, :], part[rows + 96:, :]], 1)
            for part in parts
        ],
        0,
    )
    kept = shuffle(
        kept,
        lambda r: ((r >> 4) & 3) << 6 | ((r >> 3) & 1) << 5 | (r >> 6) << 3 | (r & 7),
    )
    for k, out in enumerate(outs):
        out[rows // 2:, :] = kept[64 * k:64 * (k + 1), :]


def merge(info, parts, sign):
    rows = parts[0].shape[0] - EXTRA
    return pl.pallas_call(
        merge_kernel,
        in_specs=[smem()] + [vmem()] * 5,
        out_specs=[vmem()] * RING,
        out_shape=[jax.ShapeDtypeStruct((rows // 2 + 64, 2 * HD), BF16)] * RING,
        compiler_params=pltpu.CompilerParams(vmem_limit_bytes=24 << 20),
        cost_estimate=pl.CostEstimate(
            flops=400_000_000, bytes_accessed=2 << 20, transcendentals=0
        ),
    )(info, *parts, sign)


def out_kernel(c0, c1, c2, c3, w0, w1, w2, w3, o0, o1, o2, o3, sum_out):
    outs = (o0, o1, o2, o3)
    contexts = (c0, c1, c2, c3)
    span = sum_out.shape[0]
    for k in (2, 1, 3, 0):
        columns = slice(k * 256, (k + 1) * 256)
        whole = None
        for c, w in zip(contexts, (w0, w1, w2, w3)):
            part = jnp.dot(c[:span, :], w[:, columns], preferred_element_type=F32)
            whole = part if whole is None else whole + part
        if k:
            outs[k][:span, :] = whole.astype(BF16)
        else:
            sum_out[...] = whole
    kept = jnp.concatenate([c[span:, :] for c in contexts], 0)
    kept = shuffle(
        kept,
        lambda r: ((r >> 4) & 3) << 6
        | ((r >> 2) & 3) << 4
        | ((r >> 1) & 1) << 3
        | (r >> 6) << 1
        | (r & 1),
    )
    for k, out in enumerate(outs):
        begin = span if k else 0
        out[begin:, :] = kept[64 * k:64 * (k + 1), :]


def project_out(contexts, weights):
    total = contexts[0].shape[0]
    span = total - 64
    return pl.pallas_call(
        out_kernel,
        in_specs=[vmem()] * 8,
        out_specs=[vmem()] * 5,
        out_shape=[jax.ShapeDtypeStruct((total if k else 64, 256), BF16) for k in range(4)]
        + [jax.ShapeDtypeStruct((span, 256), F32)],
        compiler_params=pltpu.CompilerParams(vmem_limit_bytes=24 << 20),
        cost_estimate=pl.CostEstimate(
            flops=2 * span * 1024 * 1024, bytes_accessed=5 << 20, transcendentals=0
        ),
    )(*contexts, *weights)


def finish_kernel(info, share, kept, a1, a2, a3, attn_out, kept_out):
    x, core, z, y = (info[i] for i in range(4))
    arrived = (a1, a2, a3)
    span = share.shape[0]
    whole = share[...]
    for part in arrived:
        whole = whole + part[:span, :].astype(F32)
    attn_out[...] = whole.astype(BF16)
    rows = jnp.concatenate([kept[...]] + [part[span:, :] for part in arrived], 0)
    place = lax.broadcasted_iota(jnp.int32, (1, 256), 1)
    back_second, back_first = place >> 6, (place >> 4) & 3
    from_x = (x + (place >> 2)) & 3
    from_core = (core + (place >> 1)) & 1
    from_z = (z - jnp.where(core == 0, back_first, back_second)) & 3
    from_y = (y - jnp.where(core == 0, back_second, back_first)) & 3
    target = device_at(from_x, from_core, from_z, from_y) * 2 + (place & 1)
    here = lax.broadcasted_iota(jnp.int32, (256, 256), 0)
    moves = jnp.where(here == target, 1.0, 0.0).astype(BF16)
    kept_out[...] = jnp.dot(moves, rows, preferred_element_type=F32).astype(BF16)


def finish(info, share, kept, arrived):
    return pl.pallas_call(
        finish_kernel,
        in_specs=[smem()] + [vmem()] * 5,
        out_specs=[vmem()] * 2,
        out_shape=[
            jax.ShapeDtypeStruct(share.shape, BF16),
            jax.ShapeDtypeStruct((256, 2 * HD), BF16),
        ],
        compiler_params=pltpu.CompilerParams(vmem_limit_bytes=24 << 20),
    )(info, share, kept, *arrived)


def shards(
    tokens, norm_gain, w_query, w_key, w_value, w_out, prefix_keys, prefix_values, keep_rows, owners
):
    seq = lax.axis_index("seq")
    tp = lax.axis_index("tp")
    seq_count = lax.axis_size("seq")
    span = tokens.shape[0]
    prefix_len = prefix_keys.shape[0] * seq_count
    info = jnp.stack(
        [seq // 2, seq % 2, tp // RING, tp % RING, tp % 2, seq, tp // 2, seq * 0]
    ).astype(jnp.int32)
    near, far = rope_tables(span, seq_count, prefix_len)
    near, far = jnp.asarray(near), jnp.asarray(far)
    sign = jnp.asarray(signs(), BF16)

    own = jnp.concatenate([prefix_keys.T, prefix_values.T], 0)
    other = to_head_pair(own)
    sib_own = to_sibling(own)
    q, kv, *pieces = project(
        info, tokens, norm_gain.reshape(-1, HD), w_query, w_key.T, w_value.T, near, far, sign, w_out
    )
    kv_other = to_head_pair(kv)
    queries = [q] + [along_x(q, d) for d in (1, 2, 3)]
    weights = [pieces[0]] + [along_first(pieces[d], d) for d in (1, 2, 3)]
    kv_other, other, queries[1], queries[3] = lax.optimization_barrier(
        (kv_other, other, queries[1], queries[3])
    )
    sib_other = to_sibling(other)
    seg, stay, go = segment(
        info, kv, kv_other, near, far, sign, keep_rows[0], owners.reshape(owners.shape[1:3])
    )
    came = to_sibling(go)
    sib_seg = to_sibling(seg)
    parts = [None] * RING
    for d in (3, 1, 2, 0):
        part = attend(
            d, info, queries[d], own, other, sib_own, sib_other, seg, sib_seg, stay, came
        )
        parts[d] = along_x(part, -d) if d else part
    contexts = merge(info, parts, sign)
    contexts = [contexts[0]] + [along_first(contexts[d], d) for d in (1, 2, 3)]
    *shares, share = project_out(contexts, weights)
    arrived = [along_second(shares[k], k) for k in (1, 2, 3)]
    return tuple(finish(info, share, shares[0], arrived))


def solution(mesh):
    return jax.shard_map(
        shards,
        mesh=mesh,
        in_specs=(
            P("seq", None),
            P(),
            P(None, "tp"),
            P(None, "tp"),
            P(None, "tp"),
            P("tp", None),
            P("seq", "tp"),
            P("seq", "tp"),
            P("seq", None, None),
            P("seq", None, None, None),
        ),
        out_specs=(P("seq", "tp"), P(("seq", "tp"), None)),
        check_vma=False,
    )
```

```python
import functools
import math

import jax
import jax.numpy as jnp
import numpy as np
from jax import lax
from jax.experimental import pallas as pl
from jax.experimental.pallas import tpu as pltpu
from jax.sharding import PartitionSpec as P

EPSILON = 1e-05
ROPE_BASE = 500000.0
LOWEST = -1e30
LOG2E = math.log2(math.e)
SAFE_BOUND = 60.0
HD = 128
HALF = 64
AXES = ("seq", "tp")
RING = 4
TILE = 512
CHUNKS = 4
EXTRA = 32 + 128

NT = (((1,), (1,)), ((), ()))
TN = (((0,), (1,)), ((), ()))
F32 = jnp.float32
BF16 = jnp.bfloat16


def device_at(x, core, z, y):
    return ((x & 3) * 2 + core) * 16 + (z & 3) * 4 + (y & 3)


def pairs_of(move):
    return [
        (device_at(x, c, z, y), device_at(*move(x, c, z, y)))
        for x in range(RING)
        for c in range(2)
        for z in range(RING)
        for y in range(RING)
    ]


def send(value, move):
    return lax.ppermute(value, AXES, pairs_of(move))


def to_sibling(value):
    return send(value, lambda x, c, z, y: (x, 1 - c, z, y))


def to_head_pair(value):
    return send(value, lambda x, c, z, y: (x, c, z, y ^ 1))


def along_x(value, step):
    return send(value, lambda x, c, z, y: (x + step, c, z, y))


def along_first(value, step):
    return send(
        value, lambda x, c, z, y: (x, c, z + step, y) if c == 0 else (x, c, z, y + step)
    )


def along_second(value, step):
    return send(
        value, lambda x, c, z, y: (x, c, z, y + step) if c == 0 else (x, c, z + step, y)
    )


def position():
    seq, tp = lax.axis_index("seq"), lax.axis_index("tp")
    return seq >> 1, seq & 1, tp >> 2, tp & 3, tp & 1, seq, tp >> 1


def signs():
    index = np.arange(HD)
    both = index[:, None] & index[None, :]
    parity = np.zeros((HD, HD), np.int64)
    for bit in range(7):
        parity += both >> bit & 1
    plain = (1 - 2 * (parity % 2)).astype(np.float32)
    return np.stack([plain, np.roll(plain, HALF, axis=1)])


def rope_tables(span, spans, prefix):
    freq = np.exp(-np.arange(HALF) * (2.0 * math.log(ROPE_BASE) / HD))
    freq = np.concatenate([freq, freq])
    near = np.arange(span)[:, None] * freq[None, :]
    far = (prefix + span * np.arange(spans))[:, None] * freq[None, :]
    near = np.stack([np.cos(near), np.sin(near)]).astype(np.float32)
    far = np.stack([np.cos(far), np.sin(far)]).astype(np.float32)
    return near, far


def rope_factors(near, far, number):
    cos_far, sin_far = far[0, pl.ds(number, 1), :], far[1, pl.ds(number, 1), :]
    cosine = near[0] * cos_far - near[1] * sin_far
    sine = near[1] * cos_far + near[0] * sin_far
    lane = lax.broadcasted_iota(jnp.int32, (1, HD), 1)
    return cosine, jnp.where(lane < HALF, -sine, sine)


def project_kernel(
    tokens, gain, w_q, w_kt, w_vt, near, far, sign, w_out, q_out, kv_out, w0, w1, w2, w3,
    held, held_q, held_kv, held_near, held_w, sum_q, sum_kv, sems, cut_sems,
):
    x, core, z, y, parity, number, group = position()
    span, width = tokens.shape
    block = width // CHUNKS
    parts = [pl.ds(i * block, block) for i in range(CHUNKS)]
    arrive = []
    for i, at in enumerate(parts):
        moves = (
            (tokens.at[:, at], held.at[:, at]),
            (w_q.at[at], held_q.at[at]),
            (w_kt.at[:, at], held_kv.at[:HALF, at]),
            (w_vt.at[:, at], held_kv.at[HALF:, at]),
        )
        arrive.append([
            pltpu.make_async_copy(start, end, sems.at[4 * i + j])
            for j, (start, end) in enumerate(moves)
        ])
    tables = pltpu.make_async_copy(near, held_near, sems.at[4 * CHUNKS])
    for copies in arrive:
        for copy in copies:
            copy.start()
    tables.start()
    whole = pltpu.make_async_copy(w_out, held_w, sems.at[4 * CHUNKS + 1])
    whole.start()
    cuts = []
    for d, piece in enumerate((w0, w1, w2, w3)):
        for k in range(RING):
            row = (z + jnp.where(core == 0, d, k)) & 3
            col = (y + jnp.where(core == 0, k, d)) & 3
            begin = pl.multiple_of((row * RING + col) * 256, 256)
            cuts.append(
                pltpu.make_async_copy(
                    held_w.at[:, pl.ds(begin, 256)],
                    piece.at[:, pl.ds(k * 256, 256)],
                    cut_sems.at[d * RING + k],
                )
            )
    squares = None
    per = block // HD
    for i, at in enumerate(parts):
        for copy in arrive[i]:
            copy.wait()
        gains = jnp.concatenate([gain[j:j + 1, :] for j in range(i * per, (i + 1) * per)], 1)
        begin, end = i * block, (i + 1) * block
        hidden = held[:, begin:end].astype(F32)
        weighted = (hidden * gains.astype(F32)).astype(BF16)
        hidden = hidden * hidden
        for j in range(per):
            square = hidden[:, j * HD:(j + 1) * HD]
            squares = square if squares is None else squares + square
        part_q = jnp.dot(weighted, held_q[begin:end, :], preferred_element_type=F32)
        part_kv = lax.dot_general(
            weighted, held_kv[:, begin:end], NT, preferred_element_type=F32
        )
        if i == 0:
            sum_q[...] = part_q
            sum_kv[...] = part_kv
        else:
            sum_q[...] += part_q
            sum_kv[...] += part_kv
    whole.wait()
    for copy in cuts:
        copy.start()
    scale = lax.rsqrt(jnp.sum(squares, -1, keepdims=True) / width + EPSILON)
    kv_out[...] = (sum_kv[...] * scale).astype(BF16)
    tables.wait()
    cosine, sine = rope_factors(held_near, far, number)
    turn = sign[parity]
    for h in range(2):
        head = sum_q[:, h * HD:(h + 1) * HD] * scale
        head = head * cosine + pltpu.roll(head, HALF, 1) * sine
        head = (head * HD ** -0.5).astype(BF16)
        head = jnp.dot(head, turn, preferred_element_type=F32)
        q_out[h * span:(h + 1) * span, :] = (head * (HD ** -0.5 * LOG2E)).astype(BF16)
    for copy in cuts:
        copy.wait()


def project(tokens, gain, w_q, w_kt, w_vt, near, far, sign, w_out):
    span, width = tokens.shape
    remain = pl.BlockSpec(memory_space=pl.ANY)
    return pl.pallas_call(
        project_kernel,
        in_specs=[remain, vmem()] + [remain] * 4 + [vmem(), vmem(), remain],
        out_specs=[vmem(), vmem()] + [remain] * 4,
        out_shape=[
            jax.ShapeDtypeStruct((2 * span, HD), BF16),
            jax.ShapeDtypeStruct((span, HD), BF16),
        ] + [jax.ShapeDtypeStruct((w_out.shape[0], 1024), BF16)] * 4,
        scratch_shapes=[
            pltpu.VMEM((span, width), BF16),
            pltpu.VMEM((width, 2 * HD), BF16),
            pltpu.VMEM((HD, width), BF16),
            pltpu.VMEM(near.shape, F32),
            pltpu.VMEM(w_out.shape, BF16),
            pltpu.VMEM((span, 2 * HD), F32),
            pltpu.VMEM((span, HD), F32),
            pltpu.SemaphoreType.DMA((4 * CHUNKS + 2,)),
            pltpu.SemaphoreType.DMA((RING * RING,)),
        ],
        compiler_params=pltpu.CompilerParams(vmem_limit_bytes=60 << 20),
        cost_estimate=pl.CostEstimate(
            flops=2 * span * width * 384, bytes_accessed=7 << 20, transcendentals=0
        ),
    )(tokens, gain, w_q, w_kt, w_vt, near, far, sign, w_out)


def segment_kernel(own, other, near, far, sign, rows, owners, seg_out, stay_out, go_out):
    x, core, z, y, parity, number, group = position()
    odd = parity == 1
    mine, theirs = own[...].astype(F32), other[...].astype(F32)
    first = jnp.where(odd, theirs, mine)
    second = jnp.where(odd, mine, theirs)
    lane = lax.broadcasted_iota(jnp.int32, (1, HD), 1)
    key = jnp.where(lane < HALF, first, pltpu.roll(second, HALF, 1))
    value = jnp.where(lane < HALF, pltpu.roll(first, HALF, 1), second).astype(BF16)
    cosine, sine = rope_factors(near, far, number)
    key = (key * cosine + pltpu.roll(key, HALF, 1) * sine).astype(BF16)
    turn = sign[parity]
    unit = HD ** -0.5
    seg_out[:HD, :] = (lax.dot_general(turn, key, TN, preferred_element_type=F32) * unit).astype(BF16)
    seg_out[HD:, :] = (lax.dot_general(turn, value, TN, preferred_element_type=F32) * unit).astype(BF16)
    plain = sign[0]
    pair = jnp.concatenate(
        [
            (jnp.dot(key, plain, preferred_element_type=F32) * unit).astype(BF16),
            (jnp.dot(value, plain, preferred_element_type=F32) * unit).astype(BF16),
        ],
        1,
    )
    span, keep = own.shape[0], rows.shape[1]
    row = rows[pl.ds(group, 1), :]
    owner = owners[pl.ds(group, 1), :]
    place = lax.broadcasted_iota(jnp.int32, (256, 1), 0)
    to_core = jnp.where(place >= 128, 1 - core, core)
    step_first, step_second = (place >> 3) & 3, (place >> 1) & 3
    to_x = (x + (place >> 5)) & 3
    to_z = (z + jnp.where(to_core == 0, step_first, step_second)) & 3
    to_y = (y + jnp.where(to_core == 0, step_second, step_first)) & 3
    named = owner == device_at(to_x, to_core, to_z, to_y)
    before = lax.broadcasted_iota(jnp.int32, (keep, keep), 0) < lax.broadcasted_iota(
        jnp.int32, (keep, keep), 1
    )
    rank = jnp.dot(
        jnp.where(named, 1.0, 0.0).astype(BF16),
        jnp.where(before, 1.0, 0.0).astype(BF16),
        preferred_element_type=F32,
    )
    slot = (2 * parity + (place & 1)).astype(F32)
    picks = jnp.where(jnp.logical_and(named, rank == slot), 1.0, 0.0).astype(BF16)
    places = jnp.where(
        lax.broadcasted_iota(jnp.int32, (span, keep), 0) == row, 1.0, 0.0
    ).astype(BF16)
    chosen = lax.dot_general(picks, places, NT, preferred_element_type=F32).astype(BF16)
    kept = jnp.dot(chosen, pair, preferred_element_type=F32).astype(BF16)
    stay_out[...] = kept[:128, :]
    go_out[...] = kept[128:, :]


def vmem():
    return pl.BlockSpec(memory_space=pltpu.VMEM)


def segment(own, other, near, far, sign, rows, owners):
    span = own.shape[0]
    return pl.pallas_call(
        segment_kernel,
        in_specs=[vmem()] * 7,
        out_specs=[vmem()] * 3,
        out_shape=[jax.ShapeDtypeStruct((2 * HD, span), BF16)]
        + [jax.ShapeDtypeStruct((128, 2 * HD), BF16)] * 2,
        compiler_params=pltpu.CompilerParams(vmem_limit_bytes=24 << 20),
        cost_estimate=pl.CostEstimate(
            flops=400_000_000, bytes_accessed=2 << 20, transcendentals=0
        ),
    )(own, other, near, far, sign, rows, owners)


def attend_kernel(
    step, q, own, other, sib_own, sib_other, seg, sib_seg, stay, came, out, acc, total, top, held
):
    x, core = position()[:2]
    rows = q.shape[0]
    span = seg.shape[1]
    blocks = own.shape[1] // TILE
    prefix = ((own, other), (sib_own, sib_other))

    def prefix_tile(pair, columns):
        mine, theirs = pair
        keys = jnp.concatenate([mine[:HALF, columns], theirs[:HALF, columns]], 0)
        values = jnp.concatenate([mine[HALF:, columns], theirs[HALF:, columns]], 0)
        return keys, values

    squares = []
    for pair in prefix:
        for ref in pair:
            half = ref[:HALF, :].astype(F32)
            squares.append(jnp.sum(half * half, 0, keepdims=True))
    longest = jnp.maximum(jnp.max(squares[0] + squares[1]), jnp.max(squares[2] + squares[3]))
    for ref in (seg, sib_seg):
        part = ref[:HD, :].astype(F32)
        longest = jnp.maximum(longest, jnp.max(jnp.sum(part * part, 0, keepdims=True)))
    query_f = q[...].astype(F32)
    widest = jnp.max(jnp.sum(query_f * query_f, 1, keepdims=True))
    calm = longest * widest < SAFE_BOUND * SAFE_BOUND

    if step == 0:
        whole_flags = (None, core == 1)
    else:
        later = lax.rem(x + RING - step, RING) > x
        whole_flags = (later, later)

    def causal(begin, count):
        token = lax.rem(lax.broadcasted_iota(jnp.int32, (count, span), 0) + begin, span)
        return lax.broadcasted_iota(jnp.int32, (count, span), 1) <= token

    acc[...] = jnp.zeros_like(acc)
    total[...] = jnp.zeros_like(total)

    @pl.when(calm)
    def _():
        def tile(keys, values, masked=False):
            scores = jnp.dot(q[...], keys, preferred_element_type=F32)
            weights = jnp.exp2(scores)
            if masked:
                weights = jnp.where(causal(0, rows), weights, 0.0)
            part = weights[:, :HD]
            for i in range(1, TILE // HD):
                part = part + weights[:, i * HD:(i + 1) * HD]
            mixed = lax.dot_general(weights.astype(BF16), values, NT, preferred_element_type=F32)
            acc[...] += mixed
            total[...] += part

        for pair in prefix:
            def some_tiles(i, carry, pair=pair):
                for j in range(2):
                    begin = pl.multiple_of((2 * i + j) * TILE, TILE)
                    tile(*prefix_tile(pair, pl.ds(begin, TILE)))
                return carry

            lax.fori_loop(0, blocks // 2, some_tiles, 0)
        for ref, flag in zip((seg, sib_seg), whole_flags):
            if flag is None:
                tile(ref[:HD, :], ref[HD:, :], masked=True)
            else:
                @pl.when(flag)
                def _(ref=ref):
                    tile(ref[:HD, :], ref[HD:, :])
        top[...] = jnp.zeros_like(top)

    @pl.when(jnp.logical_not(calm))
    def _():
        top[...] = jnp.full_like(top, LOWEST)
        chunk = 256
        seg_flag = 1 if whole_flags[0] is None else whole_flags[0].astype(jnp.int32)
        sib_flag = whole_flags[1].astype(jnp.int32)

        def some_keys(b, carry):
            column = pl.ds(pl.multiple_of(lax.rem(b, blocks) * TILE, TILE), TILE)
            for number, pair in enumerate(prefix):
                @pl.when(b // blocks == number)
                def _(pair=pair):
                    for i in range(2):
                        for j, ref in enumerate(pair):
                            begin = i * HD + j * HALF
                            held[begin:begin + HALF, :] = ref[i * HALF:(i + 1) * HALF, column]

            for number, ref in enumerate((seg, sib_seg)):
                @pl.when(b == 2 * blocks + number)
                def _(ref=ref):
                    held[...] = ref[...]

            last = b == 2 * blocks
            flag = jnp.where(last, seg_flag, jnp.where(b > 2 * blocks, sib_flag, 1))
            causal_from = 0 if step else jnp.where(last, 0, -span)

            def some_rows(r, carry):
                begin = pl.multiple_of(r * chunk, chunk)
                at = pl.ds(begin, chunk)
                scores = jnp.dot(q[at, :], held[:HD, :], preferred_element_type=F32)
                if step == 0:
                    token = lax.rem(
                        lax.broadcasted_iota(jnp.int32, (chunk, span), 0) + begin, span
                    )
                    column = lax.broadcasted_iota(jnp.int32, (chunk, span), 1) + causal_from
                    scores = jnp.where(column <= token, scores, -jnp.inf)
                old = top[at, :]
                new = jnp.maximum(old, jnp.max(scores, 1, keepdims=True))
                weights = jnp.exp2(scores - new[:, :1])
                factor = jnp.exp2(old - new)
                part = weights[:, :HD]
                for i in range(1, TILE // HD):
                    part = part + weights[:, i * HD:(i + 1) * HD]
                mixed = lax.dot_general(
                    weights.astype(BF16), held[HD:, :], NT, preferred_element_type=F32
                )
                acc[at, :] = acc[at, :] * factor + mixed
                total[at, :] = total[at, :] * factor + part
                top[at, :] = new
                return carry

            @pl.when(flag == 1)
            def _():
                lax.fori_loop(0, rows // chunk, some_rows, 0)

            return carry

        lax.fori_loop(0, 2 * blocks + 2, some_keys, 0)

    summed = jnp.sum(total[...], 1, keepdims=True)
    out[:rows, :] = (acc[...] / summed).astype(BF16)
    level = top[...] + jnp.log2(summed)
    eye = lax.broadcasted_iota(jnp.int32, (1, HD, HD), 1) == lax.broadcasted_iota(
        jnp.int32, (1, HD, HD), 2
    )
    packed = jnp.sum(jnp.where(eye, level.reshape(rows // HD, HD, HD), 0.0), 1)
    high = packed.astype(BF16).astype(F32)
    rest = packed - high
    middle = rest.astype(BF16).astype(F32)
    low = rest - middle
    out[rows:rows + 32, :] = jnp.concatenate(
        [high, middle, low, jnp.zeros_like(high)], 0
    ).astype(BF16)
    back = (RING - step) % RING
    for i, ref in enumerate((stay, came, stay, came)):
        out[rows + 32 * (i + 1):rows + 32 * (i + 2), :] = ref[
            32 * back:32 * (back + 1), i // 2 * HD:(i // 2 + 1) * HD
        ]


def attend(step, q, *rest):
    rows = q.shape[0]
    return pl.pallas_call(
        functools.partial(attend_kernel, step),
        in_specs=[vmem()] * 9,
        out_specs=vmem(),
        out_shape=jax.ShapeDtypeStruct((rows + EXTRA, HD), BF16),
        scratch_shapes=[pltpu.VMEM((rows, HD), F32)] * 3 + [pltpu.VMEM((2 * HD, TILE), BF16)],
        compiler_params=pltpu.CompilerParams(vmem_limit_bytes=32 << 20),
        cost_estimate=pl.CostEstimate(
            flops=8 * rows * HD * 4096, bytes_accessed=4 << 20, transcendentals=rows * 4096
        ),
    )(q, *rest)


def shuffle(rows, source):
    here = lax.broadcasted_iota(jnp.int32, (256, 256), 0)
    there = lax.broadcasted_iota(jnp.int32, (256, 256), 1)
    moves = jnp.where(source(here) == there, 1.0, 0.0).astype(BF16)
    return jnp.dot(moves, rows, preferred_element_type=F32).astype(BF16)


def merge_kernel(p0, p1, p2, p3, sign, *outs):
    parity = position()[4]
    parts = (p0, p1, p2, p3)
    rows = p0.shape[0] - EXTRA
    count = rows // HD
    levels = []
    for part in parts:
        stats = part[rows:rows + 32, :].astype(F32)
        levels.append(stats[:count] + stats[count:2 * count] + stats[2 * count:3 * count])
    most = functools.reduce(jnp.maximum, levels)
    shares = [jnp.exp2(level - most) for level in levels]
    whole = functools.reduce(jnp.add, shares)
    shares = [share / whole for share in shares]
    eye = lax.broadcasted_iota(jnp.int32, (HD, HD), 0) == lax.broadcasted_iota(
        jnp.int32, (HD, HD), 1
    )
    turn = sign[parity]
    per_head = count // 2
    for b in range(count):
        left, right = [], []
        for share, part in zip(shares, parts):
            block = part[b * HD:(b + 1) * HD, :]
            left.append(jnp.where(eye, share[b:b + 1, :], 0.0).astype(BF16))
            right.append(block)
        mixed = jnp.dot(
            jnp.concatenate(left, 1), jnp.concatenate(right, 0), preferred_element_type=F32
        )
        plain = lax.dot_general(mixed.astype(BF16), turn, NT, preferred_element_type=F32)
        head, place = b // per_head, b % per_head
        block = (plain * HD ** -0.5).astype(BF16)
        for out in outs:
            out[place * HD:(place + 1) * HD, head * HD:(head + 1) * HD] = block
    kept = jnp.concatenate(
        [
            jnp.concatenate([part[rows + 32:rows + 96, :], part[rows + 96:, :]], 1)
            for part in parts
        ],
        0,
    )
    kept = shuffle(
        kept,
        lambda r: ((r >> 4) & 3) << 6 | ((r >> 3) & 1) << 5 | (r >> 6) << 3 | (r & 7),
    )
    for k, out in enumerate(outs):
        out[rows // 2:, :] = kept[64 * k:64 * (k + 1), :]


def merge(parts, sign):
    rows = parts[0].shape[0] - EXTRA
    return pl.pallas_call(
        merge_kernel,
        in_specs=[vmem()] * 5,
        out_specs=[vmem()] * RING,
        out_shape=[jax.ShapeDtypeStruct((rows // 2 + 64, 2 * HD), BF16)] * RING,
        compiler_params=pltpu.CompilerParams(vmem_limit_bytes=24 << 20),
        cost_estimate=pl.CostEstimate(
            flops=400_000_000, bytes_accessed=2 << 20, transcendentals=0
        ),
    )(*parts, sign)


def out_kernel(c0, c1, c2, c3, w0, w1, w2, w3, o0, o1, o2, o3, sum_out):
    outs = (o0, o1, o2, o3)
    contexts = (c0, c1, c2, c3)
    span = sum_out.shape[0]
    for k in (2, 1, 3, 0):
        columns = slice(k * 256, (k + 1) * 256)
        whole = None
        for c, w in zip(contexts, (w0, w1, w2, w3)):
            part = jnp.dot(c[:span, :], w[:, columns], preferred_element_type=F32)
            whole = part if whole is None else whole + part
        if k:
            outs[k][:span, :] = whole.astype(BF16)
        else:
            sum_out[...] = whole
    kept = jnp.concatenate([c[span:, :] for c in contexts], 0)
    kept = shuffle(
        kept,
        lambda r: ((r >> 4) & 3) << 6
        | ((r >> 2) & 3) << 4
        | ((r >> 1) & 1) << 3
        | (r >> 6) << 1
        | (r & 1),
    )
    for k, out in enumerate(outs):
        begin = span if k else 0
        out[begin:, :] = kept[64 * k:64 * (k + 1), :]


def project_out(contexts, weights):
    total = contexts[0].shape[0]
    span = total - 64
    return pl.pallas_call(
        out_kernel,
        in_specs=[vmem()] * 8,
        out_specs=[vmem()] * 5,
        out_shape=[jax.ShapeDtypeStruct((total if k else 64, 256), BF16) for k in range(4)]
        + [jax.ShapeDtypeStruct((span, 256), F32)],
        compiler_params=pltpu.CompilerParams(vmem_limit_bytes=24 << 20),
        cost_estimate=pl.CostEstimate(
            flops=2 * span * 1024 * 1024, bytes_accessed=5 << 20, transcendentals=0
        ),
    )(*contexts, *weights)


def finish_kernel(share, kept, a1, a2, a3, attn_out, kept_out):
    x, core, z, y = position()[:4]
    arrived = (a1, a2, a3)
    span = share.shape[0]
    whole = share[...]
    for part in arrived:
        whole = whole + part[:span, :].astype(F32)
    attn_out[...] = whole.astype(BF16)
    rows = jnp.concatenate([kept[...]] + [part[span:, :] for part in arrived], 0)
    place = lax.broadcasted_iota(jnp.int32, (1, 256), 1)
    back_second, back_first = place >> 6, (place >> 4) & 3
    from_x = (x + (place >> 2)) & 3
    from_core = (core + (place >> 1)) & 1
    from_z = (z - jnp.where(core == 0, back_first, back_second)) & 3
    from_y = (y - jnp.where(core == 0, back_second, back_first)) & 3
    target = device_at(from_x, from_core, from_z, from_y) * 2 + (place & 1)
    here = lax.broadcasted_iota(jnp.int32, (256, 256), 0)
    moves = jnp.where(here == target, 1.0, 0.0).astype(BF16)
    kept_out[...] = jnp.dot(moves, rows, preferred_element_type=F32).astype(BF16)


def finish(share, kept, arrived):
    return pl.pallas_call(
        finish_kernel,
        in_specs=[vmem()] * 5,
        out_specs=[vmem()] * 2,
        out_shape=[
            jax.ShapeDtypeStruct(share.shape, BF16),
            jax.ShapeDtypeStruct((256, 2 * HD), BF16),
        ],
        compiler_params=pltpu.CompilerParams(vmem_limit_bytes=24 << 20),
    )(share, kept, *arrived)


def shards(
    tokens, norm_gain, w_query, w_key, w_value, w_out, prefix_keys, prefix_values, keep_rows, owners
):
    seq_count = lax.axis_size("seq")
    span = tokens.shape[0]
    prefix_len = prefix_keys.shape[0] * seq_count
    near, far = rope_tables(span, seq_count, prefix_len)
    near, far = jnp.asarray(near), jnp.asarray(far)
    sign = jnp.asarray(signs(), BF16)

    own = jnp.concatenate([prefix_keys.T, prefix_values.T], 0)
    other = to_head_pair(own)
    sib_own = to_sibling(own)
    q, kv, *pieces = project(
        tokens, norm_gain.reshape(-1, HD), w_query, w_key.T, w_value.T, near, far, sign, w_out
    )
    kv_other = to_head_pair(kv)
    queries = [q] + [along_x(q, d) for d in (1, 2, 3)]
    weights = [pieces[0]] + [along_first(pieces[d], d) for d in (1, 2, 3)]
    kv_other, other, queries[1], queries[3] = lax.optimization_barrier(
        (kv_other, other, queries[1], queries[3])
    )
    sib_other = to_sibling(other)
    seg, stay, go = segment(
        kv, kv_other, near, far, sign, keep_rows[0], owners.reshape(owners.shape[1:3])
    )
    came = to_sibling(go)
    sib_seg = to_sibling(seg)
    queries[3], weights[2] = lax.optimization_barrier((queries[3], weights[2]))
    parts = [None] * RING
    for d in (3, 1, 2, 0):
        part = attend(
            d, queries[d], own, other, sib_own, sib_other, seg, sib_seg, stay, came
        )
        parts[d] = along_x(part, -d) if d else part
    contexts = merge(parts, sign)
    contexts = [contexts[0]] + [along_first(contexts[d], d) for d in (1, 2, 3)]
    *shares, share = project_out(contexts, weights)
    arrived = [along_second(shares[k], k) for k in (1, 2, 3)]
    return tuple(finish(share, shares[0], arrived))


def solution(mesh):
    return jax.shard_map(
        shards,
        mesh=mesh,
        in_specs=(
            P("seq", None),
            P(),
            P(None, "tp"),
            P(None, "tp"),
            P(None, "tp"),
            P("tp", None),
            P("seq", "tp"),
            P("seq", "tp"),
            P("seq", None, None),
            P("seq", None, None, None),
        ),
        out_specs=(P("seq", "tp"), P(("seq", "tp"), None)),
        check_vma=False,
    )
```

```python
import functools
import math

import jax
import jax.numpy as jnp
import numpy as np
from jax import lax
from jax.experimental import pallas as pl
from jax.experimental.pallas import tpu as pltpu
from jax.sharding import PartitionSpec as P

EPSILON = 1e-05
ROPE_BASE = 500000.0
LOWEST = -1e30
LOG2E = math.log2(math.e)
SAFE_BOUND = 60.0
HD = 128
HALF = 64
AXES = ("seq", "tp")
RING = 4
TILE = 512
CHUNKS = 4
CUT_AT = 2
WHOLE_AT = 1
NOTE = 16
EXTRA = 32 + 128

NT = (((1,), (1,)), ((), ()))
TN = (((0,), (1,)), ((), ()))
F32 = jnp.float32
BF16 = jnp.bfloat16


def device_at(x, core, z, y):
    return ((x & 3) * 2 + core) * 16 + (z & 3) * 4 + (y & 3)


def pairs_of(move):
    return [
        (device_at(x, c, z, y), device_at(*move(x, c, z, y)))
        for x in range(RING)
        for c in range(2)
        for z in range(RING)
        for y in range(RING)
    ]


def send(value, move):
    return lax.ppermute(value, AXES, pairs_of(move))


def to_sibling(value):
    return send(value, lambda x, c, z, y: (x, 1 - c, z, y))


def to_head_pair(value):
    return send(value, lambda x, c, z, y: (x, c, z, y ^ 1))


def along_x(value, step):
    return send(value, lambda x, c, z, y: (x + step, c, z, y))


def along_first(value, step):
    return send(
        value, lambda x, c, z, y: (x, c, z + step, y) if c == 0 else (x, c, z, y + step)
    )


def along_second(value, step):
    return send(
        value, lambda x, c, z, y: (x, c, z, y + step) if c == 0 else (x, c, z + step, y)
    )


def position():
    seq, tp = lax.axis_index("seq"), lax.axis_index("tp")
    return seq >> 1, seq & 1, tp >> 2, tp & 3, tp & 1, seq, tp >> 1


def signs():
    index = np.arange(HD)
    both = index[:, None] & index[None, :]
    parity = np.zeros((HD, HD), np.int64)
    for bit in range(7):
        parity += both >> bit & 1
    plain = (1 - 2 * (parity % 2)).astype(np.float32)
    return np.stack([plain, np.roll(plain, HALF, axis=1)])


def rope_tables(span, spans, prefix):
    freq = np.exp(-np.arange(HALF) * (2.0 * math.log(ROPE_BASE) / HD))
    freq = np.concatenate([freq, freq])
    near = np.arange(span)[:, None] * freq[None, :]
    far = (prefix + span * np.arange(spans))[:, None] * freq[None, :]
    near = np.stack([np.cos(near), np.sin(near)]).astype(np.float32)
    far = np.stack([np.cos(far), np.sin(far)]).astype(np.float32)
    return near, far


def rope_factors(near, far, number):
    cos_far, sin_far = far[0, pl.ds(number, 1), :], far[1, pl.ds(number, 1), :]
    cosine = near[0] * cos_far - near[1] * sin_far
    sine = near[1] * cos_far + near[0] * sin_far
    lane = lax.broadcasted_iota(jnp.int32, (1, HD), 1)
    return cosine, jnp.where(lane < HALF, -sine, sine)


def project_kernel(
    tokens, gain, w_q, w_kt, w_vt, near, far, sign, w_out, q_out, kv_out, w0, w1, w2, w3,
    held, held_q, held_kv, held_near, held_w, sum_q, sum_kv, sems, cut_sems,
):
    x, core, z, y, parity, number, group = position()
    span, width = tokens.shape
    block = width // CHUNKS
    parts = [pl.ds(i * block, block) for i in range(CHUNKS)]
    arrive = []
    for i, at in enumerate(parts):
        moves = (
            (tokens.at[:, at], held.at[:, at]),
            (w_q.at[at], held_q.at[at]),
            (w_kt.at[:, at], held_kv.at[:HALF, at]),
            (w_vt.at[:, at], held_kv.at[HALF:, at]),
        )
        arrive.append([
            pltpu.make_async_copy(start, end, sems.at[4 * i + j])
            for j, (start, end) in enumerate(moves)
        ])
    tables = pltpu.make_async_copy(near, held_near, sems.at[4 * CHUNKS])
    whole = pltpu.make_async_copy(w_out, held_w, sems.at[4 * CHUNKS + 1])
    for i, copies in enumerate(arrive):
        for copy in copies:
            copy.start()
        if i == WHOLE_AT:
            whole.start()
    tables.start()
    cuts = []
    for d, piece in enumerate((w0, w1, w2, w3)):
        for k in range(RING):
            row = (z + jnp.where(core == 0, d, k)) & 3
            col = (y + jnp.where(core == 0, k, d)) & 3
            begin = pl.multiple_of((row * RING + col) * 256, 256)
            cuts.append(
                pltpu.make_async_copy(
                    held_w.at[:, pl.ds(begin, 256)],
                    piece.at[:, pl.ds(k * 256, 256)],
                    cut_sems.at[d * RING + k],
                )
            )
    squares = None
    per = block // HD
    for i, at in enumerate(parts):
        for copy in arrive[i]:
            copy.wait()
        if i == CUT_AT:
            whole.wait()
            for copy in cuts:
                copy.start()
        gains = jnp.concatenate([gain[j:j + 1, :] for j in range(i * per, (i + 1) * per)], 1)
        begin, end = i * block, (i + 1) * block
        hidden = held[:, begin:end].astype(F32)
        weighted = (hidden * gains.astype(F32)).astype(BF16)
        hidden = hidden * hidden
        for j in range(per):
            square = hidden[:, j * HD:(j + 1) * HD]
            squares = square if squares is None else squares + square
        part_q = jnp.dot(weighted, held_q[begin:end, :], preferred_element_type=F32)
        part_kv = lax.dot_general(
            weighted, held_kv[:, begin:end], NT, preferred_element_type=F32
        )
        if i == 0:
            sum_q[...] = part_q
            sum_kv[...] = part_kv
        else:
            sum_q[...] += part_q
            sum_kv[...] += part_kv
    scale = lax.rsqrt(jnp.sum(squares, -1, keepdims=True) / width + EPSILON)
    kv_out[...] = (sum_kv[...] * scale).astype(BF16)
    tables.wait()
    cosine, sine = rope_factors(held_near, far, number)
    turn = sign[parity]
    for h in range(2):
        head = sum_q[:, h * HD:(h + 1) * HD] * scale
        head = head * cosine + pltpu.roll(head, HALF, 1) * sine
        head = (head * HD ** -0.5).astype(BF16)
        head = jnp.dot(head, turn, preferred_element_type=F32)
        q_out[h * span:(h + 1) * span, :] = (head * (HD ** -0.5 * LOG2E)).astype(BF16)
    for copy in cuts:
        copy.wait()


def project(tokens, gain, w_q, w_kt, w_vt, near, far, sign, w_out):
    span, width = tokens.shape
    remain = pl.BlockSpec(memory_space=pl.ANY)
    return pl.pallas_call(
        project_kernel,
        in_specs=[remain, vmem()] + [remain] * 4 + [vmem(), vmem(), remain],
        out_specs=[vmem(), vmem()] + [remain] * 4,
        out_shape=[
            jax.ShapeDtypeStruct((2 * span, HD), BF16),
            jax.ShapeDtypeStruct((span, HD), BF16),
        ] + [jax.ShapeDtypeStruct((w_out.shape[0], 1024), BF16)] * 4,
        scratch_shapes=[
            pltpu.VMEM((span, width), BF16),
            pltpu.VMEM((width, 2 * HD), BF16),
            pltpu.VMEM((HD, width), BF16),
            pltpu.VMEM(near.shape, F32),
            pltpu.VMEM(w_out.shape, BF16),
            pltpu.VMEM((span, 2 * HD), F32),
            pltpu.VMEM((span, HD), F32),
            pltpu.SemaphoreType.DMA((4 * CHUNKS + 2,)),
            pltpu.SemaphoreType.DMA((RING * RING,)),
        ],
        compiler_params=pltpu.CompilerParams(vmem_limit_bytes=60 << 20),
        cost_estimate=pl.CostEstimate(
            flops=2 * span * width * 384, bytes_accessed=7 << 20, transcendentals=0
        ),
    )(tokens, gain, w_q, w_kt, w_vt, near, far, sign, w_out)


def largest(rows, axis):
    return jnp.max(jnp.sum(rows * rows, axis, keepdims=True))


def segment_kernel(
    own, other, prefix, prefix_other, near, far, sign, rows, owners, seg_out, stay_out, go_out
):
    x, core, z, y, parity, number, group = position()
    odd = parity == 1
    mine, theirs = own[...].astype(F32), other[...].astype(F32)
    first = jnp.where(odd, theirs, mine)
    second = jnp.where(odd, mine, theirs)
    lane = lax.broadcasted_iota(jnp.int32, (1, HD), 1)
    key = jnp.where(lane < HALF, first, pltpu.roll(second, HALF, 1))
    value = jnp.where(lane < HALF, pltpu.roll(first, HALF, 1), second).astype(BF16)
    cosine, sine = rope_factors(near, far, number)
    key = (key * cosine + pltpu.roll(key, HALF, 1) * sine).astype(BF16)
    turn = sign[parity]
    unit = HD ** -0.5
    for i, part in enumerate((key, value)):
        turned = lax.dot_general(turn, part, TN, preferred_element_type=F32) * unit
        seg_out[i * HD:(i + 1) * HD, :] = turned.astype(BF16)
    longest = largest(seg_out[:HD, :].astype(F32), 0)
    halves = [ref[:HALF, :].astype(F32) for ref in (prefix, prefix_other)]
    longest = jnp.maximum(longest, largest(jnp.concatenate(halves, 0), 0)) * 1.01
    seg_out[2 * HD:, :] = jnp.full((NOTE, own.shape[0]), longest, F32).astype(BF16)
    plain = sign[0]
    pair = jnp.concatenate(
        [
            (jnp.dot(key, plain, preferred_element_type=F32) * unit).astype(BF16),
            (jnp.dot(value, plain, preferred_element_type=F32) * unit).astype(BF16),
        ],
        1,
    )
    span, keep = own.shape[0], rows.shape[1]
    row = rows[pl.ds(group, 1), :]
    owner = owners[pl.ds(group, 1), :]
    place = lax.broadcasted_iota(jnp.int32, (256, 1), 0)
    to_core = jnp.where(place >= 128, 1 - core, core)
    step_first, step_second = (place >> 3) & 3, (place >> 1) & 3
    to_x = (x + (place >> 5)) & 3
    to_z = (z + jnp.where(to_core == 0, step_first, step_second)) & 3
    to_y = (y + jnp.where(to_core == 0, step_second, step_first)) & 3
    named = owner == device_at(to_x, to_core, to_z, to_y)
    before = lax.broadcasted_iota(jnp.int32, (keep, keep), 0) < lax.broadcasted_iota(
        jnp.int32, (keep, keep), 1
    )
    rank = jnp.dot(
        jnp.where(named, 1.0, 0.0).astype(BF16),
        jnp.where(before, 1.0, 0.0).astype(BF16),
        preferred_element_type=F32,
    )
    slot = (2 * parity + (place & 1)).astype(F32)
    picks = jnp.where(jnp.logical_and(named, rank == slot), 1.0, 0.0).astype(BF16)
    places = jnp.where(
        lax.broadcasted_iota(jnp.int32, (span, keep), 0) == row, 1.0, 0.0
    ).astype(BF16)
    chosen = lax.dot_general(picks, places, NT, preferred_element_type=F32).astype(BF16)
    kept = jnp.dot(chosen, pair, preferred_element_type=F32).astype(BF16)
    stay_out[...] = kept[:128, :]
    go_out[...] = kept[128:, :]


def vmem():
    return pl.BlockSpec(memory_space=pltpu.VMEM)


def segment(own, *rest):
    span = own.shape[0]
    return pl.pallas_call(
        segment_kernel,
        in_specs=[vmem()] * 9,
        out_specs=[vmem()] * 3,
        out_shape=[jax.ShapeDtypeStruct((2 * HD + NOTE, span), BF16)]
        + [jax.ShapeDtypeStruct((128, 2 * HD), BF16)] * 2,
        compiler_params=pltpu.CompilerParams(vmem_limit_bytes=24 << 20),
        cost_estimate=pl.CostEstimate(
            flops=400_000_000, bytes_accessed=2 << 20, transcendentals=0
        ),
    )(own, *rest)


def attend_kernel(
    step, q, own, other, sib_own, sib_other, seg, sib_seg, stay, came, out, acc, total, top, held
):
    x, core = position()[:2]
    rows = q.shape[0]
    span = seg.shape[1]
    blocks = own.shape[1] // TILE
    prefix = ((own, other), (sib_own, sib_other))

    def prefix_tile(pair, columns):
        mine, theirs = pair
        keys = jnp.concatenate([mine[:HALF, columns], theirs[:HALF, columns]], 0)
        values = jnp.concatenate([mine[HALF:, columns], theirs[HALF:, columns]], 0)
        return keys, values

    longest = jnp.maximum(
        jnp.max(seg[2 * HD:, :HD].astype(F32)), jnp.max(sib_seg[2 * HD:, :HD].astype(F32))
    )
    widest = largest(q[...].astype(F32), 1)
    calm = longest * widest < SAFE_BOUND * SAFE_BOUND

    if step == 0:
        whole_flags = (None, core == 1)
    else:
        later = lax.rem(x + RING - step, RING) > x
        whole_flags = (later, later)

    def causal(begin, count):
        token = lax.rem(lax.broadcasted_iota(jnp.int32, (count, span), 0) + begin, span)
        return lax.broadcasted_iota(jnp.int32, (count, span), 1) <= token

    acc[...] = jnp.zeros_like(acc)
    total[...] = jnp.zeros_like(total)

    @pl.when(calm)
    def _():
        def tile(keys, values, masked=False):
            scores = jnp.dot(q[...], keys, preferred_element_type=F32)
            weights = jnp.exp2(scores)
            if masked:
                weights = jnp.where(causal(0, rows), weights, 0.0)
            part = weights[:, :HD]
            for i in range(1, TILE // HD):
                part = part + weights[:, i * HD:(i + 1) * HD]
            mixed = lax.dot_general(weights.astype(BF16), values, NT, preferred_element_type=F32)
            acc[...] += mixed
            total[...] += part

        for pair in prefix:
            def some_tiles(i, carry, pair=pair):
                for j in range(2):
                    begin = pl.multiple_of((2 * i + j) * TILE, TILE)
                    tile(*prefix_tile(pair, pl.ds(begin, TILE)))
                return carry

            lax.fori_loop(0, blocks // 2, some_tiles, 0)
        for ref, flag in zip((seg, sib_seg), whole_flags):
            if flag is None:
                tile(ref[:HD, :], ref[HD:2 * HD, :], masked=True)
            else:
                @pl.when(flag)
                def _(ref=ref):
                    tile(ref[:HD, :], ref[HD:2 * HD, :])
        top[...] = jnp.zeros_like(top)

    @pl.when(jnp.logical_not(calm))
    def _():
        top[...] = jnp.full_like(top, LOWEST)
        chunk = 256
        seg_flag = 1 if whole_flags[0] is None else whole_flags[0].astype(jnp.int32)
        sib_flag = whole_flags[1].astype(jnp.int32)

        def some_keys(b, carry):
            column = pl.ds(pl.multiple_of(lax.rem(b, blocks) * TILE, TILE), TILE)
            for number, pair in enumerate(prefix):
                @pl.when(b // blocks == number)
                def _(pair=pair):
                    for i in range(2):
                        for j, ref in enumerate(pair):
                            begin = i * HD + j * HALF
                            held[begin:begin + HALF, :] = ref[i * HALF:(i + 1) * HALF, column]

            for number, ref in enumerate((seg, sib_seg)):
                @pl.when(b == 2 * blocks + number)
                def _(ref=ref):
                    held[...] = ref[:2 * HD, :]

            last = b == 2 * blocks
            flag = jnp.where(last, seg_flag, jnp.where(b > 2 * blocks, sib_flag, 1))
            causal_from = 0 if step else jnp.where(last, 0, -span)

            def some_rows(r, carry):
                begin = pl.multiple_of(r * chunk, chunk)
                at = pl.ds(begin, chunk)
                scores = jnp.dot(q[at, :], held[:HD, :], preferred_element_type=F32)
                if step == 0:
                    token = lax.rem(
                        lax.broadcasted_iota(jnp.int32, (chunk, span), 0) + begin, span
                    )
                    column = lax.broadcasted_iota(jnp.int32, (chunk, span), 1) + causal_from
                    scores = jnp.where(column <= token, scores, -jnp.inf)
                old = top[at, :]
                new = jnp.maximum(old, jnp.max(scores, 1, keepdims=True))
                weights = jnp.exp2(scores - new[:, :1])
                factor = jnp.exp2(old - new)
                part = weights[:, :HD]
                for i in range(1, TILE // HD):
                    part = part + weights[:, i * HD:(i + 1) * HD]
                mixed = lax.dot_general(
                    weights.astype(BF16), held[HD:, :], NT, preferred_element_type=F32
                )
                acc[at, :] = acc[at, :] * factor + mixed
                total[at, :] = total[at, :] * factor + part
                top[at, :] = new
                return carry

            @pl.when(flag == 1)
            def _():
                lax.fori_loop(0, rows // chunk, some_rows, 0)

            return carry

        lax.fori_loop(0, 2 * blocks + 2, some_keys, 0)

    summed = jnp.sum(total[...], 1, keepdims=True)
    out[:rows, :] = (acc[...] / summed).astype(BF16)
    level = top[...] + jnp.log2(summed)
    eye = lax.broadcasted_iota(jnp.int32, (1, HD, HD), 1) == lax.broadcasted_iota(
        jnp.int32, (1, HD, HD), 2
    )
    packed = jnp.sum(jnp.where(eye, level.reshape(rows // HD, HD, HD), 0.0), 1)
    high = packed.astype(BF16).astype(F32)
    rest = packed - high
    middle = rest.astype(BF16).astype(F32)
    low = rest - middle
    out[rows:rows + 32, :] = jnp.concatenate(
        [high, middle, low, jnp.zeros_like(high)], 0
    ).astype(BF16)
    back = (RING - step) % RING
    for i, ref in enumerate((stay, came, stay, came)):
        out[rows + 32 * (i + 1):rows + 32 * (i + 2), :] = ref[
            32 * back:32 * (back + 1), i // 2 * HD:(i // 2 + 1) * HD
        ]


def attend(step, q, *rest):
    rows = q.shape[0]
    return pl.pallas_call(
        functools.partial(attend_kernel, step),
        in_specs=[vmem()] * 9,
        out_specs=vmem(),
        out_shape=jax.ShapeDtypeStruct((rows + EXTRA, HD), BF16),
        scratch_shapes=[pltpu.VMEM((rows, HD), F32)] * 3 + [pltpu.VMEM((2 * HD, TILE), BF16)],
        compiler_params=pltpu.CompilerParams(vmem_limit_bytes=32 << 20),
        cost_estimate=pl.CostEstimate(
            flops=8 * rows * HD * 4096, bytes_accessed=4 << 20, transcendentals=rows * 4096
        ),
    )(q, *rest)


def shuffle(rows, source):
    here = lax.broadcasted_iota(jnp.int32, (256, 256), 0)
    there = lax.broadcasted_iota(jnp.int32, (256, 256), 1)
    moves = jnp.where(source(here) == there, 1.0, 0.0).astype(BF16)
    return jnp.dot(moves, rows, preferred_element_type=F32).astype(BF16)


def merge_kernel(p0, p1, p2, p3, sign, *outs):
    parity = position()[4]
    parts = (p0, p1, p2, p3)
    rows = p0.shape[0] - EXTRA
    count = rows // HD
    levels = []
    for part in parts:
        stats = part[rows:rows + 32, :].astype(F32)
        levels.append(stats[:count] + stats[count:2 * count] + stats[2 * count:3 * count])
    most = functools.reduce(jnp.maximum, levels)
    shares = [jnp.exp2(level - most) for level in levels]
    whole = functools.reduce(jnp.add, shares)
    shares = [share / whole for share in shares]
    eye = lax.broadcasted_iota(jnp.int32, (HD, HD), 0) == lax.broadcasted_iota(
        jnp.int32, (HD, HD), 1
    )
    turn = sign[parity]
    per_head = count // 2
    for b in range(count):
        left, right = [], []
        for share, part in zip(shares, parts):
            block = part[b * HD:(b + 1) * HD, :]
            left.append(jnp.where(eye, share[b:b + 1, :], 0.0).astype(BF16))
            right.append(block)
        mixed = jnp.dot(
            jnp.concatenate(left, 1), jnp.concatenate(right, 0), preferred_element_type=F32
        )
        plain = lax.dot_general(mixed.astype(BF16), turn, NT, preferred_element_type=F32)
        head, place = b // per_head, b % per_head
        block = (plain * HD ** -0.5).astype(BF16)
        for out in outs:
            out[place * HD:(place + 1) * HD, head * HD:(head + 1) * HD] = block
    kept = jnp.concatenate(
        [
            jnp.concatenate([part[rows + 32:rows + 96, :], part[rows + 96:, :]], 1)
            for part in parts
        ],
        0,
    )
    kept = shuffle(
        kept,
        lambda r: ((r >> 4) & 3) << 6 | ((r >> 3) & 1) << 5 | (r >> 6) << 3 | (r & 7),
    )
    for k, out in enumerate(outs):
        out[rows // 2:, :] = kept[64 * k:64 * (k + 1), :]


def merge(parts, sign):
    rows = parts[0].shape[0] - EXTRA
    return pl.pallas_call(
        merge_kernel,
        in_specs=[vmem()] * 5,
        out_specs=[vmem()] * RING,
        out_shape=[jax.ShapeDtypeStruct((rows // 2 + 64, 2 * HD), BF16)] * RING,
        compiler_params=pltpu.CompilerParams(vmem_limit_bytes=24 << 20),
        cost_estimate=pl.CostEstimate(
            flops=400_000_000, bytes_accessed=2 << 20, transcendentals=0
        ),
    )(*parts, sign)


def out_kernel(c0, c1, c2, c3, w0, w1, w2, w3, o0, o1, o2, o3, sum_out):
    outs = (o0, o1, o2, o3)
    contexts = (c0, c1, c2, c3)
    span = sum_out.shape[0]
    for k in (2, 1, 3, 0):
        columns = slice(k * 256, (k + 1) * 256)
        whole = None
        for c, w in zip(contexts, (w0, w1, w2, w3)):
            part = jnp.dot(c[:span, :], w[:, columns], preferred_element_type=F32)
            whole = part if whole is None else whole + part
        if k:
            outs[k][:span, :] = whole.astype(BF16)
        else:
            sum_out[...] = whole
    kept = jnp.concatenate([c[span:, :] for c in contexts], 0)
    kept = shuffle(
        kept,
        lambda r: ((r >> 4) & 3) << 6
        | ((r >> 2) & 3) << 4
        | ((r >> 1) & 1) << 3
        | (r >> 6) << 1
        | (r & 1),
    )
    for k, out in enumerate(outs):
        begin = span if k else 0
        out[begin:, :] = kept[64 * k:64 * (k + 1), :]


def project_out(contexts, weights):
    total = contexts[0].shape[0]
    span = total - 64
    return pl.pallas_call(
        out_kernel,
        in_specs=[vmem()] * 8,
        out_specs=[vmem()] * 5,
        out_shape=[jax.ShapeDtypeStruct((total if k else 64, 256), BF16) for k in range(4)]
        + [jax.ShapeDtypeStruct((span, 256), F32)],
        compiler_params=pltpu.CompilerParams(vmem_limit_bytes=24 << 20),
        cost_estimate=pl.CostEstimate(
            flops=2 * span * 1024 * 1024, bytes_accessed=5 << 20, transcendentals=0
        ),
    )(*contexts, *weights)


def finish_kernel(share, kept, a1, a2, a3, attn_out, kept_out):
    x, core, z, y = position()[:4]
    arrived = (a1, a2, a3)
    span = share.shape[0]
    whole = share[...]
    for part in arrived:
        whole = whole + part[:span, :].astype(F32)
    attn_out[...] = whole.astype(BF16)
    rows = jnp.concatenate([kept[...]] + [part[span:, :] for part in arrived], 0)
    place = lax.broadcasted_iota(jnp.int32, (1, 256), 1)
    back_second, back_first = place >> 6, (place >> 4) & 3
    from_x = (x + (place >> 2)) & 3
    from_core = (core + (place >> 1)) & 1
    from_z = (z - jnp.where(core == 0, back_first, back_second)) & 3
    from_y = (y - jnp.where(core == 0, back_second, back_first)) & 3
    target = device_at(from_x, from_core, from_z, from_y) * 2 + (place & 1)
    here = lax.broadcasted_iota(jnp.int32, (256, 256), 0)
    moves = jnp.where(here == target, 1.0, 0.0).astype(BF16)
    kept_out[...] = jnp.dot(moves, rows, preferred_element_type=F32).astype(BF16)


def finish(share, kept, arrived):
    return pl.pallas_call(
        finish_kernel,
        in_specs=[vmem()] * 5,
        out_specs=[vmem()] * 2,
        out_shape=[
            jax.ShapeDtypeStruct(share.shape, BF16),
            jax.ShapeDtypeStruct((256, 2 * HD), BF16),
        ],
        compiler_params=pltpu.CompilerParams(vmem_limit_bytes=24 << 20),
    )(share, kept, *arrived)


def shards(
    tokens, norm_gain, w_query, w_key, w_value, w_out, prefix_keys, prefix_values, keep_rows, owners
):
    seq_count = lax.axis_size("seq")
    span = tokens.shape[0]
    prefix_len = prefix_keys.shape[0] * seq_count
    near, far = rope_tables(span, seq_count, prefix_len)
    near, far = jnp.asarray(near), jnp.asarray(far)
    sign = jnp.asarray(signs(), BF16)

    own = jnp.concatenate([prefix_keys.T, prefix_values.T], 0)
    other = to_head_pair(own)
    sib_own = to_sibling(own)
    q, kv, *pieces = project(
        tokens, norm_gain.reshape(-1, HD), w_query, w_key.T, w_value.T, near, far, sign, w_out
    )
    kv_other = to_head_pair(kv)
    queries = [q] + [along_x(q, d) for d in (1, 2, 3)]
    weights = [pieces[0]] + [along_first(pieces[d], d) for d in (1, 2, 3)]
    kv_other, other, queries[1], queries[3] = lax.optimization_barrier(
        (kv_other, other, queries[1], queries[3])
    )
    sib_other = to_sibling(other)
    seg, stay, go = segment(
        kv, kv_other, own, other, near, far, sign, keep_rows[0], owners.reshape(owners.shape[1:3])
    )
    came = to_sibling(go)
    sib_seg = to_sibling(seg)
    queries[3], weights[2] = lax.optimization_barrier((queries[3], weights[2]))
    parts = [None] * RING
    for d in (3, 1, 2, 0):
        part = attend(
            d, queries[d], own, other, sib_own, sib_other, seg, sib_seg, stay, came
        )
        parts[d] = along_x(part, -d) if d else part
    contexts = merge(parts, sign)
    contexts = [contexts[0]] + [along_first(contexts[d], d) for d in (1, 2, 3)]
    *shares, share = project_out(contexts, weights)
    arrived = [along_second(shares[k], k) for k in (1, 2, 3)]
    return tuple(finish(share, shares[0], arrived))


def solution(mesh):
    return jax.shard_map(
        shards,
        mesh=mesh,
        in_specs=(
            P("seq", None),
            P(),
            P(None, "tp"),
            P(None, "tp"),
            P(None, "tp"),
            P("tp", None),
            P("seq", "tp"),
            P("seq", "tp"),
            P("seq", None, None),
            P("seq", None, None, None),
        ),
        out_specs=(P("seq", "tp"), P(("seq", "tp"), None)),
        check_vma=False,
    )
```

```python
import functools
import math

import jax
import jax.numpy as jnp
import numpy as np
from jax import lax
from jax.experimental import pallas as pl
from jax.experimental.pallas import tpu as pltpu
from jax.sharding import PartitionSpec as P

EPSILON = 1e-05
ROPE_BASE = 500000.0
LOWEST = -1e30
LOG2E = math.log2(math.e)
SAFE_BOUND = 60.0
HD = 128
HALF = 64
AXES = ("seq", "tp")
RING = 4
TILE = 512
CHUNKS = 4
CUT_AT = 2
WHOLE_AT = 1
NOTE = 16
EXTRA = 32 + 128

NT = (((1,), (1,)), ((), ()))
TN = (((0,), (1,)), ((), ()))
F32 = jnp.float32
BF16 = jnp.bfloat16


def device_at(x, core, z, y):
    return ((x & 3) * 2 + core) * 16 + (z & 3) * 4 + (y & 3)


def pairs_of(move):
    return [
        (device_at(x, c, z, y), device_at(*move(x, c, z, y)))
        for x in range(RING)
        for c in range(2)
        for z in range(RING)
        for y in range(RING)
    ]


def send(value, move):
    return lax.ppermute(value, AXES, pairs_of(move))


def to_sibling(value):
    return send(value, lambda x, c, z, y: (x, 1 - c, z, y))


def to_head_pair(value):
    return send(value, lambda x, c, z, y: (x, c, z, y ^ 1))


def along_x(value, step):
    return send(value, lambda x, c, z, y: (x + step, c, z, y))


def along_first(value, step):
    return send(
        value, lambda x, c, z, y: (x, c, z + step, y) if c == 0 else (x, c, z, y + step)
    )


def along_second(value, step):
    return send(
        value, lambda x, c, z, y: (x, c, z, y + step) if c == 0 else (x, c, z + step, y)
    )


def position():
    seq, tp = lax.axis_index("seq"), lax.axis_index("tp")
    return seq >> 1, seq & 1, tp >> 2, tp & 3, tp & 1, seq, tp >> 1


def signs():
    index = np.arange(HD)
    both = index[:, None] & index[None, :]
    parity = np.zeros((HD, HD), np.int64)
    for bit in range(7):
        parity += both >> bit & 1
    plain = (1 - 2 * (parity % 2)).astype(np.float32)
    return np.stack([plain, np.roll(plain, HALF, axis=1)])


def rope_tables(span, spans, prefix):
    freq = np.exp(-np.arange(HALF) * (2.0 * math.log(ROPE_BASE) / HD))
    freq = np.concatenate([freq, freq])
    near = np.arange(span)[:, None] * freq[None, :]
    far = (prefix + span * np.arange(spans))[:, None] * freq[None, :]
    near = np.stack([np.cos(near), np.sin(near)]).astype(np.float32)
    far = np.stack([np.cos(far), np.sin(far)]).astype(np.float32)
    return near, far


def rope_factors(near, far, number):
    cos_far, sin_far = far[0, pl.ds(number, 1), :], far[1, pl.ds(number, 1), :]
    cosine = near[0] * cos_far - near[1] * sin_far
    sine = near[1] * cos_far + near[0] * sin_far
    lane = lax.broadcasted_iota(jnp.int32, (1, HD), 1)
    return cosine, jnp.where(lane < HALF, -sine, sine)


def project_kernel(
    tokens, gain, w_q, w_kt, w_vt, near, far, sign, w_out, q_out, kv_out, w0, w1, w2, w3,
    held, held_q, held_kv, held_near, held_w, sum_q, sum_kv, sems, cut_sems,
):
    x, core, z, y, parity, number, group = position()
    span, width = tokens.shape
    block = width // CHUNKS
    parts = [pl.ds(i * block, block) for i in range(CHUNKS)]
    arrive = []
    for i, at in enumerate(parts):
        moves = (
            (tokens.at[:, at], held.at[:, at]),
            (w_q.at[at], held_q.at[at]),
            (w_kt.at[:, at], held_kv.at[:HALF, at]),
            (w_vt.at[:, at], held_kv.at[HALF:, at]),
        )
        arrive.append([
            pltpu.make_async_copy(start, end, sems.at[4 * i + j])
            for j, (start, end) in enumerate(moves)
        ])
    tables = pltpu.make_async_copy(near, held_near, sems.at[4 * CHUNKS])
    whole = pltpu.make_async_copy(w_out, held_w, sems.at[4 * CHUNKS + 1])
    for i, copies in enumerate(arrive):
        for copy in copies:
            copy.start()
        if i == WHOLE_AT:
            whole.start()
    tables.start()
    cuts = []
    for d, piece in enumerate((w0, w1, w2, w3)):
        for k in range(RING):
            row = (z + jnp.where(core == 0, d, k)) & 3
            col = (y + jnp.where(core == 0, k, d)) & 3
            begin = pl.multiple_of((row * RING + col) * 256, 256)
            cuts.append(
                pltpu.make_async_copy(
                    held_w.at[:, pl.ds(begin, 256)],
                    piece.at[:, pl.ds(k * 256, 256)],
                    cut_sems.at[d * RING + k],
                )
            )
    squares = None
    per = block // HD
    for i, at in enumerate(parts):
        for copy in arrive[i]:
            copy.wait()
        if i == CUT_AT:
            whole.wait()
            for copy in cuts:
                copy.start()
        gains = jnp.concatenate([gain[j:j + 1, :] for j in range(i * per, (i + 1) * per)], 1)
        begin, end = i * block, (i + 1) * block
        hidden = held[:, begin:end].astype(F32)
        weighted = (hidden * gains.astype(F32)).astype(BF16)
        hidden = hidden * hidden
        for j in range(per):
            square = hidden[:, j * HD:(j + 1) * HD]
            squares = square if squares is None else squares + square
        part_q = jnp.dot(weighted, held_q[begin:end, :], preferred_element_type=F32)
        part_kv = lax.dot_general(
            weighted, held_kv[:, begin:end], NT, preferred_element_type=F32
        )
        if i == 0:
            sum_q[...] = part_q
            sum_kv[...] = part_kv
        else:
            sum_q[...] += part_q
            sum_kv[...] += part_kv
    scale = lax.rsqrt(jnp.sum(squares, -1, keepdims=True) / width + EPSILON)
    kv_out[...] = (sum_kv[...] * scale).astype(BF16)
    tables.wait()
    cosine, sine = rope_factors(held_near, far, number)
    turn = sign[parity]
    for h in range(2):
        head = sum_q[:, h * HD:(h + 1) * HD] * scale
        head = head * cosine + pltpu.roll(head, HALF, 1) * sine
        head = (head * HD ** -0.5).astype(BF16)
        head = jnp.dot(head, turn, preferred_element_type=F32)
        q_out[h * span:(h + 1) * span, :] = (head * (HD ** -0.5 * LOG2E)).astype(BF16)
    for copy in cuts:
        copy.wait()


def project(tokens, gain, w_q, w_kt, w_vt, near, far, sign, w_out):
    span, width = tokens.shape
    remain = pl.BlockSpec(memory_space=pl.ANY)
    return pl.pallas_call(
        project_kernel,
        in_specs=[remain, vmem()] + [remain] * 4 + [vmem(), vmem(), remain],
        out_specs=[vmem(), vmem()] + [remain] * 4,
        out_shape=[
            jax.ShapeDtypeStruct((2 * span, HD), BF16),
            jax.ShapeDtypeStruct((span, HD), BF16),
        ] + [jax.ShapeDtypeStruct((w_out.shape[0], 1024), BF16)] * 4,
        scratch_shapes=[
            pltpu.VMEM((span, width), BF16),
            pltpu.VMEM((width, 2 * HD), BF16),
            pltpu.VMEM((HD, width), BF16),
            pltpu.VMEM(near.shape, F32),
            pltpu.VMEM(w_out.shape, BF16),
            pltpu.VMEM((span, 2 * HD), F32),
            pltpu.VMEM((span, HD), F32),
            pltpu.SemaphoreType.DMA((4 * CHUNKS + 2,)),
            pltpu.SemaphoreType.DMA((RING * RING,)),
        ],
        compiler_params=pltpu.CompilerParams(vmem_limit_bytes=60 << 20),
        cost_estimate=pl.CostEstimate(
            flops=2 * span * width * 384, bytes_accessed=7 << 20, transcendentals=0
        ),
    )(tokens, gain, w_q, w_kt, w_vt, near, far, sign, w_out)


def largest(rows, axis):
    return jnp.max(jnp.sum(rows * rows, axis, keepdims=True))


def segment_kernel(
    own, other, prefix, prefix_other, near, far, sign, rows, owners, seg_out, stay_out,
    held, sem,
):
    x, core, z, y, parity, number, group = position()
    odd = parity == 1
    arrive = pltpu.make_async_copy(own, held, sem)
    arrive.start()
    span, keep = own.shape[0], rows.shape[1]
    row = rows[pl.ds(group, 1), :]
    owner = owners[pl.ds(group, 1), :]
    place = lax.broadcasted_iota(jnp.int32, (256, 1), 0)
    to_core = jnp.where(place >= 128, 1 - core, core)
    step_first, step_second = (place >> 3) & 3, (place >> 1) & 3
    to_x = (x + (place >> 5)) & 3
    to_z = (z + jnp.where(to_core == 0, step_first, step_second)) & 3
    to_y = (y + jnp.where(to_core == 0, step_second, step_first)) & 3
    named = owner == device_at(to_x, to_core, to_z, to_y)
    before = lax.broadcasted_iota(jnp.int32, (keep, keep), 0) < lax.broadcasted_iota(
        jnp.int32, (keep, keep), 1
    )
    rank = jnp.dot(
        jnp.where(named, 1.0, 0.0).astype(BF16),
        jnp.where(before, 1.0, 0.0).astype(BF16),
        preferred_element_type=F32,
    )
    slot = (2 * parity + (place & 1)).astype(F32)
    picks = jnp.where(jnp.logical_and(named, rank == slot), 1.0, 0.0).astype(BF16)
    places = jnp.where(
        lax.broadcasted_iota(jnp.int32, (span, keep), 0) == row, 1.0, 0.0
    ).astype(BF16)
    chosen = lax.dot_general(picks, places, NT, preferred_element_type=F32).astype(BF16)
    arrive.wait()
    mine, theirs = held[...].astype(F32), other[...].astype(F32)
    first = jnp.where(odd, theirs, mine)
    second = jnp.where(odd, mine, theirs)
    lane = lax.broadcasted_iota(jnp.int32, (1, HD), 1)
    key = jnp.where(lane < HALF, first, pltpu.roll(second, HALF, 1))
    value = jnp.where(lane < HALF, pltpu.roll(first, HALF, 1), second).astype(BF16)
    cosine, sine = rope_factors(near, far, number)
    key = (key * cosine + pltpu.roll(key, HALF, 1) * sine).astype(BF16)
    turn = sign[parity]
    unit = HD ** -0.5
    for i, part in enumerate((key, value)):
        turned = lax.dot_general(turn, part, TN, preferred_element_type=F32) * unit
        seg_out[i * HD:(i + 1) * HD, :] = turned.astype(BF16)
    longest = largest(seg_out[:HD, :].astype(F32), 0)
    halves = [ref[:HALF, :].astype(F32) for ref in (prefix, prefix_other)]
    longest = jnp.maximum(longest, largest(jnp.concatenate(halves, 0), 0)) * 1.01
    seg_out[2 * HD:2 * HD + NOTE, :] = jnp.full((NOTE, own.shape[0]), longest, F32).astype(BF16)
    plain = sign[0]
    pair = jnp.concatenate(
        [
            (jnp.dot(key, plain, preferred_element_type=F32) * unit).astype(BF16),
            (jnp.dot(value, plain, preferred_element_type=F32) * unit).astype(BF16),
        ],
        1,
    )
    kept = jnp.dot(chosen, pair, preferred_element_type=F32).astype(BF16)
    stay_out[...] = kept[:128, :]
    for i in range(2):
        seg_out[2 * HD + NOTE:, i * 256:(i + 1) * 256] = kept[128 + 64 * i:192 + 64 * i, :]


def vmem():
    return pl.BlockSpec(memory_space=pltpu.VMEM)


def segment(own, *rest):
    span = own.shape[0]
    return pl.pallas_call(
        segment_kernel,
        in_specs=[pl.BlockSpec(memory_space=pl.ANY)] + [vmem()] * 8,
        out_specs=[vmem()] * 2,
        out_shape=[
            jax.ShapeDtypeStruct((2 * HD + NOTE + 64, span), BF16),
            jax.ShapeDtypeStruct((128, 2 * HD), BF16),
        ],
        scratch_shapes=[pltpu.VMEM((span, HD), BF16), pltpu.SemaphoreType.DMA],
        compiler_params=pltpu.CompilerParams(vmem_limit_bytes=24 << 20),
        cost_estimate=pl.CostEstimate(
            flops=400_000_000, bytes_accessed=2 << 20, transcendentals=0
        ),
    )(own, *rest)


def attend_kernel(
    step, q, own, other, sib_own, sib_other, seg, sib_seg, stay, out, acc, total, top, held
):
    x, core = position()[:2]
    rows = q.shape[0]
    span = seg.shape[1]
    blocks = own.shape[1] // TILE
    prefix = ((own, other), (sib_own, sib_other))

    def prefix_tile(pair, columns):
        mine, theirs = pair
        keys = jnp.concatenate([mine[:HALF, columns], theirs[:HALF, columns]], 0)
        values = jnp.concatenate([mine[HALF:, columns], theirs[HALF:, columns]], 0)
        return keys, values

    longest = jnp.maximum(
        jnp.max(seg[2 * HD:2 * HD + NOTE, :HD].astype(F32)),
        jnp.max(sib_seg[2 * HD:2 * HD + NOTE, :HD].astype(F32)),
    )
    widest = largest(q[...].astype(F32), 1)
    calm = longest * widest < SAFE_BOUND * SAFE_BOUND

    if step == 0:
        whole_flags = (None, core == 1)
    else:
        later = lax.rem(x + RING - step, RING) > x
        whole_flags = (later, later)

    def causal(begin, count):
        token = lax.rem(lax.broadcasted_iota(jnp.int32, (count, span), 0) + begin, span)
        return lax.broadcasted_iota(jnp.int32, (count, span), 1) <= token

    acc[...] = jnp.zeros_like(acc)
    total[...] = jnp.zeros_like(total)

    @pl.when(calm)
    def _():
        def tile(keys, values, masked=False):
            scores = jnp.dot(q[...], keys, preferred_element_type=F32)
            weights = jnp.exp2(scores)
            if masked:
                weights = jnp.where(causal(0, rows), weights, 0.0)
            part = weights[:, :HD]
            for i in range(1, TILE // HD):
                part = part + weights[:, i * HD:(i + 1) * HD]
            mixed = lax.dot_general(weights.astype(BF16), values, NT, preferred_element_type=F32)
            acc[...] += mixed
            total[...] += part

        for pair in prefix:
            def some_tiles(i, carry, pair=pair):
                for j in range(2):
                    begin = pl.multiple_of((2 * i + j) * TILE, TILE)
                    tile(*prefix_tile(pair, pl.ds(begin, TILE)))
                return carry

            lax.fori_loop(0, blocks // 2, some_tiles, 0)
        for ref, flag in zip((seg, sib_seg), whole_flags):
            if flag is None:
                tile(ref[:HD, :], ref[HD:2 * HD, :], masked=True)
            else:
                @pl.when(flag)
                def _(ref=ref):
                    tile(ref[:HD, :], ref[HD:2 * HD, :])
        top[...] = jnp.zeros_like(top)

    @pl.when(jnp.logical_not(calm))
    def _():
        top[...] = jnp.full_like(top, LOWEST)
        chunk = 256
        seg_flag = 1 if whole_flags[0] is None else whole_flags[0].astype(jnp.int32)
        sib_flag = whole_flags[1].astype(jnp.int32)

        def some_keys(b, carry):
            column = pl.ds(pl.multiple_of(lax.rem(b, blocks) * TILE, TILE), TILE)
            for number, pair in enumerate(prefix):
                @pl.when(b // blocks == number)
                def _(pair=pair):
                    for i in range(2):
                        for j, ref in enumerate(pair):
                            begin = i * HD + j * HALF
                            held[begin:begin + HALF, :] = ref[i * HALF:(i + 1) * HALF, column]

            for number, ref in enumerate((seg, sib_seg)):
                @pl.when(b == 2 * blocks + number)
                def _(ref=ref):
                    held[...] = ref[:2 * HD, :]

            last = b == 2 * blocks
            flag = jnp.where(last, seg_flag, jnp.where(b > 2 * blocks, sib_flag, 1))
            causal_from = 0 if step else jnp.where(last, 0, -span)

            def some_rows(r, carry):
                begin = pl.multiple_of(r * chunk, chunk)
                at = pl.ds(begin, chunk)
                scores = jnp.dot(q[at, :], held[:HD, :], preferred_element_type=F32)
                if step == 0:
                    token = lax.rem(
                        lax.broadcasted_iota(jnp.int32, (chunk, span), 0) + begin, span
                    )
                    column = lax.broadcasted_iota(jnp.int32, (chunk, span), 1) + causal_from
                    scores = jnp.where(column <= token, scores, -jnp.inf)
                old = top[at, :]
                new = jnp.maximum(old, jnp.max(scores, 1, keepdims=True))
                weights = jnp.exp2(scores - new[:, :1])
                factor = jnp.exp2(old - new)
                part = weights[:, :HD]
                for i in range(1, TILE // HD):
                    part = part + weights[:, i * HD:(i + 1) * HD]
                mixed = lax.dot_general(
                    weights.astype(BF16), held[HD:, :], NT, preferred_element_type=F32
                )
                acc[at, :] = acc[at, :] * factor + mixed
                total[at, :] = total[at, :] * factor + part
                top[at, :] = new
                return carry

            @pl.when(flag == 1)
            def _():
                lax.fori_loop(0, rows // chunk, some_rows, 0)

            return carry

        lax.fori_loop(0, 2 * blocks + 2, some_keys, 0)

    summed = jnp.sum(total[...], 1, keepdims=True)
    out[:rows, :] = (acc[...] / summed).astype(BF16)
    level = top[...] + jnp.log2(summed)
    eye = lax.broadcasted_iota(jnp.int32, (1, HD, HD), 1) == lax.broadcasted_iota(
        jnp.int32, (1, HD, HD), 2
    )
    packed = jnp.sum(jnp.where(eye, level.reshape(rows // HD, HD, HD), 0.0), 1)
    high = packed.astype(BF16).astype(F32)
    rest = packed - high
    middle = rest.astype(BF16).astype(F32)
    low = rest - middle
    out[rows:rows + 32, :] = jnp.concatenate(
        [high, middle, low, jnp.zeros_like(high)], 0
    ).astype(BF16)
    back = (RING - step) % RING
    begin, lanes = 2 * HD + NOTE + 32 * (back % 2), 2 * HD * (back // 2)
    for i in range(2):
        place, half = rows + 32 + 64 * i, slice(i * HD, (i + 1) * HD)
        out[place:place + 32, :] = stay[32 * back:32 * (back + 1), half]
        half = slice(lanes + i * HD, lanes + (i + 1) * HD)
        out[place + 32:place + 64, :] = sib_seg[begin:begin + 32, half]


def attend(step, q, *rest):
    rows = q.shape[0]
    return pl.pallas_call(
        functools.partial(attend_kernel, step),
        in_specs=[vmem()] * 8,
        out_specs=vmem(),
        out_shape=jax.ShapeDtypeStruct((rows + EXTRA, HD), BF16),
        scratch_shapes=[pltpu.VMEM((rows, HD), F32)] * 3 + [pltpu.VMEM((2 * HD, TILE), BF16)],
        compiler_params=pltpu.CompilerParams(vmem_limit_bytes=32 << 20),
        cost_estimate=pl.CostEstimate(
            flops=8 * rows * HD * 4096, bytes_accessed=4 << 20, transcendentals=rows * 4096
        ),
    )(q, *rest)


def shuffle(rows, source):
    here = lax.broadcasted_iota(jnp.int32, (256, 256), 0)
    there = lax.broadcasted_iota(jnp.int32, (256, 256), 1)
    moves = jnp.where(source(here) == there, 1.0, 0.0).astype(BF16)
    return jnp.dot(moves, rows, preferred_element_type=F32).astype(BF16)


def merge_kernel(p0, p1, p2, p3, sign, *outs):
    parity = position()[4]
    parts = (p0, p1, p2, p3)
    rows = p0.shape[0] - EXTRA
    count = rows // HD
    levels = []
    for part in parts:
        stats = part[rows:rows + 32, :].astype(F32)
        levels.append(stats[:count] + stats[count:2 * count] + stats[2 * count:3 * count])
    most = functools.reduce(jnp.maximum, levels)
    shares = [jnp.exp2(level - most) for level in levels]
    whole = functools.reduce(jnp.add, shares)
    shares = [share / whole for share in shares]
    eye = lax.broadcasted_iota(jnp.int32, (HD, HD), 0) == lax.broadcasted_iota(
        jnp.int32, (HD, HD), 1
    )
    turn = sign[parity]
    per_head = count // 2
    for b in range(count):
        left, right = [], []
        for share, part in zip(shares, parts):
            block = part[b * HD:(b + 1) * HD, :]
            left.append(jnp.where(eye, share[b:b + 1, :], 0.0).astype(BF16))
            right.append(block)
        mixed = jnp.dot(
            jnp.concatenate(left, 1), jnp.concatenate(right, 0), preferred_element_type=F32
        )
        plain = lax.dot_general(mixed.astype(BF16), turn, NT, preferred_element_type=F32)
        head, place = b // per_head, b % per_head
        block = (plain * HD ** -0.5).astype(BF16)
        for out in outs:
            out[place * HD:(place + 1) * HD, head * HD:(head + 1) * HD] = block
    kept = jnp.concatenate(
        [
            jnp.concatenate([part[rows + 32:rows + 96, :], part[rows + 96:, :]], 1)
            for part in parts
        ],
        0,
    )
    kept = shuffle(
        kept,
        lambda r: ((r >> 4) & 3) << 6 | ((r >> 3) & 1) << 5 | (r >> 6) << 3 | (r & 7),
    )
    for k, out in enumerate(outs):
        out[rows // 2:, :] = kept[64 * k:64 * (k + 1), :]


def merge(parts, sign):
    rows = parts[0].shape[0] - EXTRA
    return pl.pallas_call(
        merge_kernel,
        in_specs=[vmem()] * 5,
        out_specs=[vmem()] * RING,
        out_shape=[jax.ShapeDtypeStruct((rows // 2 + 64, 2 * HD), BF16)] * RING,
        compiler_params=pltpu.CompilerParams(vmem_limit_bytes=24 << 20),
        cost_estimate=pl.CostEstimate(
            flops=400_000_000, bytes_accessed=2 << 20, transcendentals=0
        ),
    )(*parts, sign)


def out_kernel(places, c0, c1, c2, c3, w0, w1, w2, w3, *outs):
    contexts = (c0, c1, c2, c3)
    span = c0.shape[0] - 64
    kept = jnp.concatenate([c[span:, :] for c in contexts], 0)
    kept = shuffle(
        kept,
        lambda r: ((r >> 4) & 3) << 6
        | ((r >> 2) & 3) << 4
        | ((r >> 1) & 1) << 3
        | (r >> 6) << 1
        | (r & 1),
    )
    for k, out in zip(places, outs):
        columns = slice(k * 256, (k + 1) * 256)
        whole = None
        for c, w in zip(contexts, (w0, w1, w2, w3)):
            part = jnp.dot(c[:span, :], w[:, columns], preferred_element_type=F32)
            whole = part if whole is None else whole + part
        begin = span if k else 0
        if k:
            out[:span, :] = whole.astype(BF16)
        else:
            outs[-1][...] = whole
        out[begin:, :] = kept[64 * k:64 * (k + 1), :]


def project_out(places, contexts, weights):
    total = contexts[0].shape[0]
    span = total - 64
    shapes = [jax.ShapeDtypeStruct((total if k else 64, 256), BF16) for k in places]
    if 0 in places:
        shapes.append(jax.ShapeDtypeStruct((span, 256), F32))
    return pl.pallas_call(
        functools.partial(out_kernel, places),
        in_specs=[vmem()] * 8,
        out_specs=[vmem()] * len(shapes),
        out_shape=shapes,
        compiler_params=pltpu.CompilerParams(vmem_limit_bytes=24 << 20),
        cost_estimate=pl.CostEstimate(
            flops=512 * span * 1024 * len(places), bytes_accessed=5 << 20, transcendentals=0
        ),
    )(*contexts, *weights)


def finish_kernel(share, kept, a1, a2, a3, attn_out, kept_out):
    x, core, z, y = position()[:4]
    arrived = (a1, a2, a3)
    span = share.shape[0]
    whole = share[...]
    for part in arrived:
        whole = whole + part[:span, :].astype(F32)
    attn_out[...] = whole.astype(BF16)
    rows = jnp.concatenate([kept[...]] + [part[span:, :] for part in arrived], 0)
    place = lax.broadcasted_iota(jnp.int32, (1, 256), 1)
    back_second, back_first = place >> 6, (place >> 4) & 3
    from_x = (x + (place >> 2)) & 3
    from_core = (core + (place >> 1)) & 1
    from_z = (z - jnp.where(core == 0, back_first, back_second)) & 3
    from_y = (y - jnp.where(core == 0, back_second, back_first)) & 3
    target = device_at(from_x, from_core, from_z, from_y) * 2 + (place & 1)
    here = lax.broadcasted_iota(jnp.int32, (256, 256), 0)
    moves = jnp.where(here == target, 1.0, 0.0).astype(BF16)
    kept_out[...] = jnp.dot(moves, rows, preferred_element_type=F32).astype(BF16)


def finish(share, kept, arrived):
    return pl.pallas_call(
        finish_kernel,
        in_specs=[vmem()] * 5,
        out_specs=[vmem()] * 2,
        out_shape=[
            jax.ShapeDtypeStruct(share.shape, BF16),
            jax.ShapeDtypeStruct((256, 2 * HD), BF16),
        ],
        compiler_params=pltpu.CompilerParams(vmem_limit_bytes=24 << 20),
    )(share, kept, *arrived)


def shards(
    tokens, norm_gain, w_query, w_key, w_value, w_out, prefix_keys, prefix_values, keep_rows, owners
):
    seq_count = lax.axis_size("seq")
    span = tokens.shape[0]
    prefix_len = prefix_keys.shape[0] * seq_count
    near, far = rope_tables(span, seq_count, prefix_len)
    near, far = jnp.asarray(near), jnp.asarray(far)
    sign = jnp.asarray(signs(), BF16)

    own = jnp.concatenate([prefix_keys.T, prefix_values.T], 0)
    other = to_head_pair(own)
    sib_own = to_sibling(own)
    q, kv, *pieces = project(
        tokens, norm_gain.reshape(-1, HD), w_query, w_key.T, w_value.T, near, far, sign, w_out
    )
    kv_other = to_head_pair(kv)
    queries = [q] + [along_x(q, d) for d in (1, 2, 3)]
    weights = [pieces[0]] + [along_first(pieces[d], d) for d in (1, 2, 3)]
    kv_other, other, queries[1], queries[3] = lax.optimization_barrier(
        (kv_other, other, queries[1], queries[3])
    )
    sib_other = to_sibling(other)
    seg, stay = segment(
        kv, kv_other, own, other, near, far, sign, keep_rows[0], owners.reshape(owners.shape[1:3])
    )
    sib_seg = to_sibling(seg)
    queries[3], weights[2] = lax.optimization_barrier((queries[3], weights[2]))
    parts = [None] * RING
    for d in (3, 1, 2, 0):
        part = attend(
            d, queries[d], own, other, sib_own, sib_other, seg, sib_seg, stay
        )
        parts[d] = along_x(part, -d) if d else part
    contexts = merge(parts, sign)
    contexts = [contexts[0]] + [along_first(contexts[d], d) for d in (1, 2, 3)]
    far_share, = project_out((2,), contexts, weights)
    share_1, share_3, kept_own, share = project_out((1, 3, 0), contexts, weights)
    arrived = [
        along_second(value, k) for value, k in ((share_1, 1), (far_share, 2), (share_3, 3))
    ]
    return tuple(finish(share, kept_own, arrived))


def solution(mesh):
    return jax.shard_map(
        shards,
        mesh=mesh,
        in_specs=(
            P("seq", None),
            P(),
            P(None, "tp"),
            P(None, "tp"),
            P(None, "tp"),
            P("tp", None),
            P("seq", "tp"),
            P("seq", "tp"),
            P("seq", None, None),
            P("seq", None, None, None),
        ),
        out_specs=(P("seq", "tp"), P(("seq", "tp"), None)),
        check_vma=False,
    )
```

```python
import functools
import math

import jax
import jax.numpy as jnp
import numpy as np
from jax import lax
from jax.experimental import pallas as pl
from jax.experimental.pallas import tpu as pltpu
from jax.sharding import PartitionSpec as P

EPSILON = 1e-05
ROPE_BASE = 500000.0
LOWEST = -1e30
LOG2E = math.log2(math.e)
SAFE_BOUND = 60.0
HD = 128
HALF = 64
AXES = ("seq", "tp")
RING = 4
TILE = 512
CHUNKS = 4
CUT_AT = 2
WHOLE_AT = 1
NOTE = 16
SPANS = 8
EXTRA = 32 + 128

NT = (((1,), (1,)), ((), ()))
TN = (((0,), (1,)), ((), ()))
F32 = jnp.float32
BF16 = jnp.bfloat16


def device_at(x, core, z, y):
    return ((x & 3) * 2 + core) * 16 + (z & 3) * 4 + (y & 3)


def pairs_of(move):
    return [
        (device_at(x, c, z, y), device_at(*move(x, c, z, y)))
        for x in range(RING)
        for c in range(2)
        for z in range(RING)
        for y in range(RING)
    ]


def send(value, move):
    return lax.ppermute(value, AXES, pairs_of(move))


def to_sibling(value):
    return send(value, lambda x, c, z, y: (x, 1 - c, z, y))


def to_head_pair(value):
    return send(value, lambda x, c, z, y: (x, c, z, y ^ 1))


def along_x(value, step):
    return send(value, lambda x, c, z, y: (x + step, c, z, y))


def along_first(value, step):
    return send(
        value, lambda x, c, z, y: (x, c, z + step, y) if c == 0 else (x, c, z, y + step)
    )


def along_second(value, step):
    return send(
        value, lambda x, c, z, y: (x, c, z, y + step) if c == 0 else (x, c, z + step, y)
    )


def position():
    seq, tp = lax.axis_index("seq"), lax.axis_index("tp")
    return seq >> 1, seq & 1, tp >> 2, tp & 3, tp & 1, seq, tp >> 1


def signs():
    index = np.arange(HD)
    both = index[:, None] & index[None, :]
    parity = np.zeros((HD, HD), np.int64)
    for bit in range(7):
        parity += both >> bit & 1
    plain = (1 - 2 * (parity % 2)).astype(np.float32)
    return np.concatenate([plain, np.roll(plain, HALF, axis=1)])


def rope_tables(span, spans, prefix):
    freq = np.exp(-np.arange(HALF) * (2.0 * math.log(ROPE_BASE) / HD))
    freq = np.concatenate([freq, freq])
    near = np.arange(span)[:, None] * freq[None, :]
    far = (prefix + span * np.arange(spans))[:, None] * freq[None, :]
    both = [np.cos(near), np.sin(near), np.cos(far), np.sin(far), signs()]
    return np.concatenate(both).astype(np.float32)


def turn_of(tables, parity, span):
    begin = 2 * span + 2 * SPANS + HD * parity
    return tables[pl.ds(begin, HD), :].astype(BF16)


def rope_factors(tables, number, span):
    cos_near, sin_near = tables[:span, :], tables[span:2 * span, :]
    cos_far = tables[pl.ds(2 * span + number, 1), :]
    sin_far = tables[pl.ds(2 * span + SPANS + number, 1), :]
    cosine = cos_near * cos_far - sin_near * sin_far
    sine = sin_near * cos_far + cos_near * sin_far
    lane = lax.broadcasted_iota(jnp.int32, (1, HD), 1)
    return cosine, jnp.where(lane < HALF, -sine, sine)


def project_kernel(
    tokens, gain, w_q, w_kt, w_vt, near, w_out, q_out, kv_out, w0, w1, w2, w3,
    held, held_q, held_kv, held_near, held_w, sum_q, sum_kv, sems, cut_sems,
):
    x, core, z, y, parity, number, group = position()
    span, width = tokens.shape
    block = width // CHUNKS
    parts = [pl.ds(i * block, block) for i in range(CHUNKS)]
    arrive = []
    for i, at in enumerate(parts):
        moves = (
            (tokens.at[:, at], held.at[:, at]),
            (w_q.at[at], held_q.at[at]),
            (w_kt.at[:, at], held_kv.at[:HALF, at]),
            (w_vt.at[:, at], held_kv.at[HALF:, at]),
        )
        arrive.append([
            pltpu.make_async_copy(start, end, sems.at[4 * i + j])
            for j, (start, end) in enumerate(moves)
        ])
    tables = pltpu.make_async_copy(near, held_near, sems.at[4 * CHUNKS])
    whole = pltpu.make_async_copy(w_out, held_w, sems.at[4 * CHUNKS + 1])
    for i, copies in enumerate(arrive):
        for copy in copies:
            copy.start()
        if i == WHOLE_AT:
            whole.start()
    tables.start()
    cuts = []
    for d, piece in enumerate((w0, w1, w2, w3)):
        for k in range(RING):
            row = (z + jnp.where(core == 0, d, k)) & 3
            col = (y + jnp.where(core == 0, k, d)) & 3
            begin = pl.multiple_of((row * RING + col) * 256, 256)
            cuts.append(
                pltpu.make_async_copy(
                    held_w.at[:, pl.ds(begin, 256)],
                    piece.at[:, pl.ds(k * 256, 256)],
                    cut_sems.at[d * RING + k],
                )
            )
    squares = None
    per = block // HD
    for i, at in enumerate(parts):
        for copy in arrive[i]:
            copy.wait()
        if i == CUT_AT:
            whole.wait()
            for copy in cuts:
                copy.start()
        gains = jnp.concatenate([gain[j:j + 1, :] for j in range(i * per, (i + 1) * per)], 1)
        begin, end = i * block, (i + 1) * block
        hidden = held[:, begin:end].astype(F32)
        weighted = (hidden * gains.astype(F32)).astype(BF16)
        hidden = hidden * hidden
        for j in range(per):
            square = hidden[:, j * HD:(j + 1) * HD]
            squares = square if squares is None else squares + square
        part_q = jnp.dot(weighted, held_q[begin:end, :], preferred_element_type=F32)
        part_kv = lax.dot_general(
            weighted, held_kv[:, begin:end], NT, preferred_element_type=F32
        )
        if i == 0:
            sum_q[...] = part_q
            sum_kv[...] = part_kv
        else:
            sum_q[...] += part_q
            sum_kv[...] += part_kv
    scale = lax.rsqrt(jnp.sum(squares, -1, keepdims=True) / width + EPSILON)
    kv_out[...] = (sum_kv[...] * scale).astype(BF16)
    tables.wait()
    cosine, sine = rope_factors(held_near, number, span)
    turn = turn_of(held_near, parity, span)
    for h in range(2):
        head = sum_q[:, h * HD:(h + 1) * HD] * scale
        head = head * cosine + pltpu.roll(head, HALF, 1) * sine
        head = (head * HD ** -0.5).astype(BF16)
        head = jnp.dot(head, turn, preferred_element_type=F32)
        q_out[h * span:(h + 1) * span, :] = (head * (HD ** -0.5 * LOG2E)).astype(BF16)
    for copy in cuts:
        copy.wait()


def project(tokens, gain, w_q, w_kt, w_vt, near, w_out):
    span, width = tokens.shape
    remain = pl.BlockSpec(memory_space=pl.ANY)
    return pl.pallas_call(
        project_kernel,
        in_specs=[remain, vmem()] + [remain] * 5,
        out_specs=[vmem(), vmem()] + [remain] * 4,
        out_shape=[
            jax.ShapeDtypeStruct((2 * span, HD), BF16),
            jax.ShapeDtypeStruct((span, HD), BF16),
        ] + [jax.ShapeDtypeStruct((w_out.shape[0], 1024), BF16)] * 4,
        scratch_shapes=[
            pltpu.VMEM((span, width), BF16),
            pltpu.VMEM((width, 2 * HD), BF16),
            pltpu.VMEM((HD, width), BF16),
            pltpu.VMEM(near.shape, F32),
            pltpu.VMEM(w_out.shape, BF16),
            pltpu.VMEM((span, 2 * HD), F32),
            pltpu.VMEM((span, HD), F32),
            pltpu.SemaphoreType.DMA((4 * CHUNKS + 2,)),
            pltpu.SemaphoreType.DMA((RING * RING,)),
        ],
        compiler_params=pltpu.CompilerParams(vmem_limit_bytes=52 << 20),
        cost_estimate=pl.CostEstimate(
            flops=2 * span * width * 384, bytes_accessed=7 << 20, transcendentals=0
        ),
    )(tokens, gain, w_q, w_kt, w_vt, near, w_out)


def largest(rows, axis):
    return jnp.max(jnp.sum(rows * rows, axis, keepdims=True))


def segment_kernel(
    own, other, prefix, prefix_other, tables, rows, owners, seg_out, stay_out,
    held, sem,
):
    x, core, z, y, parity, number, group = position()
    odd = parity == 1
    arrive = pltpu.make_async_copy(own, held, sem)
    arrive.start()
    span, keep = own.shape[0], rows.shape[1]
    row = rows[pl.ds(group, 1), :]
    owner = owners[pl.ds(group, 1), :]
    place = lax.broadcasted_iota(jnp.int32, (256, 1), 0)
    to_core = jnp.where(place >= 128, 1 - core, core)
    step_first, step_second = (place >> 3) & 3, (place >> 1) & 3
    to_x = (x + (place >> 5)) & 3
    to_z = (z + jnp.where(to_core == 0, step_first, step_second)) & 3
    to_y = (y + jnp.where(to_core == 0, step_second, step_first)) & 3
    named = owner == device_at(to_x, to_core, to_z, to_y)
    before = lax.broadcasted_iota(jnp.int32, (keep, keep), 0) < lax.broadcasted_iota(
        jnp.int32, (keep, keep), 1
    )
    rank = jnp.dot(
        jnp.where(named, 1.0, 0.0).astype(BF16),
        jnp.where(before, 1.0, 0.0).astype(BF16),
        preferred_element_type=F32,
    )
    slot = (2 * parity + (place & 1)).astype(F32)
    picks = jnp.where(jnp.logical_and(named, rank == slot), 1.0, 0.0).astype(BF16)
    places = jnp.where(
        lax.broadcasted_iota(jnp.int32, (span, keep), 0) == row, 1.0, 0.0
    ).astype(BF16)
    chosen = lax.dot_general(picks, places, NT, preferred_element_type=F32).astype(BF16)
    arrive.wait()
    mine, theirs = held[...].astype(F32), other[...].astype(F32)
    first = jnp.where(odd, theirs, mine)
    second = jnp.where(odd, mine, theirs)
    lane = lax.broadcasted_iota(jnp.int32, (1, HD), 1)
    key = jnp.where(lane < HALF, first, pltpu.roll(second, HALF, 1))
    value = jnp.where(lane < HALF, pltpu.roll(first, HALF, 1), second).astype(BF16)
    cosine, sine = rope_factors(tables, number, own.shape[0])
    key = (key * cosine + pltpu.roll(key, HALF, 1) * sine).astype(BF16)
    turn = turn_of(tables, parity, own.shape[0])
    unit = HD ** -0.5
    for i, part in enumerate((key, value)):
        turned = lax.dot_general(turn, part, TN, preferred_element_type=F32) * unit
        seg_out[i * HD:(i + 1) * HD, :] = turned.astype(BF16)
    longest = largest(seg_out[:HD, :].astype(F32), 0)
    halves = [ref[:HALF, :].astype(F32) for ref in (prefix, prefix_other)]
    longest = jnp.maximum(longest, largest(jnp.concatenate(halves, 0), 0)) * 1.01
    seg_out[2 * HD:2 * HD + NOTE, :] = jnp.full((NOTE, own.shape[0]), longest, F32).astype(BF16)
    plain = turn_of(tables, 0, own.shape[0])
    pair = jnp.concatenate(
        [
            (jnp.dot(key, plain, preferred_element_type=F32) * unit).astype(BF16),
            (jnp.dot(value, plain, preferred_element_type=F32) * unit).astype(BF16),
        ],
        1,
    )
    kept = jnp.dot(chosen, pair, preferred_element_type=F32).astype(BF16)
    stay_out[...] = kept[:128, :]
    for i in range(2):
        seg_out[2 * HD + NOTE:, i * 256:(i + 1) * 256] = kept[128 + 64 * i:192 + 64 * i, :]


def vmem():
    return pl.BlockSpec(memory_space=pltpu.VMEM)


def segment(own, *rest):
    span = own.shape[0]
    return pl.pallas_call(
        segment_kernel,
        in_specs=[pl.BlockSpec(memory_space=pl.ANY)] + [vmem()] * 6,
        out_specs=[vmem()] * 2,
        out_shape=[
            jax.ShapeDtypeStruct((2 * HD + NOTE + 64, span), BF16),
            jax.ShapeDtypeStruct((128, 2 * HD), BF16),
        ],
        scratch_shapes=[pltpu.VMEM((span, HD), BF16), pltpu.SemaphoreType.DMA],
        compiler_params=pltpu.CompilerParams(vmem_limit_bytes=24 << 20),
        cost_estimate=pl.CostEstimate(
            flops=400_000_000, bytes_accessed=2 << 20, transcendentals=0
        ),
    )(own, *rest)


def attend_kernel(
    step, q, own, other, sib_own, sib_other, seg, sib_seg, stay, out, acc, total, top, held
):
    x, core = position()[:2]
    rows = q.shape[0]
    span = seg.shape[1]
    blocks = own.shape[1] // TILE
    prefix = ((own, other), (sib_own, sib_other))

    def prefix_tile(pair, columns):
        mine, theirs = pair
        keys = jnp.concatenate([mine[:HALF, columns], theirs[:HALF, columns]], 0)
        values = jnp.concatenate([mine[HALF:, columns], theirs[HALF:, columns]], 0)
        return keys, values

    longest = jnp.maximum(
        jnp.max(seg[2 * HD:2 * HD + NOTE, :HD].astype(F32)),
        jnp.max(sib_seg[2 * HD:2 * HD + NOTE, :HD].astype(F32)),
    )
    widest = largest(q[...].astype(F32), 1)
    calm = longest * widest < SAFE_BOUND * SAFE_BOUND

    if step == 0:
        whole_flags = (None, core == 1)
    else:
        later = lax.rem(x + RING - step, RING) > x
        whole_flags = (later, later)

    def causal(begin, count):
        token = lax.rem(lax.broadcasted_iota(jnp.int32, (count, span), 0) + begin, span)
        return lax.broadcasted_iota(jnp.int32, (count, span), 1) <= token

    acc[...] = jnp.zeros_like(acc)
    total[...] = jnp.zeros_like(total)

    @pl.when(calm)
    def _():
        def tile(keys, values, masked=False):
            scores = jnp.dot(q[...], keys, preferred_element_type=F32)
            weights = jnp.exp2(scores)
            if masked:
                weights = jnp.where(causal(0, rows), weights, 0.0)
            part = weights[:, :HD]
            for i in range(1, TILE // HD):
                part = part + weights[:, i * HD:(i + 1) * HD]
            mixed = lax.dot_general(weights.astype(BF16), values, NT, preferred_element_type=F32)
            acc[...] += mixed
            total[...] += part

        for pair in prefix:
            def some_tiles(i, carry, pair=pair):
                for j in range(2):
                    begin = pl.multiple_of((2 * i + j) * TILE, TILE)
                    tile(*prefix_tile(pair, pl.ds(begin, TILE)))
                return carry

            lax.fori_loop(0, blocks // 2, some_tiles, 0)
        for ref, flag in zip((seg, sib_seg), whole_flags):
            if flag is None:
                tile(ref[:HD, :], ref[HD:2 * HD, :], masked=True)
            else:
                @pl.when(flag)
                def _(ref=ref):
                    tile(ref[:HD, :], ref[HD:2 * HD, :])
        top[...] = jnp.zeros_like(top)

    @pl.when(jnp.logical_not(calm))
    def _():
        top[...] = jnp.full_like(top, LOWEST)
        chunk = 256
        seg_flag = 1 if whole_flags[0] is None else whole_flags[0].astype(jnp.int32)
        sib_flag = whole_flags[1].astype(jnp.int32)

        def some_keys(b, carry):
            column = pl.ds(pl.multiple_of(lax.rem(b, blocks) * TILE, TILE), TILE)
            for number, pair in enumerate(prefix):
                @pl.when(b // blocks == number)
                def _(pair=pair):
                    for i in range(2):
                        for j, ref in enumerate(pair):
                            begin = i * HD + j * HALF
                            held[begin:begin + HALF, :] = ref[i * HALF:(i + 1) * HALF, column]

            for number, ref in enumerate((seg, sib_seg)):
                @pl.when(b == 2 * blocks + number)
                def _(ref=ref):
                    held[...] = ref[:2 * HD, :]

            last = b == 2 * blocks
            flag = jnp.where(last, seg_flag, jnp.where(b > 2 * blocks, sib_flag, 1))
            causal_from = 0 if step else jnp.where(last, 0, -span)

            def some_rows(r, carry):
                begin = pl.multiple_of(r * chunk, chunk)
                at = pl.ds(begin, chunk)
                scores = jnp.dot(q[at, :], held[:HD, :], preferred_element_type=F32)
                if step == 0:
                    token = lax.rem(
                        lax.broadcasted_iota(jnp.int32, (chunk, span), 0) + begin, span
                    )
                    column = lax.broadcasted_iota(jnp.int32, (chunk, span), 1) + causal_from
                    scores = jnp.where(column <= token, scores, -jnp.inf)
                old = top[at, :]
                new = jnp.maximum(old, jnp.max(scores, 1, keepdims=True))
                weights = jnp.exp2(scores - new[:, :1])
                factor = jnp.exp2(old - new)
                part = weights[:, :HD]
                for i in range(1, TILE // HD):
                    part = part + weights[:, i * HD:(i + 1) * HD]
                mixed = lax.dot_general(
                    weights.astype(BF16), held[HD:, :], NT, preferred_element_type=F32
                )
                acc[at, :] = acc[at, :] * factor + mixed
                total[at, :] = total[at, :] * factor + part
                top[at, :] = new
                return carry

            @pl.when(flag == 1)
            def _():
                lax.fori_loop(0, rows // chunk, some_rows, 0)

            return carry

        lax.fori_loop(0, 2 * blocks + 2, some_keys, 0)

    summed = jnp.sum(total[...], 1, keepdims=True)
    out[:rows, :] = (acc[...] / summed).astype(BF16)
    level = top[...] + jnp.log2(summed)
    eye = lax.broadcasted_iota(jnp.int32, (1, HD, HD), 1) == lax.broadcasted_iota(
        jnp.int32, (1, HD, HD), 2
    )
    packed = jnp.sum(jnp.where(eye, level.reshape(rows // HD, HD, HD), 0.0), 1)
    high = packed.astype(BF16).astype(F32)
    rest = packed - high
    middle = rest.astype(BF16).astype(F32)
    low = rest - middle
    out[rows:rows + 32, :] = jnp.concatenate(
        [high, middle, low, jnp.zeros_like(high)], 0
    ).astype(BF16)
    back = (RING - step) % RING
    begin, lanes = 2 * HD + NOTE + 32 * (back % 2), 2 * HD * (back // 2)
    for i in range(2):
        place, half = rows + 32 + 64 * i, slice(i * HD, (i + 1) * HD)
        out[place:place + 32, :] = stay[32 * back:32 * (back + 1), half]
        half = slice(lanes + i * HD, lanes + (i + 1) * HD)
        out[place + 32:place + 64, :] = sib_seg[begin:begin + 32, half]


def attend(step, q, *rest):
    rows = q.shape[0]
    return pl.pallas_call(
        functools.partial(attend_kernel, step),
        in_specs=[vmem()] * 8,
        out_specs=vmem(),
        out_shape=jax.ShapeDtypeStruct((rows + EXTRA, HD), BF16),
        scratch_shapes=[pltpu.VMEM((rows, HD), F32)] * 3 + [pltpu.VMEM((2 * HD, TILE), BF16)],
        compiler_params=pltpu.CompilerParams(vmem_limit_bytes=32 << 20),
        cost_estimate=pl.CostEstimate(
            flops=8 * rows * HD * 4096, bytes_accessed=4 << 20, transcendentals=rows * 4096
        ),
    )(q, *rest)


def shuffle(rows, source):
    here = lax.broadcasted_iota(jnp.int32, (256, 256), 0)
    there = lax.broadcasted_iota(jnp.int32, (256, 256), 1)
    moves = jnp.where(source(here) == there, 1.0, 0.0).astype(BF16)
    return jnp.dot(moves, rows, preferred_element_type=F32).astype(BF16)


def merge_kernel(p0, p1, p2, p3, sign, *outs):
    parity = position()[4]
    parts = (p0, p1, p2, p3)
    rows = p0.shape[0] - EXTRA
    count = rows // HD
    levels = []
    for part in parts:
        stats = part[rows:rows + 32, :].astype(F32)
        levels.append(stats[:count] + stats[count:2 * count] + stats[2 * count:3 * count])
    most = functools.reduce(jnp.maximum, levels)
    shares = [jnp.exp2(level - most) for level in levels]
    whole = functools.reduce(jnp.add, shares)
    shares = [share / whole for share in shares]
    eye = lax.broadcasted_iota(jnp.int32, (HD, HD), 0) == lax.broadcasted_iota(
        jnp.int32, (HD, HD), 1
    )
    turn = sign[pl.ds(HD * parity, HD), :]
    per_head = count // 2
    for b in range(count):
        left, right = [], []
        for share, part in zip(shares, parts):
            block = part[b * HD:(b + 1) * HD, :]
            left.append(jnp.where(eye, share[b:b + 1, :], 0.0).astype(BF16))
            right.append(block)
        mixed = jnp.dot(
            jnp.concatenate(left, 1), jnp.concatenate(right, 0), preferred_element_type=F32
        )
        plain = lax.dot_general(mixed.astype(BF16), turn, NT, preferred_element_type=F32)
        head, place = b // per_head, b % per_head
        block = (plain * HD ** -0.5).astype(BF16)
        for out in outs:
            out[place * HD:(place + 1) * HD, head * HD:(head + 1) * HD] = block
    kept = jnp.concatenate(
        [
            jnp.concatenate([part[rows + 32:rows + 96, :], part[rows + 96:, :]], 1)
            for part in parts
        ],
        0,
    )
    kept = shuffle(
        kept,
        lambda r: ((r >> 4) & 3) << 6 | ((r >> 3) & 1) << 5 | (r >> 6) << 3 | (r & 7),
    )
    for k, out in enumerate(outs):
        out[rows // 2:, :] = kept[64 * k:64 * (k + 1), :]


def merge(parts, sign):
    rows = parts[0].shape[0] - EXTRA
    return pl.pallas_call(
        merge_kernel,
        in_specs=[vmem()] * 5,
        out_specs=[vmem()] * RING,
        out_shape=[jax.ShapeDtypeStruct((rows // 2 + 64, 2 * HD), BF16)] * RING,
        compiler_params=pltpu.CompilerParams(vmem_limit_bytes=24 << 20),
        cost_estimate=pl.CostEstimate(
            flops=400_000_000, bytes_accessed=2 << 20, transcendentals=0
        ),
    )(*parts, sign)


def out_kernel(places, c0, c1, c2, c3, w0, w1, w2, w3, *outs):
    contexts = (c0, c1, c2, c3)
    span = c0.shape[0] - 64
    kept = jnp.concatenate([c[span:, :] for c in contexts], 0)
    kept = shuffle(
        kept,
        lambda r: ((r >> 4) & 3) << 6
        | ((r >> 2) & 3) << 4
        | ((r >> 1) & 1) << 3
        | (r >> 6) << 1
        | (r & 1),
    )
    for k, out in zip(places, outs):
        columns = slice(k * 256, (k + 1) * 256)
        whole = None
        for c, w in zip(contexts, (w0, w1, w2, w3)):
            part = jnp.dot(c[:span, :], w[:, columns], preferred_element_type=F32)
            whole = part if whole is None else whole + part
        begin = span if k else 0
        if k:
            out[:span, :] = whole.astype(BF16)
        else:
            outs[-1][...] = whole
        out[begin:, :] = kept[64 * k:64 * (k + 1), :]


def project_out(places, contexts, weights):
    total = contexts[0].shape[0]
    span = total - 64
    shapes = [jax.ShapeDtypeStruct((total if k else 64, 256), BF16) for k in places]
    if 0 in places:
        shapes.append(jax.ShapeDtypeStruct((span, 256), F32))
    return pl.pallas_call(
        functools.partial(out_kernel, places),
        in_specs=[vmem()] * 8,
        out_specs=[vmem()] * len(shapes),
        out_shape=shapes,
        compiler_params=pltpu.CompilerParams(vmem_limit_bytes=24 << 20),
        cost_estimate=pl.CostEstimate(
            flops=512 * span * 1024 * len(places), bytes_accessed=5 << 20, transcendentals=0
        ),
    )(*contexts, *weights)


def finish_kernel(share, kept, a1, a2, a3, attn_out, kept_out):
    x, core, z, y = position()[:4]
    arrived = (a1, a2, a3)
    span = share.shape[0]
    whole = share[...]
    for part in arrived:
        whole = whole + part[:span, :].astype(F32)
    attn_out[...] = whole.astype(BF16)
    rows = jnp.concatenate([kept[...]] + [part[span:, :] for part in arrived], 0)
    place = lax.broadcasted_iota(jnp.int32, (1, 256), 1)
    back_second, back_first = place >> 6, (place >> 4) & 3
    from_x = (x + (place >> 2)) & 3
    from_core = (core + (place >> 1)) & 1
    from_z = (z - jnp.where(core == 0, back_first, back_second)) & 3
    from_y = (y - jnp.where(core == 0, back_second, back_first)) & 3
    target = device_at(from_x, from_core, from_z, from_y) * 2 + (place & 1)
    here = lax.broadcasted_iota(jnp.int32, (256, 256), 0)
    moves = jnp.where(here == target, 1.0, 0.0).astype(BF16)
    kept_out[...] = jnp.dot(moves, rows, preferred_element_type=F32).astype(BF16)


def finish(share, kept, arrived):
    return pl.pallas_call(
        finish_kernel,
        in_specs=[vmem()] * 5,
        out_specs=[vmem()] * 2,
        out_shape=[
            jax.ShapeDtypeStruct(share.shape, BF16),
            jax.ShapeDtypeStruct((256, 2 * HD), BF16),
        ],
        compiler_params=pltpu.CompilerParams(vmem_limit_bytes=24 << 20),
    )(share, kept, *arrived)


def shards(
    tokens, norm_gain, w_query, w_key, w_value, w_out, prefix_keys, prefix_values, keep_rows, owners
):
    seq_count = lax.axis_size("seq")
    span = tokens.shape[0]
    prefix_len = prefix_keys.shape[0] * seq_count
    tables = jnp.asarray(rope_tables(span, SPANS, prefix_len))
    sign = jnp.asarray(signs(), BF16)

    own = jnp.concatenate([prefix_keys.T, prefix_values.T], 0)
    other = to_head_pair(own)
    sib_own = to_sibling(own)
    q, kv, *pieces = project(
        tokens, norm_gain.reshape(-1, HD), w_query, w_key.T, w_value.T, tables, w_out
    )
    kv_other = to_head_pair(kv)
    queries = [q] + [along_x(q, d) for d in (1, 2, 3)]
    weights = [pieces[0]] + [along_first(pieces[d], d) for d in (1, 2, 3)]
    kv_other, other, queries[1], queries[3] = lax.optimization_barrier(
        (kv_other, other, queries[1], queries[3])
    )
    sib_other = to_sibling(other)
    seg, stay = segment(
        kv, kv_other, own, other, tables, keep_rows[0], owners.reshape(owners.shape[1:3])
    )
    sib_seg = to_sibling(seg)
    queries[3], weights[2] = lax.optimization_barrier((queries[3], weights[2]))
    parts = [None] * RING
    for d in (3, 1, 2, 0):
        part = attend(
            d, queries[d], own, other, sib_own, sib_other, seg, sib_seg, stay
        )
        parts[d] = along_x(part, -d) if d else part
    contexts = merge(parts, sign)
    contexts = [contexts[0]] + [along_first(contexts[d], d) for d in (1, 2, 3)]
    far_share, = project_out((2,), contexts, weights)
    share_1, share_3, kept_own, share = project_out((1, 3, 0), contexts, weights)
    arrived = [
        along_second(value, k) for value, k in ((share_1, 1), (far_share, 2), (share_3, 3))
    ]
    return tuple(finish(share, kept_own, arrived))


def solution(mesh):
    return jax.shard_map(
        shards,
        mesh=mesh,
        in_specs=(
            P("seq", None),
            P(),
            P(None, "tp"),
            P(None, "tp"),
            P(None, "tp"),
            P("tp", None),
            P("seq", "tp"),
            P("seq", "tp"),
            P("seq", None, None),
            P("seq", None, None, None),
        ),
        out_specs=(P("seq", "tp"), P(("seq", "tp"), None)),
        check_vma=False,
    )
```

```python
import functools
import math

import jax
import jax.numpy as jnp
import numpy as np
from jax import lax
from jax.experimental import pallas as pl
from jax.experimental.pallas import tpu as pltpu
from jax.sharding import PartitionSpec as P

EPSILON = 1e-05
ROPE_BASE = 500000.0
LOWEST = -1e30
LOG2E = math.log2(math.e)
SAFE_BOUND = 60.0
HD = 128
HALF = 64
AXES = ("seq", "tp")
RING = 4
TILE = 512
CHUNKS = 4
CUT_AT = 2
WHOLE_AT = 1
NOTE = 16
SPANS = 8
EXTRA = 32 + 128

NT = (((1,), (1,)), ((), ()))
TN = (((0,), (1,)), ((), ()))
F32 = jnp.float32
BF16 = jnp.bfloat16


def device_at(x, core, z, y):
    return ((x & 3) * 2 + core) * 16 + (z & 3) * 4 + (y & 3)


def pairs_of(move):
    return [
        (device_at(x, c, z, y), device_at(*move(x, c, z, y)))
        for x in range(RING)
        for c in range(2)
        for z in range(RING)
        for y in range(RING)
    ]


def send(value, move):
    return lax.ppermute(value, AXES, pairs_of(move))


def to_sibling(value):
    return send(value, lambda x, c, z, y: (x, 1 - c, z, y))


def to_head_pair(value):
    return send(value, lambda x, c, z, y: (x, c, z, y ^ 1))


def along_x(value, step):
    return send(value, lambda x, c, z, y: (x + step, c, z, y))


def along_first(value, step):
    return send(
        value, lambda x, c, z, y: (x, c, z + step, y) if c == 0 else (x, c, z, y + step)
    )


def along_second(value, step):
    return send(
        value, lambda x, c, z, y: (x, c, z, y + step) if c == 0 else (x, c, z + step, y)
    )


def position():
    seq, tp = lax.axis_index("seq"), lax.axis_index("tp")
    return seq >> 1, seq & 1, tp >> 2, tp & 3, tp & 1, seq, tp >> 1


def signs():
    index = np.arange(HD)
    both = index[:, None] & index[None, :]
    parity = np.zeros((HD, HD), np.int64)
    for bit in range(7):
        parity += both >> bit & 1
    plain = (1 - 2 * (parity % 2)).astype(np.float32)
    return np.concatenate([plain, np.roll(plain, HALF, axis=1)])


def rope_tables(span, spans, prefix):
    freq = np.exp(-np.arange(HALF) * (2.0 * math.log(ROPE_BASE) / HD))
    freq = np.concatenate([freq, freq])
    near = np.arange(span)[:, None] * freq[None, :]
    far = (prefix + span * np.arange(spans))[:, None] * freq[None, :]
    both = [np.cos(near), np.sin(near), np.cos(far), np.sin(far), signs()]
    return np.concatenate(both).astype(np.float32)


def turn_of(tables, parity, span):
    begin = 2 * span + 2 * SPANS + HD * parity
    return tables[pl.ds(begin, HD), :].astype(BF16)


def rope_factors(tables, number, span):
    cos_near, sin_near = tables[:span, :], tables[span:2 * span, :]
    cos_far = tables[pl.ds(2 * span + number, 1), :]
    sin_far = tables[pl.ds(2 * span + SPANS + number, 1), :]
    cosine = cos_near * cos_far - sin_near * sin_far
    sine = sin_near * cos_far + cos_near * sin_far
    lane = lax.broadcasted_iota(jnp.int32, (1, HD), 1)
    return cosine, jnp.where(lane < HALF, -sine, sine)


def project_kernel(
    tokens, gain, w_q, w_kt, w_vt, near, w_out, q_out, kv_out, w0, w1, w2, w3,
    held, held_q, held_kv, held_near, held_w, sum_q, sum_kv, sems, cut_sems,
):
    x, core, z, y, parity, number, group = position()
    span, width = tokens.shape
    block = width // CHUNKS
    parts = [pl.ds(i * block, block) for i in range(CHUNKS)]
    arrive = []
    for i, at in enumerate(parts):
        moves = (
            (tokens.at[:, at], held.at[:, at]),
            (w_q.at[at], held_q.at[at]),
            (w_kt.at[:, at], held_kv.at[:HALF, at]),
            (w_vt.at[:, at], held_kv.at[HALF:, at]),
        )
        arrive.append([
            pltpu.make_async_copy(start, end, sems.at[4 * i + j])
            for j, (start, end) in enumerate(moves)
        ])
    tables = pltpu.make_async_copy(near, held_near, sems.at[4 * CHUNKS])
    whole = pltpu.make_async_copy(w_out, held_w, sems.at[4 * CHUNKS + 1])
    for i, copies in enumerate(arrive):
        for copy in copies:
            copy.start()
        if i == WHOLE_AT:
            whole.start()
    tables.start()
    cuts = []
    for d, piece in enumerate((w0, w1, w2, w3)):
        for k in range(RING):
            row = (z + jnp.where(core == 0, d, k)) & 3
            col = (y + jnp.where(core == 0, k, d)) & 3
            begin = pl.multiple_of((row * RING + col) * 256, 256)
            cuts.append(
                pltpu.make_async_copy(
                    held_w.at[:, pl.ds(begin, 256)],
                    piece.at[:, pl.ds(k * 256, 256)],
                    cut_sems.at[d * RING + k],
                )
            )
    squares = None
    per = block // HD
    for i, at in enumerate(parts):
        for copy in arrive[i]:
            copy.wait()
        if i == CUT_AT:
            whole.wait()
            for copy in cuts:
                copy.start()
        gains = jnp.concatenate([gain[j:j + 1, :] for j in range(i * per, (i + 1) * per)], 1)
        begin, end = i * block, (i + 1) * block
        hidden = held[:, begin:end].astype(F32)
        weighted = (hidden * gains.astype(F32)).astype(BF16)
        hidden = hidden * hidden
        for j in range(per):
            square = hidden[:, j * HD:(j + 1) * HD]
            squares = square if squares is None else squares + square
        part_q = jnp.dot(weighted, held_q[begin:end, :], preferred_element_type=F32)
        part_kv = lax.dot_general(
            weighted, held_kv[:, begin:end], NT, preferred_element_type=F32
        )
        if i == 0:
            sum_q[...] = part_q
            sum_kv[...] = part_kv
        else:
            sum_q[...] += part_q
            sum_kv[...] += part_kv
    scale = lax.rsqrt(jnp.sum(squares, -1, keepdims=True) / width + EPSILON)
    kv_out[...] = (sum_kv[...] * scale).astype(BF16)
    tables.wait()
    cosine, sine = rope_factors(held_near, number, span)
    turn = turn_of(held_near, parity, span)
    for h in range(2):
        head = sum_q[:, h * HD:(h + 1) * HD] * scale
        head = head * cosine + pltpu.roll(head, HALF, 1) * sine
        head = (head * HD ** -0.5).astype(BF16)
        head = jnp.dot(head, turn, preferred_element_type=F32)
        q_out[h * span:(h + 1) * span, :] = (head * (HD ** -0.5 * LOG2E)).astype(BF16)
    for copy in cuts:
        copy.wait()


def project(tokens, gain, w_q, w_kt, w_vt, near, w_out):
    span, width = tokens.shape
    remain = pl.BlockSpec(memory_space=pl.ANY)
    return pl.pallas_call(
        project_kernel,
        in_specs=[remain, vmem()] + [remain] * 5,
        out_specs=[vmem(), vmem()] + [remain] * 4,
        out_shape=[
            jax.ShapeDtypeStruct((2 * span, HD), BF16),
            jax.ShapeDtypeStruct((span, HD), BF16),
        ] + [jax.ShapeDtypeStruct((w_out.shape[0], 1024), BF16)] * 4,
        scratch_shapes=[
            pltpu.VMEM((span, width), BF16),
            pltpu.VMEM((width, 2 * HD), BF16),
            pltpu.VMEM((HD, width), BF16),
            pltpu.VMEM(near.shape, F32),
            pltpu.VMEM(w_out.shape, BF16),
            pltpu.VMEM((span, 2 * HD), F32),
            pltpu.VMEM((span, HD), F32),
            pltpu.SemaphoreType.DMA((4 * CHUNKS + 2,)),
            pltpu.SemaphoreType.DMA((RING * RING,)),
        ],
        compiler_params=pltpu.CompilerParams(vmem_limit_bytes=52 << 20),
        cost_estimate=pl.CostEstimate(
            flops=2 * span * width * 384, bytes_accessed=7 << 20, transcendentals=0
        ),
    )(tokens, gain, w_q, w_kt, w_vt, near, w_out)


def largest(rows, axis):
    return jnp.max(jnp.sum(rows * rows, axis, keepdims=True))


def segment_kernel(
    own, other, prefix, prefix_other, tables, rows, owners, seg_out, stay_out,
    held, sem,
):
    x, core, z, y, parity, number, group = position()
    odd = parity == 1
    arrive = pltpu.make_async_copy(own, held, sem)
    arrive.start()
    span, keep = own.shape[0], rows.shape[1]
    row = rows[pl.ds(group, 1), :]
    owner = owners[pl.ds(group, 1), :]
    place = lax.broadcasted_iota(jnp.int32, (256, 1), 0)
    to_core = jnp.where(place >= 128, 1 - core, core)
    step_first, step_second = (place >> 3) & 3, (place >> 1) & 3
    to_x = (x + (place >> 5)) & 3
    to_z = (z + jnp.where(to_core == 0, step_first, step_second)) & 3
    to_y = (y + jnp.where(to_core == 0, step_second, step_first)) & 3
    named = owner == device_at(to_x, to_core, to_z, to_y)
    before = lax.broadcasted_iota(jnp.int32, (keep, keep), 0) < lax.broadcasted_iota(
        jnp.int32, (keep, keep), 1
    )
    rank = jnp.dot(
        jnp.where(named, 1.0, 0.0).astype(BF16),
        jnp.where(before, 1.0, 0.0).astype(BF16),
        preferred_element_type=F32,
    )
    slot = (2 * parity + (place & 1)).astype(F32)
    picks = jnp.where(jnp.logical_and(named, rank == slot), 1.0, 0.0).astype(BF16)
    places = jnp.where(
        lax.broadcasted_iota(jnp.int32, (span, keep), 0) == row, 1.0, 0.0
    ).astype(BF16)
    chosen = lax.dot_general(picks, places, NT, preferred_element_type=F32).astype(BF16)
    arrive.wait()
    mine, theirs = held[...].astype(F32), other[...].astype(F32)
    first = jnp.where(odd, theirs, mine)
    second = jnp.where(odd, mine, theirs)
    lane = lax.broadcasted_iota(jnp.int32, (1, HD), 1)
    key = jnp.where(lane < HALF, first, pltpu.roll(second, HALF, 1))
    value = jnp.where(lane < HALF, pltpu.roll(first, HALF, 1), second).astype(BF16)
    cosine, sine = rope_factors(tables, number, own.shape[0])
    key = (key * cosine + pltpu.roll(key, HALF, 1) * sine).astype(BF16)
    turn = turn_of(tables, parity, own.shape[0])
    unit = HD ** -0.5
    for i, part in enumerate((key, value)):
        turned = lax.dot_general(turn, part, TN, preferred_element_type=F32) * unit
        seg_out[i * HD:(i + 1) * HD, :] = turned.astype(BF16)
    longest = largest(seg_out[:HD, :].astype(F32), 0)
    halves = [ref[:HALF, :].astype(F32) for ref in (prefix, prefix_other)]
    longest = jnp.maximum(longest, largest(jnp.concatenate(halves, 0), 0)) * 1.01
    seg_out[2 * HD:2 * HD + NOTE, :] = jnp.full((NOTE, own.shape[0]), longest, F32).astype(BF16)
    plain = turn_of(tables, 0, own.shape[0])
    pair = jnp.concatenate(
        [
            (jnp.dot(key, plain, preferred_element_type=F32) * unit).astype(BF16),
            (jnp.dot(value, plain, preferred_element_type=F32) * unit).astype(BF16),
        ],
        1,
    )
    kept = jnp.dot(chosen, pair, preferred_element_type=F32).astype(BF16)
    stay_out[...] = kept[:128, :]
    for i in range(2):
        seg_out[2 * HD + NOTE:, i * 256:(i + 1) * 256] = kept[128 + 64 * i:192 + 64 * i, :]


def vmem():
    return pl.BlockSpec(memory_space=pltpu.VMEM)


def segment(own, *rest):
    span = own.shape[0]
    return pl.pallas_call(
        segment_kernel,
        in_specs=[pl.BlockSpec(memory_space=pl.ANY)] + [vmem()] * 6,
        out_specs=[vmem()] * 2,
        out_shape=[
            jax.ShapeDtypeStruct((2 * HD + NOTE + 64, span), BF16),
            jax.ShapeDtypeStruct((128, 2 * HD), BF16),
        ],
        scratch_shapes=[pltpu.VMEM((span, HD), BF16), pltpu.SemaphoreType.DMA],
        compiler_params=pltpu.CompilerParams(vmem_limit_bytes=24 << 20),
        cost_estimate=pl.CostEstimate(
            flops=400_000_000, bytes_accessed=2 << 20, transcendentals=0
        ),
    )(own, *rest)


def attend_kernel(
    step, q, own, other, sib_own, sib_other, seg, sib_seg, stay, out, acc, total, top, held
):
    x, core = position()[:2]
    rows = q.shape[0]
    span = seg.shape[1]
    blocks = own.shape[1] // TILE
    prefix = ((own, other), (sib_own, sib_other))

    def prefix_tile(pair, columns):
        mine, theirs = pair
        keys = jnp.concatenate([mine[:HALF, columns], theirs[:HALF, columns]], 0)
        values = jnp.concatenate([mine[HALF:, columns], theirs[HALF:, columns]], 0)
        return keys, values

    longest = jnp.maximum(
        jnp.max(seg[2 * HD:2 * HD + NOTE, :HD].astype(F32)),
        jnp.max(sib_seg[2 * HD:2 * HD + NOTE, :HD].astype(F32)),
    )
    widest = largest(q[...].astype(F32), 1)
    calm = longest * widest < SAFE_BOUND * SAFE_BOUND

    if step == 0:
        whole_flags = (None, core == 1)
    else:
        later = lax.rem(x + RING - step, RING) > x
        whole_flags = (later, later)

    def causal(begin, count):
        token = lax.rem(lax.broadcasted_iota(jnp.int32, (count, span), 0) + begin, span)
        return lax.broadcasted_iota(jnp.int32, (count, span), 1) <= token

    acc[...] = jnp.zeros_like(acc)
    total[...] = jnp.zeros_like(total)

    @pl.when(calm)
    def _():
        def tile(keys, values, masked=False):
            scores = jnp.dot(q[...], keys, preferred_element_type=F32)
            weights = jnp.exp2(scores)
            if masked:
                weights = jnp.where(causal(0, rows), weights, 0.0)
            part = weights[:, :HD]
            for i in range(1, TILE // HD):
                part = part + weights[:, i * HD:(i + 1) * HD]
            mixed = lax.dot_general(weights.astype(BF16), values, NT, preferred_element_type=F32)
            acc[...] += mixed
            total[...] += part

        for pair in prefix:
            def some_tiles(i, carry, pair=pair):
                for j in range(unroll):
                    begin = pl.multiple_of((unroll * i + j) * TILE, TILE)
                    tile(*prefix_tile(pair, pl.ds(begin, TILE)))
                return carry

            unroll = blocks if step < 2 else 2
            lax.fori_loop(0, blocks // unroll, some_tiles, 0)
        for ref, flag in zip((seg, sib_seg), whole_flags):
            if flag is None:
                tile(ref[:HD, :], ref[HD:2 * HD, :], masked=True)
            else:
                @pl.when(flag)
                def _(ref=ref):
                    tile(ref[:HD, :], ref[HD:2 * HD, :])
        top[...] = jnp.zeros_like(top)

    @pl.when(jnp.logical_not(calm))
    def _():
        top[...] = jnp.full_like(top, LOWEST)
        chunk = 256
        seg_flag = 1 if whole_flags[0] is None else whole_flags[0].astype(jnp.int32)
        sib_flag = whole_flags[1].astype(jnp.int32)

        def some_keys(b, carry):
            column = pl.ds(pl.multiple_of(lax.rem(b, blocks) * TILE, TILE), TILE)
            for number, pair in enumerate(prefix):
                @pl.when(b // blocks == number)
                def _(pair=pair):
                    for i in range(2):
                        for j, ref in enumerate(pair):
                            begin = i * HD + j * HALF
                            held[begin:begin + HALF, :] = ref[i * HALF:(i + 1) * HALF, column]

            for number, ref in enumerate((seg, sib_seg)):
                @pl.when(b == 2 * blocks + number)
                def _(ref=ref):
                    held[...] = ref[:2 * HD, :]

            last = b == 2 * blocks
            flag = jnp.where(last, seg_flag, jnp.where(b > 2 * blocks, sib_flag, 1))
            causal_from = 0 if step else jnp.where(last, 0, -span)

            def some_rows(r, carry):
                begin = pl.multiple_of(r * chunk, chunk)
                at = pl.ds(begin, chunk)
                scores = jnp.dot(q[at, :], held[:HD, :], preferred_element_type=F32)
                if step == 0:
                    token = lax.rem(
                        lax.broadcasted_iota(jnp.int32, (chunk, span), 0) + begin, span
                    )
                    column = lax.broadcasted_iota(jnp.int32, (chunk, span), 1) + causal_from
                    scores = jnp.where(column <= token, scores, -jnp.inf)
                old = top[at, :]
                new = jnp.maximum(old, jnp.max(scores, 1, keepdims=True))
                weights = jnp.exp2(scores - new[:, :1])
                factor = jnp.exp2(old - new)
                part = weights[:, :HD]
                for i in range(1, TILE // HD):
                    part = part + weights[:, i * HD:(i + 1) * HD]
                mixed = lax.dot_general(
                    weights.astype(BF16), held[HD:, :], NT, preferred_element_type=F32
                )
                acc[at, :] = acc[at, :] * factor + mixed
                total[at, :] = total[at, :] * factor + part
                top[at, :] = new
                return carry

            @pl.when(flag == 1)
            def _():
                lax.fori_loop(0, rows // chunk, some_rows, 0)

            return carry

        lax.fori_loop(0, 2 * blocks + 2, some_keys, 0)

    summed = jnp.sum(total[...], 1, keepdims=True)
    out[:rows, :] = (acc[...] / summed).astype(BF16)
    level = top[...] + jnp.log2(summed)
    eye = lax.broadcasted_iota(jnp.int32, (1, HD, HD), 1) == lax.broadcasted_iota(
        jnp.int32, (1, HD, HD), 2
    )
    packed = jnp.sum(jnp.where(eye, level.reshape(rows // HD, HD, HD), 0.0), 1)
    high = packed.astype(BF16).astype(F32)
    rest = packed - high
    middle = rest.astype(BF16).astype(F32)
    low = rest - middle
    out[rows:rows + 32, :] = jnp.concatenate(
        [high, middle, low, jnp.zeros_like(high)], 0
    ).astype(BF16)
    back = (RING - step) % RING
    begin, lanes = 2 * HD + NOTE + 32 * (back % 2), 2 * HD * (back // 2)
    for i in range(2):
        place, half = rows + 32 + 64 * i, slice(i * HD, (i + 1) * HD)
        out[place:place + 32, :] = stay[32 * back:32 * (back + 1), half]
        half = slice(lanes + i * HD, lanes + (i + 1) * HD)
        out[place + 32:place + 64, :] = sib_seg[begin:begin + 32, half]


def attend(step, q, *rest):
    rows = q.shape[0]
    return pl.pallas_call(
        functools.partial(attend_kernel, step),
        in_specs=[vmem()] * 8,
        out_specs=vmem(),
        out_shape=jax.ShapeDtypeStruct((rows + EXTRA, HD), BF16),
        scratch_shapes=[pltpu.VMEM((rows, HD), F32)] * 3 + [pltpu.VMEM((2 * HD, TILE), BF16)],
        compiler_params=pltpu.CompilerParams(vmem_limit_bytes=32 << 20),
        cost_estimate=pl.CostEstimate(
            flops=8 * rows * HD * 4096, bytes_accessed=4 << 20, transcendentals=rows * 4096
        ),
    )(q, *rest)


def shuffle(rows, source):
    here = lax.broadcasted_iota(jnp.int32, (256, 256), 0)
    there = lax.broadcasted_iota(jnp.int32, (256, 256), 1)
    moves = jnp.where(source(here) == there, 1.0, 0.0).astype(BF16)
    return jnp.dot(moves, rows, preferred_element_type=F32).astype(BF16)


def merge_kernel(p0, p1, p2, p3, sign, *outs):
    parity = position()[4]
    parts = (p0, p1, p2, p3)
    rows = p0.shape[0] - EXTRA
    count = rows // HD
    levels = []
    for part in parts:
        stats = part[rows:rows + 32, :].astype(F32)
        levels.append(stats[:count] + stats[count:2 * count] + stats[2 * count:3 * count])
    most = functools.reduce(jnp.maximum, levels)
    shares = [jnp.exp2(level - most) for level in levels]
    whole = functools.reduce(jnp.add, shares)
    shares = [share / whole for share in shares]
    eye = lax.broadcasted_iota(jnp.int32, (HD, HD), 0) == lax.broadcasted_iota(
        jnp.int32, (HD, HD), 1
    )
    turn = sign[pl.ds(HD * parity, HD), :]
    per_head = count // 2
    for b in range(count):
        left, right = [], []
        for share, part in zip(shares, parts):
            block = part[b * HD:(b + 1) * HD, :]
            left.append(jnp.where(eye, share[b:b + 1, :], 0.0).astype(BF16))
            right.append(block)
        mixed = jnp.dot(
            jnp.concatenate(left, 1), jnp.concatenate(right, 0), preferred_element_type=F32
        )
        plain = lax.dot_general(mixed.astype(BF16), turn, NT, preferred_element_type=F32)
        head, place = b // per_head, b % per_head
        block = (plain * HD ** -0.5).astype(BF16)
        for out in outs:
            out[place * HD:(place + 1) * HD, head * HD:(head + 1) * HD] = block
    kept = jnp.concatenate(
        [
            jnp.concatenate([part[rows + 32:rows + 96, :], part[rows + 96:, :]], 1)
            for part in parts
        ],
        0,
    )
    kept = shuffle(
        kept,
        lambda r: ((r >> 4) & 3) << 6 | ((r >> 3) & 1) << 5 | (r >> 6) << 3 | (r & 7),
    )
    for k, out in enumerate(outs):
        out[rows // 2:, :] = kept[64 * k:64 * (k + 1), :]


def merge(parts, sign):
    rows = parts[0].shape[0] - EXTRA
    return pl.pallas_call(
        merge_kernel,
        in_specs=[vmem()] * 5,
        out_specs=[vmem()] * RING,
        out_shape=[jax.ShapeDtypeStruct((rows // 2 + 64, 2 * HD), BF16)] * RING,
        compiler_params=pltpu.CompilerParams(vmem_limit_bytes=24 << 20),
        cost_estimate=pl.CostEstimate(
            flops=400_000_000, bytes_accessed=2 << 20, transcendentals=0
        ),
    )(*parts, sign)


def out_kernel(places, c0, c1, c2, c3, w0, w1, w2, w3, *outs):
    contexts = (c0, c1, c2, c3)
    span = c0.shape[0] - 64
    kept = jnp.concatenate([c[span:, :] for c in contexts], 0)
    kept = shuffle(
        kept,
        lambda r: ((r >> 4) & 3) << 6
        | ((r >> 2) & 3) << 4
        | ((r >> 1) & 1) << 3
        | (r >> 6) << 1
        | (r & 1),
    )
    for k, out in zip(places, outs):
        columns = slice(k * 256, (k + 1) * 256)
        whole = None
        for c, w in zip(contexts, (w0, w1, w2, w3)):
            part = jnp.dot(c[:span, :], w[:, columns], preferred_element_type=F32)
            whole = part if whole is None else whole + part
        begin = span if k else 0
        if k:
            out[:span, :] = whole.astype(BF16)
        else:
            outs[-1][...] = whole
        out[begin:, :] = kept[64 * k:64 * (k + 1), :]


def project_out(places, contexts, weights):
    total = contexts[0].shape[0]
    span = total - 64
    shapes = [jax.ShapeDtypeStruct((total if k else 64, 256), BF16) for k in places]
    if 0 in places:
        shapes.append(jax.ShapeDtypeStruct((span, 256), F32))
    return pl.pallas_call(
        functools.partial(out_kernel, places),
        in_specs=[vmem()] * 8,
        out_specs=[vmem()] * len(shapes),
        out_shape=shapes,
        compiler_params=pltpu.CompilerParams(vmem_limit_bytes=24 << 20),
        cost_estimate=pl.CostEstimate(
            flops=512 * span * 1024 * len(places), bytes_accessed=5 << 20, transcendentals=0
        ),
    )(*contexts, *weights)


def finish_kernel(share, kept, a1, a2, a3, attn_out, kept_out):
    x, core, z, y = position()[:4]
    arrived = (a1, a2, a3)
    span = share.shape[0]
    whole = share[...]
    for part in arrived:
        whole = whole + part[:span, :].astype(F32)
    attn_out[...] = whole.astype(BF16)
    rows = jnp.concatenate([kept[...]] + [part[span:, :] for part in arrived], 0)
    place = lax.broadcasted_iota(jnp.int32, (1, 256), 1)
    back_second, back_first = place >> 6, (place >> 4) & 3
    from_x = (x + (place >> 2)) & 3
    from_core = (core + (place >> 1)) & 1
    from_z = (z - jnp.where(core == 0, back_first, back_second)) & 3
    from_y = (y - jnp.where(core == 0, back_second, back_first)) & 3
    target = device_at(from_x, from_core, from_z, from_y) * 2 + (place & 1)
    here = lax.broadcasted_iota(jnp.int32, (256, 256), 0)
    moves = jnp.where(here == target, 1.0, 0.0).astype(BF16)
    kept_out[...] = jnp.dot(moves, rows, preferred_element_type=F32).astype(BF16)


def finish(share, kept, arrived):
    return pl.pallas_call(
        finish_kernel,
        in_specs=[vmem()] * 5,
        out_specs=[vmem()] * 2,
        out_shape=[
            jax.ShapeDtypeStruct(share.shape, BF16),
            jax.ShapeDtypeStruct((256, 2 * HD), BF16),
        ],
        compiler_params=pltpu.CompilerParams(vmem_limit_bytes=24 << 20),
    )(share, kept, *arrived)


def shards(
    tokens, norm_gain, w_query, w_key, w_value, w_out, prefix_keys, prefix_values, keep_rows, owners
):
    seq_count = lax.axis_size("seq")
    span = tokens.shape[0]
    prefix_len = prefix_keys.shape[0] * seq_count
    tables = jnp.asarray(rope_tables(span, SPANS, prefix_len))
    sign = jnp.asarray(signs(), BF16)

    own = jnp.concatenate([prefix_keys.T, prefix_values.T], 0)
    other = to_head_pair(own)
    sib_own = to_sibling(own)
    q, kv, *pieces = project(
        tokens, norm_gain.reshape(-1, HD), w_query, w_key.T, w_value.T, tables, w_out
    )
    kv_other = to_head_pair(kv)
    queries = [q] + [along_x(q, d) for d in (1, 2, 3)]
    weights = [pieces[0]] + [along_first(pieces[d], d) for d in (1, 2, 3)]
    kv_other, other, queries[1], queries[3] = lax.optimization_barrier(
        (kv_other, other, queries[1], queries[3])
    )
    sib_other = to_sibling(other)
    seg, stay = segment(
        kv, kv_other, own, other, tables, keep_rows[0], owners.reshape(owners.shape[1:3])
    )
    sib_seg = to_sibling(seg)
    queries[3], weights[2] = lax.optimization_barrier((queries[3], weights[2]))
    parts = [None] * RING
    for d in (3, 1, 2, 0):
        part = attend(
            d, queries[d], own, other, sib_own, sib_other, seg, sib_seg, stay
        )
        parts[d] = along_x(part, -d) if d else part
    contexts = merge(parts, sign)
    contexts = [contexts[0]] + [along_first(contexts[d], d) for d in (1, 2, 3)]
    far_share, = project_out((2,), contexts, weights)
    share_1, share_3, kept_own, share = project_out((1, 3, 0), contexts, weights)
    arrived = [
        along_second(value, k) for value, k in ((share_1, 1), (far_share, 2), (share_3, 3))
    ]
    return tuple(finish(share, kept_own, arrived))


def solution(mesh):
    return jax.shard_map(
        shards,
        mesh=mesh,
        in_specs=(
            P("seq", None),
            P(),
            P(None, "tp"),
            P(None, "tp"),
            P(None, "tp"),
            P("tp", None),
            P("seq", "tp"),
            P("seq", "tp"),
            P("seq", None, None),
            P("seq", None, None, None),
        ),
        out_specs=(P("seq", "tp"), P(("seq", "tp"), None)),
        check_vma=False,
    )
```

```python
import functools
import math

import jax
import jax.numpy as jnp
import numpy as np
from jax import lax
from jax.experimental import pallas as pl
from jax.experimental.pallas import tpu as pltpu
from jax.sharding import PartitionSpec as P

EPSILON = 1e-05
ROPE_BASE = 500000.0
LOWEST = -1e30
LOG2E = math.log2(math.e)
SAFE_BOUND = 60.0
HD = 128
HALF = 64
AXES = ("seq", "tp")
RING = 4
TILE = 512
CHUNKS = 4
CUT_AT = 2
WHOLE_AT = 1
NOTE = 16
SPANS = 8
EXTRA = 32 + 128

NT = (((1,), (1,)), ((), ()))
TN = (((0,), (1,)), ((), ()))
F32 = jnp.float32
BF16 = jnp.bfloat16


def device_at(x, core, z, y):
    return ((x & 3) * 2 + core) * 16 + (z & 3) * 4 + (y & 3)


def pairs_of(move):
    return [
        (device_at(x, c, z, y), device_at(*move(x, c, z, y)))
        for x in range(RING)
        for c in range(2)
        for z in range(RING)
        for y in range(RING)
    ]


def send(value, move):
    return lax.ppermute(value, AXES, pairs_of(move))


def to_sibling(value):
    return send(value, lambda x, c, z, y: (x, 1 - c, z, y))


def to_head_pair(value):
    return send(value, lambda x, c, z, y: (x, c, z, y ^ 1))


def along_x(value, step):
    return send(value, lambda x, c, z, y: (x + step, c, z, y))


def along_first(value, step):
    return send(
        value, lambda x, c, z, y: (x, c, z + step, y) if c == 0 else (x, c, z, y + step)
    )


def along_second(value, step):
    return send(
        value, lambda x, c, z, y: (x, c, z, y + step) if c == 0 else (x, c, z + step, y)
    )


def position():
    seq, tp = lax.axis_index("seq"), lax.axis_index("tp")
    return seq >> 1, seq & 1, tp >> 2, tp & 3, tp & 1, seq, tp >> 1


def signs():
    index = np.arange(HD)
    both = index[:, None] & index[None, :]
    parity = np.zeros((HD, HD), np.int64)
    for bit in range(7):
        parity += both >> bit & 1
    plain = (1 - 2 * (parity % 2)).astype(np.float32)
    return np.concatenate([plain, np.roll(plain, HALF, axis=1)])


def rope_tables(span, spans, prefix):
    freq = np.exp(-np.arange(HALF) * (2.0 * math.log(ROPE_BASE) / HD))
    freq = np.concatenate([freq, freq])
    near = np.arange(span)[:, None] * freq[None, :]
    far = (prefix + span * np.arange(spans))[:, None] * freq[None, :]
    both = [np.cos(near), np.sin(near), np.cos(far), np.sin(far), signs()]
    return np.concatenate(both).astype(np.float32)


def turn_of(tables, parity, span):
    begin = 2 * span + 2 * SPANS + HD * parity
    return tables[pl.ds(begin, HD), :].astype(BF16)


def rope_factors(tables, number, span):
    cos_near, sin_near = tables[:span, :], tables[span:2 * span, :]
    cos_far = tables[pl.ds(2 * span + number, 1), :]
    sin_far = tables[pl.ds(2 * span + SPANS + number, 1), :]
    cosine = cos_near * cos_far - sin_near * sin_far
    sine = sin_near * cos_far + cos_near * sin_far
    lane = lax.broadcasted_iota(jnp.int32, (1, HD), 1)
    return cosine, jnp.where(lane < HALF, -sine, sine)


def project_kernel(
    tokens, gain, w_q, w_kt, w_vt, near, w_out, q_out, kv_out, w0, w1, w2, w3,
    held, held_q, held_kv, held_near, held_w, sum_q, sum_kv, sems, cut_sems,
):
    x, core, z, y, parity, number, group = position()
    span, width = tokens.shape
    block = width // CHUNKS
    parts = [pl.ds(i * block, block) for i in range(CHUNKS)]
    arrive = []
    for i, at in enumerate(parts):
        moves = (
            (tokens.at[:, at], held.at[:, at]),
            (w_q.at[at], held_q.at[at]),
            (w_kt.at[:, at], held_kv.at[:HALF, at]),
            (w_vt.at[:, at], held_kv.at[HALF:, at]),
        )
        arrive.append([
            pltpu.make_async_copy(start, end, sems.at[4 * i + j])
            for j, (start, end) in enumerate(moves)
        ])
    tables = pltpu.make_async_copy(near, held_near, sems.at[4 * CHUNKS])
    whole = pltpu.make_async_copy(w_out, held_w, sems.at[4 * CHUNKS + 1])
    for i, copies in enumerate(arrive):
        for copy in copies:
            copy.start()
        if i == WHOLE_AT:
            whole.start()
    tables.start()
    cuts = []
    for d, piece in enumerate((w0, w1, w2, w3)):
        for k in range(RING):
            row = (z + jnp.where(core == 0, d, k)) & 3
            col = (y + jnp.where(core == 0, k, d)) & 3
            begin = pl.multiple_of((row * RING + col) * 256, 256)
            cuts.append(
                pltpu.make_async_copy(
                    held_w.at[:, pl.ds(begin, 256)],
                    piece.at[:, pl.ds(k * 256, 256)],
                    cut_sems.at[d * RING + k],
                )
            )
    squares = None
    per = block // HD
    for i, at in enumerate(parts):
        for copy in arrive[i]:
            copy.wait()
        if i == CUT_AT:
            whole.wait()
            for copy in cuts:
                copy.start()
        gains = jnp.concatenate([gain[j:j + 1, :] for j in range(i * per, (i + 1) * per)], 1)
        begin, end = i * block, (i + 1) * block
        hidden = held[:, begin:end].astype(F32)
        weighted = (hidden * gains.astype(F32)).astype(BF16)
        hidden = hidden * hidden
        for j in range(per):
            square = hidden[:, j * HD:(j + 1) * HD]
            squares = square if squares is None else squares + square
        part_q = jnp.dot(weighted, held_q[begin:end, :], preferred_element_type=F32)
        part_kv = lax.dot_general(
            weighted, held_kv[:, begin:end], NT, preferred_element_type=F32
        )
        if i == 0:
            sum_q[...] = part_q
            sum_kv[...] = part_kv
        else:
            sum_q[...] += part_q
            sum_kv[...] += part_kv
    scale = lax.rsqrt(jnp.sum(squares, -1, keepdims=True) / width + EPSILON)
    kv_out[...] = (sum_kv[...] * scale).astype(BF16)
    tables.wait()
    cosine, sine = rope_factors(held_near, number, span)
    turn = turn_of(held_near, parity, span)
    for h in range(2):
        head = sum_q[:, h * HD:(h + 1) * HD] * scale
        head = head * cosine + pltpu.roll(head, HALF, 1) * sine
        head = (head * HD ** -0.5).astype(BF16)
        head = jnp.dot(head, turn, preferred_element_type=F32)
        q_out[h * span:(h + 1) * span, :] = (head * (HD ** -0.5 * LOG2E)).astype(BF16)
    for copy in cuts:
        copy.wait()


def project(tokens, gain, w_q, w_kt, w_vt, near, w_out):
    span, width = tokens.shape
    remain = pl.BlockSpec(memory_space=pl.ANY)
    return pl.pallas_call(
        project_kernel,
        in_specs=[remain, vmem()] + [remain] * 5,
        out_specs=[vmem(), vmem()] + [remain] * 4,
        out_shape=[
            jax.ShapeDtypeStruct((2 * span, HD), BF16),
            jax.ShapeDtypeStruct((span, HD), BF16),
        ] + [jax.ShapeDtypeStruct((w_out.shape[0], 1024), BF16)] * 4,
        scratch_shapes=[
            pltpu.VMEM((span, width), BF16),
            pltpu.VMEM((width, 2 * HD), BF16),
            pltpu.VMEM((HD, width), BF16),
            pltpu.VMEM(near.shape, F32),
            pltpu.VMEM(w_out.shape, BF16),
            pltpu.VMEM((span, 2 * HD), F32),
            pltpu.VMEM((span, HD), F32),
            pltpu.SemaphoreType.DMA((4 * CHUNKS + 2,)),
            pltpu.SemaphoreType.DMA((RING * RING,)),
        ],
        compiler_params=pltpu.CompilerParams(vmem_limit_bytes=52 << 20),
        cost_estimate=pl.CostEstimate(
            flops=2 * span * width * 384, bytes_accessed=7 << 20, transcendentals=0
        ),
    )(tokens, gain, w_q, w_kt, w_vt, near, w_out)


def largest(rows, axis):
    return jnp.max(jnp.sum(rows * rows, axis, keepdims=True))


def segment_kernel(
    own, other, prefix, prefix_other, tables, rows, owners, seg_out, stay_out,
    held, sem,
):
    x, core, z, y, parity, number, group = position()
    odd = parity == 1
    arrive = pltpu.make_async_copy(own, held, sem)
    arrive.start()
    span, keep = own.shape[0], rows.shape[1]
    row = rows[pl.ds(group, 1), :]
    owner = owners[pl.ds(group, 1), :]
    place = lax.broadcasted_iota(jnp.int32, (256, 1), 0)
    to_core = jnp.where(place >= 128, 1 - core, core)
    step_first, step_second = (place >> 3) & 3, (place >> 1) & 3
    to_x = (x + (place >> 5)) & 3
    to_z = (z + jnp.where(to_core == 0, step_first, step_second)) & 3
    to_y = (y + jnp.where(to_core == 0, step_second, step_first)) & 3
    named = owner == device_at(to_x, to_core, to_z, to_y)
    before = lax.broadcasted_iota(jnp.int32, (keep, keep), 0) < lax.broadcasted_iota(
        jnp.int32, (keep, keep), 1
    )
    rank = jnp.dot(
        jnp.where(named, 1.0, 0.0).astype(BF16),
        jnp.where(before, 1.0, 0.0).astype(BF16),
        preferred_element_type=F32,
    )
    slot = (2 * parity + (place & 1)).astype(F32)
    picks = jnp.where(jnp.logical_and(named, rank == slot), 1.0, 0.0).astype(BF16)
    places = jnp.where(
        lax.broadcasted_iota(jnp.int32, (span, keep), 0) == row, 1.0, 0.0
    ).astype(BF16)
    chosen = lax.dot_general(picks, places, NT, preferred_element_type=F32).astype(BF16)
    arrive.wait()
    mine, theirs = held[...].astype(F32), other[...].astype(F32)
    first = jnp.where(odd, theirs, mine)
    second = jnp.where(odd, mine, theirs)
    lane = lax.broadcasted_iota(jnp.int32, (1, HD), 1)
    key = jnp.where(lane < HALF, first, pltpu.roll(second, HALF, 1))
    value = jnp.where(lane < HALF, pltpu.roll(first, HALF, 1), second).astype(BF16)
    cosine, sine = rope_factors(tables, number, own.shape[0])
    key = (key * cosine + pltpu.roll(key, HALF, 1) * sine).astype(BF16)
    turn = turn_of(tables, parity, own.shape[0])
    unit = HD ** -0.5
    for i, part in enumerate((key, value)):
        turned = lax.dot_general(turn, part, TN, preferred_element_type=F32) * unit
        seg_out[i * HD:(i + 1) * HD, :] = turned.astype(BF16)
    longest = largest(seg_out[:HD, :].astype(F32), 0)
    halves = [ref[:HALF, :].astype(F32) for ref in (prefix, prefix_other)]
    longest = jnp.maximum(longest, largest(jnp.concatenate(halves, 0), 0)) * 1.01
    seg_out[2 * HD:2 * HD + NOTE, :] = jnp.full((NOTE, own.shape[0]), longest, F32).astype(BF16)
    plain = turn_of(tables, 0, own.shape[0])
    pair = jnp.concatenate(
        [
            (jnp.dot(key, plain, preferred_element_type=F32) * unit).astype(BF16),
            (jnp.dot(value, plain, preferred_element_type=F32) * unit).astype(BF16),
        ],
        1,
    )
    kept = jnp.dot(chosen, pair, preferred_element_type=F32).astype(BF16)
    stay_out[...] = kept[:128, :]
    for i in range(2):
        seg_out[2 * HD + NOTE:, i * 256:(i + 1) * 256] = kept[128 + 64 * i:192 + 64 * i, :]


def vmem():
    return pl.BlockSpec(memory_space=pltpu.VMEM)


def segment(own, *rest):
    span = own.shape[0]
    return pl.pallas_call(
        segment_kernel,
        in_specs=[pl.BlockSpec(memory_space=pl.ANY)] + [vmem()] * 6,
        out_specs=[vmem()] * 2,
        out_shape=[
            jax.ShapeDtypeStruct((2 * HD + NOTE + 64, span), BF16),
            jax.ShapeDtypeStruct((128, 2 * HD), BF16),
        ],
        scratch_shapes=[pltpu.VMEM((span, HD), BF16), pltpu.SemaphoreType.DMA],
        compiler_params=pltpu.CompilerParams(vmem_limit_bytes=24 << 20),
        cost_estimate=pl.CostEstimate(
            flops=400_000_000, bytes_accessed=2 << 20, transcendentals=0
        ),
    )(own, *rest)


def attend_kernel(
    step, q, own, other, sib_own, sib_other, seg, sib_seg, stay, out, acc, total, top, held
):
    x, core = position()[:2]
    rows = q.shape[0]
    span = seg.shape[1]
    blocks = own.shape[1] // TILE
    prefix = ((own, other), (sib_own, sib_other))

    def prefix_tile(pair, columns):
        mine, theirs = pair
        keys = jnp.concatenate([mine[:HALF, columns], theirs[:HALF, columns]], 0)
        values = jnp.concatenate([mine[HALF:, columns], theirs[HALF:, columns]], 0)
        return keys, values

    longest = jnp.maximum(
        jnp.max(seg[2 * HD:2 * HD + NOTE, :HD].astype(F32)),
        jnp.max(sib_seg[2 * HD:2 * HD + NOTE, :HD].astype(F32)),
    )
    widest = largest(q[...].astype(F32), 1)
    calm = longest * widest < SAFE_BOUND * SAFE_BOUND

    if step == 0:
        whole_flags = (None, core == 1)
    else:
        later = lax.rem(x + RING - step, RING) > x
        whole_flags = (later, later)

    def causal(begin, count):
        token = lax.rem(lax.broadcasted_iota(jnp.int32, (count, span), 0) + begin, span)
        return lax.broadcasted_iota(jnp.int32, (count, span), 1) <= token

    acc[...] = jnp.zeros_like(acc)
    total[...] = jnp.zeros_like(total)

    @pl.when(calm)
    def _():
        def tile(keys, values, masked=False):
            scores = jnp.dot(q[...], keys, preferred_element_type=F32)
            weights = jnp.exp2(scores)
            if masked:
                weights = jnp.where(causal(0, rows), weights, 0.0)
            part = weights[:, :HD]
            for i in range(1, TILE // HD):
                part = part + weights[:, i * HD:(i + 1) * HD]
            mixed = lax.dot_general(weights.astype(BF16), values, NT, preferred_element_type=F32)
            acc[...] += mixed
            total[...] += part

        for pair in prefix:
            def some_tiles(i, carry, pair=pair):
                begin = pl.multiple_of(i * TILE, TILE)
                tile(*prefix_tile(pair, pl.ds(begin, TILE)))
                return carry

            lax.fori_loop(0, blocks, some_tiles, 0)
        for ref, flag in zip((seg, sib_seg), whole_flags):
            if flag is None:
                tile(ref[:HD, :], ref[HD:2 * HD, :], masked=True)
            else:
                @pl.when(flag)
                def _(ref=ref):
                    tile(ref[:HD, :], ref[HD:2 * HD, :])
        top[...] = jnp.zeros_like(top)

    @pl.when(jnp.logical_not(calm))
    def _():
        top[...] = jnp.full_like(top, LOWEST)
        chunk = 256
        seg_flag = 1 if whole_flags[0] is None else whole_flags[0].astype(jnp.int32)
        sib_flag = whole_flags[1].astype(jnp.int32)

        def some_keys(b, carry):
            column = pl.ds(pl.multiple_of(lax.rem(b, blocks) * TILE, TILE), TILE)
            for number, pair in enumerate(prefix):
                @pl.when(b // blocks == number)
                def _(pair=pair):
                    for i in range(2):
                        for j, ref in enumerate(pair):
                            begin = i * HD + j * HALF
                            held[begin:begin + HALF, :] = ref[i * HALF:(i + 1) * HALF, column]

            for number, ref in enumerate((seg, sib_seg)):
                @pl.when(b == 2 * blocks + number)
                def _(ref=ref):
                    held[...] = ref[:2 * HD, :]

            last = b == 2 * blocks
            flag = jnp.where(last, seg_flag, jnp.where(b > 2 * blocks, sib_flag, 1))
            causal_from = 0 if step else jnp.where(last, 0, -span)

            def some_rows(r, carry):
                begin = pl.multiple_of(r * chunk, chunk)
                at = pl.ds(begin, chunk)
                scores = jnp.dot(q[at, :], held[:HD, :], preferred_element_type=F32)
                if step == 0:
                    token = lax.rem(
                        lax.broadcasted_iota(jnp.int32, (chunk, span), 0) + begin, span
                    )
                    column = lax.broadcasted_iota(jnp.int32, (chunk, span), 1) + causal_from
                    scores = jnp.where(column <= token, scores, -jnp.inf)
                old = top[at, :]
                new = jnp.maximum(old, jnp.max(scores, 1, keepdims=True))
                weights = jnp.exp2(scores - new[:, :1])
                factor = jnp.exp2(old - new)
                part = weights[:, :HD]
                for i in range(1, TILE // HD):
                    part = part + weights[:, i * HD:(i + 1) * HD]
                mixed = lax.dot_general(
                    weights.astype(BF16), held[HD:, :], NT, preferred_element_type=F32
                )
                acc[at, :] = acc[at, :] * factor + mixed
                total[at, :] = total[at, :] * factor + part
                top[at, :] = new
                return carry

            @pl.when(flag == 1)
            def _():
                lax.fori_loop(0, rows // chunk, some_rows, 0)

            return carry

        lax.fori_loop(0, 2 * blocks + 2, some_keys, 0)

    summed = jnp.sum(total[...], 1, keepdims=True)
    out[:rows, :] = (acc[...] / summed).astype(BF16)
    level = top[...] + jnp.log2(summed)
    eye = lax.broadcasted_iota(jnp.int32, (1, HD, HD), 1) == lax.broadcasted_iota(
        jnp.int32, (1, HD, HD), 2
    )
    packed = jnp.sum(jnp.where(eye, level.reshape(rows // HD, HD, HD), 0.0), 1)
    high = packed.astype(BF16).astype(F32)
    rest = packed - high
    middle = rest.astype(BF16).astype(F32)
    low = rest - middle
    out[rows:rows + 32, :] = jnp.concatenate(
        [high, middle, low, jnp.zeros_like(high)], 0
    ).astype(BF16)
    back = (RING - step) % RING
    begin, lanes = 2 * HD + NOTE + 32 * (back % 2), 2 * HD * (back // 2)
    for i in range(2):
        place, half = rows + 32 + 64 * i, slice(i * HD, (i + 1) * HD)
        out[place:place + 32, :] = stay[32 * back:32 * (back + 1), half]
        half = slice(lanes + i * HD, lanes + (i + 1) * HD)
        out[place + 32:place + 64, :] = sib_seg[begin:begin + 32, half]


def attend(step, q, *rest):
    rows = q.shape[0]
    return pl.pallas_call(
        functools.partial(attend_kernel, step),
        in_specs=[vmem()] * 8,
        out_specs=vmem(),
        out_shape=jax.ShapeDtypeStruct((rows + EXTRA, HD), BF16),
        scratch_shapes=[pltpu.VMEM((rows, HD), F32)] * 3 + [pltpu.VMEM((2 * HD, TILE), BF16)],
        compiler_params=pltpu.CompilerParams(vmem_limit_bytes=32 << 20),
        cost_estimate=pl.CostEstimate(
            flops=8 * rows * HD * 4096, bytes_accessed=4 << 20, transcendentals=rows * 4096
        ),
    )(q, *rest)


def shuffle(rows, source):
    here = lax.broadcasted_iota(jnp.int32, (256, 256), 0)
    there = lax.broadcasted_iota(jnp.int32, (256, 256), 1)
    moves = jnp.where(source(here) == there, 1.0, 0.0).astype(BF16)
    return jnp.dot(moves, rows, preferred_element_type=F32).astype(BF16)


def merge_kernel(p0, p1, p2, p3, sign, *outs):
    parity = position()[4]
    parts = (p0, p1, p2, p3)
    rows = p0.shape[0] - EXTRA
    count = rows // HD
    levels = []
    for part in parts:
        stats = part[rows:rows + 32, :].astype(F32)
        levels.append(stats[:count] + stats[count:2 * count] + stats[2 * count:3 * count])
    most = functools.reduce(jnp.maximum, levels)
    shares = [jnp.exp2(level - most) for level in levels]
    whole = functools.reduce(jnp.add, shares)
    shares = [share / whole for share in shares]
    eye = lax.broadcasted_iota(jnp.int32, (HD, HD), 0) == lax.broadcasted_iota(
        jnp.int32, (HD, HD), 1
    )
    turn = sign[pl.ds(HD * parity, HD), :]
    per_head = count // 2
    for b in range(count):
        left, right = [], []
        for share, part in zip(shares, parts):
            block = part[b * HD:(b + 1) * HD, :]
            left.append(jnp.where(eye, share[b:b + 1, :], 0.0).astype(BF16))
            right.append(block)
        mixed = jnp.dot(
            jnp.concatenate(left, 1), jnp.concatenate(right, 0), preferred_element_type=F32
        )
        plain = lax.dot_general(mixed.astype(BF16), turn, NT, preferred_element_type=F32)
        head, place = b // per_head, b % per_head
        block = (plain * HD ** -0.5).astype(BF16)
        for out in outs:
            out[place * HD:(place + 1) * HD, head * HD:(head + 1) * HD] = block
    kept = jnp.concatenate(
        [
            jnp.concatenate([part[rows + 32:rows + 96, :], part[rows + 96:, :]], 1)
            for part in parts
        ],
        0,
    )
    kept = shuffle(
        kept,
        lambda r: ((r >> 4) & 3) << 6 | ((r >> 3) & 1) << 5 | (r >> 6) << 3 | (r & 7),
    )
    for k, out in enumerate(outs):
        out[rows // 2:, :] = kept[64 * k:64 * (k + 1), :]


def merge(parts, sign):
    rows = parts[0].shape[0] - EXTRA
    return pl.pallas_call(
        merge_kernel,
        in_specs=[vmem()] * 5,
        out_specs=[vmem()] * RING,
        out_shape=[jax.ShapeDtypeStruct((rows // 2 + 64, 2 * HD), BF16)] * RING,
        compiler_params=pltpu.CompilerParams(vmem_limit_bytes=24 << 20),
        cost_estimate=pl.CostEstimate(
            flops=400_000_000, bytes_accessed=2 << 20, transcendentals=0
        ),
    )(*parts, sign)


def out_kernel(places, c0, c1, c2, c3, w0, w1, w2, w3, *outs):
    contexts = (c0, c1, c2, c3)
    span = c0.shape[0] - 64
    kept = jnp.concatenate([c[span:, :] for c in contexts], 0)
    kept = shuffle(
        kept,
        lambda r: ((r >> 4) & 3) << 6
        | ((r >> 2) & 3) << 4
        | ((r >> 1) & 1) << 3
        | (r >> 6) << 1
        | (r & 1),
    )
    for k, out in zip(places, outs):
        columns = slice(k * 256, (k + 1) * 256)
        whole = None
        for c, w in zip(contexts, (w0, w1, w2, w3)):
            part = jnp.dot(c[:span, :], w[:, columns], preferred_element_type=F32)
            whole = part if whole is None else whole + part
        begin = span if k else 0
        if k:
            out[:span, :] = whole.astype(BF16)
        else:
            outs[-1][...] = whole
        out[begin:, :] = kept[64 * k:64 * (k + 1), :]


def project_out(places, contexts, weights):
    total = contexts[0].shape[0]
    span = total - 64
    shapes = [jax.ShapeDtypeStruct((total if k else 64, 256), BF16) for k in places]
    if 0 in places:
        shapes.append(jax.ShapeDtypeStruct((span, 256), F32))
    return pl.pallas_call(
        functools.partial(out_kernel, places),
        in_specs=[vmem()] * 8,
        out_specs=[vmem()] * len(shapes),
        out_shape=shapes,
        compiler_params=pltpu.CompilerParams(vmem_limit_bytes=24 << 20),
        cost_estimate=pl.CostEstimate(
            flops=512 * span * 1024 * len(places), bytes_accessed=5 << 20, transcendentals=0
        ),
    )(*contexts, *weights)


def finish_kernel(share, kept, a1, a2, a3, attn_out, kept_out):
    x, core, z, y = position()[:4]
    arrived = (a1, a2, a3)
    span = share.shape[0]
    whole = share[...]
    for part in arrived:
        whole = whole + part[:span, :].astype(F32)
    attn_out[...] = whole.astype(BF16)
    rows = jnp.concatenate([kept[...]] + [part[span:, :] for part in arrived], 0)
    place = lax.broadcasted_iota(jnp.int32, (1, 256), 1)
    back_second, back_first = place >> 6, (place >> 4) & 3
    from_x = (x + (place >> 2)) & 3
    from_core = (core + (place >> 1)) & 1
    from_z = (z - jnp.where(core == 0, back_first, back_second)) & 3
    from_y = (y - jnp.where(core == 0, back_second, back_first)) & 3
    target = device_at(from_x, from_core, from_z, from_y) * 2 + (place & 1)
    here = lax.broadcasted_iota(jnp.int32, (256, 256), 0)
    moves = jnp.where(here == target, 1.0, 0.0).astype(BF16)
    kept_out[...] = jnp.dot(moves, rows, preferred_element_type=F32).astype(BF16)


def finish(share, kept, arrived):
    return pl.pallas_call(
        finish_kernel,
        in_specs=[vmem()] * 5,
        out_specs=[vmem()] * 2,
        out_shape=[
            jax.ShapeDtypeStruct(share.shape, BF16),
            jax.ShapeDtypeStruct((256, 2 * HD), BF16),
        ],
        compiler_params=pltpu.CompilerParams(vmem_limit_bytes=24 << 20),
    )(share, kept, *arrived)


def shards(
    tokens, norm_gain, w_query, w_key, w_value, w_out, prefix_keys, prefix_values, keep_rows, owners
):
    seq_count = lax.axis_size("seq")
    span = tokens.shape[0]
    prefix_len = prefix_keys.shape[0] * seq_count
    tables = jnp.asarray(rope_tables(span, SPANS, prefix_len))
    sign = jnp.asarray(signs(), BF16)

    own = jnp.concatenate([prefix_keys.T, prefix_values.T], 0)
    other = to_head_pair(own)
    sib_own = to_sibling(own)
    q, kv, *pieces = project(
        tokens, norm_gain.reshape(-1, HD), w_query, w_key.T, w_value.T, tables, w_out
    )
    kv_other = to_head_pair(kv)
    queries = [q] + [along_x(q, d) for d in (1, 2, 3)]
    weights = [pieces[0]] + [along_first(pieces[d], d) for d in (1, 2, 3)]
    kv_other, other, queries[1], queries[3] = lax.optimization_barrier(
        (kv_other, other, queries[1], queries[3])
    )
    sib_other = to_sibling(other)
    seg, stay = segment(
        kv, kv_other, own, other, tables, keep_rows[0], owners.reshape(owners.shape[1:3])
    )
    sib_seg = to_sibling(seg)
    queries[3], weights[2] = lax.optimization_barrier((queries[3], weights[2]))
    parts = [None] * RING
    for d in (3, 1, 2, 0):
        part = attend(
            d, queries[d], own, other, sib_own, sib_other, seg, sib_seg, stay
        )
        parts[d] = along_x(part, -d) if d else part
    contexts = merge(parts, sign)
    contexts = [contexts[0]] + [along_first(contexts[d], d) for d in (1, 2, 3)]
    far_share, = project_out((2,), contexts, weights)
    share_1, share_3, kept_own, share = project_out((1, 3, 0), contexts, weights)
    arrived = [
        along_second(value, k) for value, k in ((share_1, 1), (far_share, 2), (share_3, 3))
    ]
    return tuple(finish(share, kept_own, arrived))


def solution(mesh):
    return jax.shard_map(
        shards,
        mesh=mesh,
        in_specs=(
            P("seq", None),
            P(),
            P(None, "tp"),
            P(None, "tp"),
            P(None, "tp"),
            P("tp", None),
            P("seq", "tp"),
            P("seq", "tp"),
            P("seq", None, None),
            P("seq", None, None, None),
        ),
        out_specs=(P("seq", "tp"), P(("seq", "tp"), None)),
        check_vma=False,
    )
```
